32 devices in a mesh: seq: 8 (over y, x, core), fsdp: 4 (over z).
Axes of the slice: x: 2, y: 2, z: 4, core: 2. Of those that a mesh axis runs over, the one named last changes fastest.
Arguments:
- inputs: bfloat16 [4, 2048, 1600], P('fsdp', 'seq'), may hold values from -6 to 6
- starts: int32 [4, 8], P('fsdp', 'seq'), may hold values from 0 to 1, as said below
- norm_gain: bfloat16 [1600], P('fsdp'), may hold values from 0.25 to 1.75
- in_weight: bfloat16 [1600, 8640], P('fsdp'), may hold values from -0.15625 to 0.15625
- conv_weight: bfloat16 [3200, 4], P('fsdp'), may hold values from -3 to 3
- conv_bias: bfloat16 [3200], P('fsdp'), may hold values from -3 to 3
- xproj_weight: bfloat16 [3200, 132], P('fsdp'), may hold values from -0.109375 to 0.109375
- dtproj_weight: bfloat16 [3200, 100], P('fsdp'), may hold values from -0.625 to 0.625
- dt_bias: bfloat16 [3200], P('fsdp'), may hold values from -6 to -1
- log_decay: bfloat16 [3200, 16], P('fsdp'), may hold values from -3 to 1
- skip_gain: bfloat16 [3200], P('fsdp'), may hold values from 0.19921875 to 1.5
- meta_tokens: bfloat16 [128, 1600], P('fsdp'), may hold values from -6 to 6
- attn_weight: bfloat16 [1600, 1600], P('fsdp'), may hold values from -0.15625 to 0.15625
- mamba_weight: bfloat16 [3200, 1600], P('fsdp'), may hold values from -0.109375 to 0.109375
- attn_gain: bfloat16 [1600], P('fsdp'), may hold values from 0.25 to 1.75
- mamba_gain: bfloat16 [1600], P('fsdp'), may hold values from 0.25 to 1.75
- ffn_gain: bfloat16 [1600], P('fsdp'), may hold values from 0.25 to 1.75
- gate_weight: bfloat16 [1600, 5504], P('fsdp'), may hold values from -0.15625 to 0.15625
- up_weight: bfloat16 [1600, 5504], P('fsdp'), may hold values from -0.15625 to 0.15625
- down_weight: bfloat16 [5504, 1600], P('fsdp'), may hold values from -0.078125 to 0.078125
- cotangent: bfloat16 [4, 2048, 1600], P('fsdp', 'seq'), may hold values from -6 to 6
Outputs:
- layer_out: bfloat16 [4, 2048, 1600], P('fsdp', 'seq')
- inputs_grad: float32 [4, 2048, 1600], P('fsdp', 'seq')
- grad_norm_gain: float32 [1600], P('fsdp')
- grad_in_weight: float32 [1600, 8640], P('fsdp')
- grad_conv_weight: float32 [3200, 4], P('fsdp')
- grad_conv_bias: float32 [3200], P('fsdp')
- grad_xproj_weight: float32 [3200, 132], P('fsdp')
- grad_dtproj_weight: float32 [3200, 100], P('fsdp')
- grad_dt_bias: float32 [3200], P('fsdp')
- grad_log_decay: float32 [3200, 16], P('fsdp')
- grad_skip_gain: float32 [3200], P('fsdp')
- grad_meta_tokens: float32 [128, 1600], P('fsdp')
- grad_attn_weight: float32 [1600, 1600], P('fsdp')
- grad_mamba_weight: float32 [3200, 1600], P('fsdp')
- grad_attn_gain: float32 [1600], P('fsdp')
- grad_mamba_gain: float32 [1600], P('fsdp')
- grad_ffn_gain: float32 [1600], P('fsdp')
- grad_gate_weight: float32 [1600, 5504], P('fsdp')
- grad_up_weight: float32 [1600, 5504], P('fsdp')
- grad_down_weight: float32 [5504, 1600], P('fsdp')
The draws below stay inside these ranges and needn't reach their ends.
Inputs may be any that keep to these rules, and one draw needn't show every extreme that they name: `starts`: 1 marks a block that begins a sequence, 0 a block that continues the one before it; the first block of every row is 1, a 1 stands only at block positions that are multiples of 8, and in one row drawn from the seed only the first block is 1.
All inputs are finite; a program needn't handle non-finite values.
Results may differ from the reference program's by a relative error of at most 0.02.
Values may be sent and summed in bfloat16 or wider, within the bound.
A program may use at most 512 MiB of HBM per device.

```python
import jax
import jax.numpy as jnp
from jax import lax

D = 1600
HQ = 25
HK = 5
HD = 64
EI = 3200
NS = 16
KC = 4
RDT = 100
FF = 5504
META = 128
WIN = 1024
TB = 256
ROWS = 4
SPAN = 2048
GAP = 8
PROJ = 8640
N_SEQ = 8


def draw_starts(key, part):
    key = jax.random.fold_in(key, 7)
    coin_key, row_key = jax.random.split(key)
    coin_flips = jax.random.randint(coin_key, (ROWS, N_SEQ), 0, 2)
    block_ids = jnp.arange(N_SEQ)
    aligned = (block_ids % GAP == 0)[None, :]
    start_flags = jnp.where(aligned, coin_flips, 0)
    start_flags = jnp.where((block_ids == 0)[None, :], 1, start_flags)
    chosen = jax.random.randint(row_key, (), 0, ROWS)
    single = (jnp.arange(ROWS) == chosen)[:, None] & (block_ids > 0)[None, :]
    return jnp.where(single, 0, start_flags).astype(jnp.int32)


def steps_of(key, shape, shards, smallest, top_value):
    gain = 1.0
    for axis_at, blocks in shards:
        steps = jax.random.uniform(jax.random.fold_in(jax.random.fold_in(key, 6), axis_at), (blocks,), jnp.float32, smallest / len(shards), top_value / len(shards))
        gain = gain * jnp.repeat(jnp.exp(steps), shape[axis_at] // blocks).reshape((-1,) + (1,) * (len(shape) - 1 - axis_at))
    return gain


def centred(key, dims, deviation, reach, cuts=(), kind=jnp.bfloat16):
    gain = steps_of(key, dims, cuts, -0.22, 0.18) if cuts else 1.0
    result = jax.random.normal(key, dims, jnp.float32) * deviation * gain
    return jnp.minimum(jnp.maximum(result, -reach), reach).astype(kind)


def setup_inputs(seed: int = 0) -> dict:
    key_list = jax.random.split(jax.random.key(seed), 22)
    inputs = centred(key_list[0], (ROWS, SPAN, D), 1.0, 6.0, ((0, 4), (1, 8)))
    starts = draw_starts(jax.random.fold_in(key_list[21], 71), 0)
    norm_gain = jnp.clip(1.0 + 0.15 * jax.random.normal(key_list[2], (D,), jnp.float32), 0.25, 1.75).astype(jnp.bfloat16)
    in_weight = centred(key_list[3], (D, PROJ), D ** -0.5, 0.15625, ((0, 4),))
    conv_weight = centred(key_list[4], (EI, KC), KC ** -0.5, 3.0, ((0, 4),))
    conv_bias = centred(key_list[5], (EI,), 0.5, 3.0, ((0, 4),))
    xproj_weight = centred(key_list[6], (EI, RDT + 2 * NS), EI ** -0.5, 0.109375, ((0, 4),))
    dtproj_weight = centred(key_list[7], (EI, RDT), RDT ** -0.5, 0.625, ((0, 4),))
    dt_bias = jnp.clip(-6.0 + 5.0 * jax.random.uniform(key_list[8], (EI,), jnp.float32) ** steps_of(key_list[8], (EI,), ((0, 4),), -0.2, 0.2), -6.0, -1.0).astype(jnp.bfloat16)
    log_decay = jnp.clip(-3.0 + 4.0 * jax.random.uniform(key_list[9], (EI, NS), jnp.float32) ** steps_of(key_list[9], (EI, NS), ((0, 4),), -0.2, 0.2), -3.0, 1.0).astype(jnp.bfloat16)
    skip_gain = jnp.clip(0.19921875 + 1.3007812 * jax.random.uniform(key_list[10], (EI,), jnp.float32) ** steps_of(key_list[10], (EI,), ((0, 4),), -0.2, 0.2), 0.19921875, 1.5).astype(jnp.bfloat16)
    meta_tokens = centred(key_list[11], (META, D), 1.0, 6.0, ((0, 4),))
    attn_weight = centred(key_list[12], (HQ * HD, D), (HQ * HD) ** -0.5, 0.15625, ((0, 4),))
    mamba_weight = centred(key_list[13], (EI, D), EI ** -0.5, 0.109375, ((0, 4),))
    attn_gain = jnp.clip(1.0 + 0.15 * jax.random.normal(key_list[14], (D,), jnp.float32), 0.25, 1.75).astype(jnp.bfloat16)
    mamba_gain = jnp.clip(1.0 + 0.15 * jax.random.normal(key_list[15], (D,), jnp.float32), 0.25, 1.75).astype(jnp.bfloat16)
    ffn_gain = jnp.clip(1.0 + 0.15 * jax.random.normal(key_list[16], (D,), jnp.float32), 0.25, 1.75).astype(jnp.bfloat16)
    gate_weight = centred(key_list[17], (D, FF), D ** -0.5, 0.15625, ((0, 4),))
    up_weight = centred(key_list[18], (D, FF), D ** -0.5, 0.15625, ((0, 4),))
    down_weight = centred(key_list[19], (FF, D), FF ** -0.5, 0.078125, ((0, 4),))
    cotangent = centred(key_list[20], (ROWS, SPAN, D), 1.0, 6.0, ((0, 4), (1, 8)))
    return {"inputs": inputs, "starts": starts, "norm_gain": norm_gain, "in_weight": in_weight, "conv_weight": conv_weight, "conv_bias": conv_bias, "xproj_weight": xproj_weight, "dtproj_weight": dtproj_weight, "dt_bias": dt_bias, "log_decay": log_decay, "skip_gain": skip_gain, "meta_tokens": meta_tokens, "attn_weight": attn_weight, "mamba_weight": mamba_weight, "attn_gain": attn_gain, "mamba_gain": mamba_gain, "ffn_gain": ffn_gain, "gate_weight": gate_weight, "up_weight": up_weight, "down_weight": down_weight, "cotangent": cotangent}


EPS = 1e-05
HIGH = lax.Precision.HIGHEST

@jax.custom_vjp
def low(v):
    return lax.optimization_barrier(v.astype(jnp.bfloat16)).astype(jnp.float32)

@jax.custom_vjp
def low_back(v):
    return v

def low_keep(v):
    return (low(v), None)

def low_pass(kept, grad):
    return (grad,)

def back_keep(v):
    return (v, None)

def back_low(kept, grad):
    return (low(grad),)
low.defvjp(low_keep, low_pass)
low_back.defvjp(back_keep, back_low)

def matmul(factor_one, factor_two):
    return jnp.dot(factor_one, factor_two, precision=HIGH, preferred_element_type=jnp.float32)

def rms_norm(values, gains):
    return values * lax.rsqrt(lax.optimization_barrier(jnp.mean(values * values, -1, keepdims=True)) + EPS) * gains

def state_scan(step_sizes, mixed, b_select, c_select, resets, a_matrix):
    row_len = step_sizes.shape[0]

    def run_block(state_now, pieces):

        def one_token(carried, token_item):
            dt_one, x_one, b_one, c_one, reset_one = token_item
            carried = jnp.exp(dt_one[:, None] * a_matrix) * carried * (1.0 - reset_one) + (dt_one * x_one)[:, None] * b_one[None, :]
            return (carried, lax.optimization_barrier(jnp.sum(carried * c_one[None, :], 1)))
        return lax.scan(one_token, state_now, pieces)
    blocks_all = row_len // TB
    pieces = tuple((series.reshape((blocks_all, TB) + series.shape[1:]) for series in (step_sizes, mixed, b_select, c_select, resets)))
    _, outputs = lax.scan(jax.checkpoint(run_block), jnp.zeros((EI, NS), jnp.float32), pieces)
    return outputs.reshape(row_len, EI)

def window_attention(queries, keys_vals, meta_kv, segments):
    row_len = queries.shape[0]
    rows_block = min(512, row_len)
    kv_cols = HK * HD
    padded_kv = jnp.concatenate([jnp.zeros((WIN, 2 * kv_cols), jnp.float32), keys_vals], 0)
    padded_seg = jnp.concatenate([jnp.full((WIN,), -1, jnp.int32), segments], 0)
    query_heads = queries.reshape(row_len, HK, HQ // HK, HD)

    def attend_block(block_index):
        first_row = block_index * rows_block
        query_part = lax.dynamic_slice_in_dim(query_heads, first_row, rows_block, 0)
        kv_part = lax.dynamic_slice_in_dim(padded_kv, first_row, WIN + rows_block, 0)
        seg_keys = lax.dynamic_slice_in_dim(padded_seg, first_row, WIN + rows_block, 0)
        seg_query = lax.dynamic_slice_in_dim(segments, first_row, rows_block, 0)
        query_pos = first_row + jnp.arange(rows_block, dtype=jnp.int32)
        key_pos = first_row - WIN + jnp.arange(WIN + rows_block, dtype=jnp.int32)
        allowed = (seg_keys[None, :] == seg_query[:, None]) & (key_pos[None, :] <= query_pos[:, None]) & (key_pos[None, :] > query_pos[:, None] - WIN)
        allowed = jnp.concatenate([jnp.ones((rows_block, META), jnp.bool_), allowed], 1)
        kv_all = jnp.concatenate([meta_kv, kv_part], 0)
        key_heads = kv_all[:, :kv_cols].reshape(-1, HK, HD)
        val_heads = kv_all[:, kv_cols:].reshape(-1, HK, HD)
        scores = jnp.einsum('thgd,shd->hgts', query_part, key_heads, precision=HIGH) * HD ** (-0.5)
        scores = low_back(jnp.where(allowed[None, None], scores, -jnp.inf))
        probabilities = low(jax.nn.softmax(scores, -1))
        context = jnp.einsum('hgts,shd->thgd', probabilities, val_heads, precision=HIGH)
        return context.reshape(rows_block, HQ * HD)
    blocks_all = row_len // rows_block
    contexts = lax.map(jax.checkpoint(attend_block), jnp.arange(blocks_all, dtype=jnp.int32))
    return contexts.reshape(row_len, HQ * HD)

def layer_row(tokens, start_row, weights):
    norm_gain, in_weight, conv_weight, conv_bias, xproj_weight, dtproj_weight, dt_bias, log_decay, skip_gain, meta_tokens, attn_weight, mamba_weight, attn_gain, mamba_gain, ffn_gain, gate_weight, up_weight, down_weight = weights
    row_len = tokens.shape[0]
    q_cols = HQ * HD
    kv_cols = HK * HD
    token_ids = jnp.arange(row_len, dtype=jnp.int32)
    block_ids = token_ids // TB
    segments = jnp.cumsum(start_row).astype(jnp.int32)[block_ids]
    resets = jnp.where(token_ids % TB == 0, start_row[block_ids], 0).astype(jnp.float32)
    normed = low(rms_norm(tokens, norm_gain))
    projected = low(low_back(matmul(normed, in_weight)))
    queries = projected[:, :q_cols]
    keys_vals = projected[:, q_cols:q_cols + 2 * kv_cols]
    mixer_in = projected[:, q_cols + 2 * kv_cols:q_cols + 2 * kv_cols + EI]
    z_gate = projected[:, q_cols + 2 * kv_cols + EI:]
    meta_normed = low(rms_norm(meta_tokens, norm_gain))
    meta_kv = low(matmul(meta_normed, in_weight[:, q_cols:q_cols + 2 * kv_cols]))
    padded = jnp.concatenate([jnp.zeros((KC - 1, EI), jnp.float32), mixer_in], 0)
    padded_seg = jnp.concatenate([jnp.full((KC - 1,), -1, jnp.int32), segments], 0)
    conv_pre = jnp.zeros((row_len, EI), jnp.float32) + conv_bias
    for offset in range(KC):
        same_seg = (padded_seg[offset:offset + row_len] == segments)[:, None]
        conv_pre = conv_pre + conv_weight[:, offset] * jnp.where(same_seg, padded[offset:offset + row_len], 0.0)
    mixed = jax.nn.silu(conv_pre)
    selected = matmul(mixed, xproj_weight)
    step_rank = selected[:, :RDT]
    b_select = selected[:, RDT:RDT + NS]
    c_select = selected[:, RDT + NS:]
    step_sizes = jax.nn.softplus(matmul(step_rank, dtproj_weight.T) + dt_bias)
    a_matrix = -jnp.exp(log_decay)
    y_full = state_scan(step_sizes, mixed, b_select, c_select, resets, a_matrix) + skip_gain * mixed
    mamba_low = low(y_full * jax.nn.silu(z_gate))
    mamba_out = low_back(matmul(mamba_low, mamba_weight))
    context = low(low_back(window_attention(queries, keys_vals, meta_kv, segments)))
    attn_out = low_back(matmul(context, attn_weight))
    middle = tokens + 0.5 * (rms_norm(attn_out, attn_gain) + rms_norm(mamba_out, mamba_gain))
    ffn_in = low(rms_norm(middle, ffn_gain))
    gate_pre = low_back(matmul(ffn_in, gate_weight))
    up_pre = low_back(matmul(ffn_in, up_weight))
    activated = low(jax.nn.silu(gate_pre) * up_pre)
    return middle + matmul(activated, down_weight)

def reference(inputs, starts, norm_gain, in_weight, conv_weight, conv_bias, xproj_weight, dtproj_weight, dt_bias, log_decay, skip_gain, meta_tokens, attn_weight, mamba_weight, attn_gain, mamba_gain, ffn_gain, gate_weight, up_weight, down_weight, cotangent):
    weights = tuple((series.astype(jnp.float32) for series in (norm_gain, in_weight, conv_weight, conv_bias, xproj_weight, dtproj_weight, dt_bias, log_decay, skip_gain, meta_tokens, attn_weight, mamba_weight, attn_gain, mamba_gain, ffn_gain, gate_weight, up_weight, down_weight)))

    def one_row(accumulated, row_data):
        tokens, start_row, cot_row = row_data
        row_out, pull_back = jax.vjp(lambda hidden, params: layer_row(hidden, start_row, params), tokens.astype(jnp.float32), weights)
        grad_tokens, grad_params = pull_back(cot_row.astype(jnp.float32))
        return (jax.tree.map(jnp.add, accumulated, grad_params), (row_out.astype(jnp.bfloat16), grad_tokens))
    zeros_all = jax.tree.map(jnp.zeros_like, weights)
    grads, (layer_outs, input_grads) = lax.scan(one_row, zeros_all, (inputs, starts, cotangent))
    return (layer_outs, input_grads, grads[0], grads[1], grads[2], grads[3], grads[4], grads[5], grads[6], grads[7], grads[8], grads[9], grads[10], grads[11], grads[12], grads[13], grads[14], grads[15], grads[16], grads[17])
```

```python
import functools

import jax
import jax.numpy as jnp
import numpy as np
from jax import lax
from jax.experimental import pallas as pl
from jax.experimental.pallas import tpu as pltpu
from jax.sharding import PartitionSpec as P

HQ = 25
HK = 5
HD = 64
EI = 3200
NS = 16
KC = 4
RDT = 100
META = 128
WIN = 1024
GAP = 8

EPS = 1e-05
HIGH = lax.Precision.HIGHEST
LANES = 128
CHUNK = 128
F32 = jnp.float32


def fold_rows(first, second, level):
    bit = (lax.broadcasted_iota(jnp.int32, first.shape, 0) >> level) & 1
    upper = bit == 0
    return jnp.where(upper, first, second) + pltpu.roll(
        jnp.where(upper, second, first), 8 - (1 << level), 0
    )


def fold_in(stack, part):
    level = 0
    while stack and stack[-1][0] == level:
        part = fold_rows(stack.pop()[1], part, level)
        level += 1
    stack.append((level, part))


def fold_in_down(stack, part):
    level = 0
    while stack and stack[-1][0] == level:
        part = fold_rows(part, stack.pop()[1], level)
        level += 1
    stack.append((level, part))


def halves(part):
    return part[:8] + part[8:]


def scan_fwd_body(info, dt_ref, x_ref, b_ref, c_ref, a_ref, y_ref, first_ref, state):
    block, piece = pl.program_id(0), pl.program_id(1)
    tiles = a_ref.shape[1] // LANES
    keep = jnp.where(piece == 0, info[1 + block], 1).astype(F32)

    @pl.when((block == 0) & (piece == 0))
    def _():
        state[...] = jnp.zeros_like(state)

    first = state[...] * keep
    first_ref[0] = first

    def cut(values, l):
        return values[:, l * LANES : (l + 1) * LANES]

    def group(g, carried):
        bt, ct, hs = carried
        rows = pl.ds(pl.multiple_of(g * 8, 8), 8)
        dt8 = dt_ref[rows, :]
        u8 = dt8 * x_ref[rows, :]
        stacks = [[] for _ in range(tiles)]
        hs = list(hs)
        for k in range(8):
            bk = jnp.broadcast_to(bt[:, k : k + 1], (NS, LANES))
            ck = jnp.broadcast_to(ct[:, k : k + 1], (NS, LANES))
            for l in range(tiles):
                dtk = cut(dt8, l)[k : k + 1]
                uk = cut(u8, l)[k : k + 1]
                hs[l] = jnp.exp(dtk * cut(a_ref[...], l)) * hs[l] + uk * bk
                fold_in(stacks[l], halves(hs[l] * ck))
        for l in range(tiles):
            y_ref[rows, l * LANES : (l + 1) * LANES] = stacks[l][0][1]
        return pltpu.roll(bt, LANES - 8, 1), pltpu.roll(ct, LANES - 8, 1), tuple(hs)

    start = tuple(cut(first, l) for l in range(tiles))
    _, _, hs = lax.fori_loop(0, CHUNK // 8, group, (b_ref[...], c_ref[...], start))
    for l in range(tiles):
        state[:, l * LANES : (l + 1) * LANES] = hs[l]


def scan_bwd_body(
    info, dt_ref, x_ref, b_ref, c_ref, gy_ref, a_ref, first_ref,
    gdt_ref, gx_ref, gb_ref, gc_ref, ga_ref, carry, states, decays,
):
    turn, piece = pl.program_id(0), pl.program_id(1)
    n_blocks, pieces = pl.num_programs(0), pl.num_programs(1)
    tiles = a_ref.shape[1] // LANES
    after = jnp.minimum(n_blocks - turn, n_blocks - 1)
    keep = jnp.where(piece == 0, info[1 + after], 1).astype(F32)

    @pl.when((turn == 0) & (piece == 0))
    def _():
        carry[...] = jnp.zeros_like(carry)
        ga_ref[...] = jnp.zeros_like(ga_ref)

    def cut(values, l):
        return values[:, l * LANES : (l + 1) * LANES]

    def again(g, carried):
        bt, hs = carried
        hs = list(hs)
        rows = pl.ds(pl.multiple_of(g * 8, 8), 8)
        dt8 = dt_ref[rows, :]
        u8 = dt8 * x_ref[rows, :]
        for k in range(8):
            bk = jnp.broadcast_to(bt[:, k : k + 1], (NS, LANES))
            for l in range(tiles):
                lane = slice(l * LANES, (l + 1) * LANES)
                decay = jnp.exp(cut(dt8, l)[k : k + 1] * cut(a_ref[...], l))
                hs[l] = decay * hs[l] + cut(u8, l)[k : k + 1] * bk
                decays[g * 8 + k, :, lane] = decay
                states[g * 8 + k + 1, :, lane] = hs[l]
        return pltpu.roll(bt, LANES - 8, 1), tuple(hs)

    states[0] = first_ref[0]
    start = tuple(cut(first_ref[0], l) for l in range(tiles))
    lax.fori_loop(0, CHUNK // 8, again, (b_ref[...], start))

    lane_ids = lax.broadcasted_iota(jnp.int32, (NS, LANES), 1)

    def group(turn_g, carried):
        bt, ct, gbt, gct, gs = carried
        g = CHUNK // 8 - 1 - turn_g
        bt, ct, gbt, gct = (pltpu.roll(v, 8, 1) for v in (bt, ct, gbt, gct))
        gs = list(gs)
        rows = pl.ds(pl.multiple_of(g * 8, 8), 8)
        dt8, x8, gy8 = dt_ref[rows, :], x_ref[rows, :], gy_ref[rows, :]
        u8 = dt8 * x8
        logs, drives = [[] for _ in range(tiles)], [[] for _ in range(tiles)]
        sums = [None] * tiles
        for k in reversed(range(8)):
            bk = jnp.broadcast_to(bt[:, k : k + 1], (NS, LANES))
            ck = jnp.broadcast_to(ct[:, k : k + 1], (NS, LANES))
            to_b = to_c = None
            for l in range(tiles):
                lane = slice(l * LANES, (l + 1) * LANES)
                gyk = cut(gy8, l)[k : k + 1]
                grad = ck * gyk + gs[l]
                gs[l] = decays[g * 8 + k, :, lane] * grad
                log = gs[l] * states[g * 8 + k, :, lane]
                fold_in_down(logs[l], halves(log * cut(a_ref[...], l)))
                fold_in_down(drives[l], halves(grad * bk))
                part_b = grad * cut(u8, l)[k : k + 1]
                part_c = states[g * 8 + k + 1, :, lane] * gyk
                to_b = part_b if to_b is None else to_b + part_b
                to_c = part_c if to_c is None else to_c + part_c
                part_a = log * cut(dt8, l)[k : k + 1]
                sums[l] = part_a if sums[l] is None else sums[l] + part_a
            gbt = jnp.where(lane_ids == k, jnp.sum(to_b, 1, keepdims=True), gbt)
            gct = jnp.where(lane_ids == k, jnp.sum(to_c, 1, keepdims=True), gct)
        for l in range(tiles):
            lane = slice(l * LANES, (l + 1) * LANES)
            driven = drives[l][0][1]
            gdt_ref[rows, lane] = logs[l][0][1] + driven * cut(x8, l)
            gx_ref[rows, lane] = driven * cut(dt8, l)
            ga_ref[:, lane] += sums[l]
        return bt, ct, gbt, gct, tuple(gs)

    zero = jnp.zeros((NS, LANES), F32)
    held = tuple(carry[:, l * LANES : (l + 1) * LANES] * keep for l in range(tiles))
    _, _, gbt, gct, gs = lax.fori_loop(
        0, CHUNK // 8, group, (b_ref[...], c_ref[...], zero, zero, held)
    )
    gb_ref[...] = gbt
    gc_ref[...] = gct
    for l in range(tiles):
        carry[:, l * LANES : (l + 1) * LANES] = gs[l]


def scan_fwd(info, dt, x, b_t, c_t, a_t, n_blocks):
    rows, width = dt.shape
    pieces = rows // n_blocks // CHUNK

    def at(i, j, info):
        return (i ^ info[0]) * pieces + j

    wide = pl.BlockSpec((CHUNK, width), lambda i, j, info: (at(i, j, info), 0))
    tall = pl.BlockSpec((NS, CHUNK), lambda i, j, info: (0, at(i, j, info)))
    whole = pl.BlockSpec((NS, width), lambda i, j, info: (0, 0))
    return pl.pallas_call(
        scan_fwd_body,
        grid_spec=pltpu.PrefetchScalarGridSpec(
            num_scalar_prefetch=1,
            grid=(n_blocks, pieces),
            in_specs=[wide, wide, tall, tall, whole],
            out_specs=[
                wide,
                pl.BlockSpec((1, NS, width), lambda i, j, info: (i * pieces + j, 0, 0)),
            ],
            scratch_shapes=[pltpu.VMEM((NS, width), F32)],
        ),
        out_shape=[
            jax.ShapeDtypeStruct((rows, width), F32),
            jax.ShapeDtypeStruct((n_blocks * pieces, NS, width), F32),
        ],
        compiler_params=pltpu.CompilerParams(vmem_limit_bytes=32 * 2**20),
        name="scan_fwd",
    )(info, dt, x, b_t, c_t, a_t)


def scan_bwd(info, dt, x, b_t, c_t, gy, a_t, firsts, n_blocks):
    rows, width = dt.shape
    pieces = rows // n_blocks // CHUNK

    def turned(i, j):
        return (n_blocks - 1 - i), (pieces - 1 - j)

    def at(i, j, info):
        i, j = turned(i, j)
        return (i ^ info[0]) * pieces + j

    wide = pl.BlockSpec((CHUNK, width), lambda i, j, info: (at(i, j, info), 0))
    tall = pl.BlockSpec((NS, CHUNK), lambda i, j, info: (0, at(i, j, info)))
    whole = pl.BlockSpec((NS, width), lambda i, j, info: (0, 0))

    def first_at(i, j, info):
        i, j = turned(i, j)
        return (i * pieces + j, 0, 0)

    return pl.pallas_call(
        scan_bwd_body,
        grid_spec=pltpu.PrefetchScalarGridSpec(
            num_scalar_prefetch=1,
            grid=(n_blocks, pieces),
            in_specs=[wide, wide, tall, tall, wide, whole, pl.BlockSpec((1, NS, width), first_at)],
            out_specs=[wide, wide, tall, tall, whole],
            scratch_shapes=[
                pltpu.VMEM((NS, width), F32),
                pltpu.VMEM((CHUNK + 1, NS, width), F32),
                pltpu.VMEM((CHUNK, NS, width), F32),
            ],
        ),
        out_shape=[
            jax.ShapeDtypeStruct((rows, width), F32),
            jax.ShapeDtypeStruct((rows, width), F32),
            jax.ShapeDtypeStruct((NS, rows), F32),
            jax.ShapeDtypeStruct((NS, rows), F32),
            jax.ShapeDtypeStruct((NS, width), F32),
        ],
        compiler_params=pltpu.CompilerParams(vmem_limit_bytes=40 * 2**20),
        name="scan_bwd",
    )(info, dt, x, b_t, c_t, gy, a_t, firsts)


def conv_fwd_body(info, x_ref, taps_ref, bias_ref, out_ref, padded, *, taps):
    block = pl.program_id(0)
    rows = x_ref.shape[0]
    keep = info[1 + block].astype(F32)

    @pl.when(block == 0)
    def _():
        padded[...] = jnp.zeros_like(padded)

    padded[0:8, :] = padded[rows : rows + 8, :] * keep
    padded[8 : rows + 8, :] = x_ref[...].astype(F32)
    total = bias_ref[...] + taps_ref[0:1, :] * padded[8 - taps + 1 : 8 - taps + 1 + rows, :]
    for i in range(1, taps):
        total += taps_ref[i : i + 1, :] * padded[8 - taps + 1 + i : 8 - taps + 1 + i + rows, :]
    out_ref[...] = total


def conv_bwd_body(info, g_ref, x_ref, taps_ref, gx_ref, gw_ref, gb_ref, padded, *, taps):
    turn = pl.program_id(0)
    n_blocks = pl.num_programs(0)
    rows = x_ref.shape[0]
    after = jnp.minimum(n_blocks - turn, n_blocks - 1)
    keep = info[1 + after].astype(F32)

    @pl.when(turn == 0)
    def _():
        padded[...] = jnp.zeros_like(padded)
        gw_ref[...] = jnp.zeros_like(gw_ref)
        gb_ref[...] = jnp.zeros_like(gb_ref)

    padded[rows : rows + 8, :] = padded[0:8, :] * keep
    padded[0:rows, :] = g_ref[...]
    x = x_ref[...].astype(F32)
    total = None
    for i in range(taps):
        moved = padded[taps - 1 - i : taps - 1 - i + rows, :]
        part = taps_ref[i : i + 1, :] * moved
        total = part if total is None else total + part
        gw_ref[i : i + 1, :] += jnp.sum(x * moved, 0, keepdims=True)
    gx_ref[...] = total.astype(gx_ref.dtype)
    gb_ref[...] += jnp.sum(padded[0:rows, :], 0, keepdims=True)


def conv_fwd(info, x, taps_t, bias, n_blocks):
    rows, width = x.shape
    block = rows // n_blocks
    wide = pl.BlockSpec((block, width), lambda i, info: (i ^ info[0], 0))
    return pl.pallas_call(
        functools.partial(conv_fwd_body, taps=taps_t.shape[0]),
        grid_spec=pltpu.PrefetchScalarGridSpec(
            num_scalar_prefetch=1,
            grid=(n_blocks,),
            in_specs=[
                wide,
                pl.BlockSpec(taps_t.shape, lambda i, info: (0, 0)),
                pl.BlockSpec((1, width), lambda i, info: (0, 0)),
            ],
            out_specs=wide,
            scratch_shapes=[pltpu.VMEM((block + 8, width), F32)],
        ),
        out_shape=jax.ShapeDtypeStruct((rows, width), F32),
        compiler_params=pltpu.CompilerParams(vmem_limit_bytes=32 * 2**20),
        name="conv_fwd",
    )(info, x, taps_t, bias)


def conv_bwd(info, grad, x, taps_t, n_blocks):
    rows, width = x.shape
    block = rows // n_blocks
    wide = pl.BlockSpec((block, width), lambda i, info: ((n_blocks - 1 - i) ^ info[0], 0))
    taps_at = pl.BlockSpec(taps_t.shape, lambda i, info: (0, 0))
    one = pl.BlockSpec((1, width), lambda i, info: (0, 0))
    return pl.pallas_call(
        functools.partial(conv_bwd_body, taps=taps_t.shape[0]),
        grid_spec=pltpu.PrefetchScalarGridSpec(
            num_scalar_prefetch=1,
            grid=(n_blocks,),
            in_specs=[wide, wide, taps_at],
            out_specs=[wide, taps_at, one],
            scratch_shapes=[pltpu.VMEM((block + 8, width), F32)],
        ),
        out_shape=[
            jax.ShapeDtypeStruct((rows, width), jnp.bfloat16),
            jax.ShapeDtypeStruct(taps_t.shape, F32),
            jax.ShapeDtypeStruct((1, width), F32),
        ],
        compiler_params=pltpu.CompilerParams(vmem_limit_bytes=32 * 2**20),
        name="conv_bwd",
    )(info, grad, x, taps_t)


def swap(values, axis, mask):
    return lax.ppermute(values, axis, [(i, i ^ mask) for i in range(lax.axis_size(axis))])


def row_blocks(block):
    n = lax.axis_size("seq")
    half = block.shape[0] // 2
    if n != 8 or half % 16:
        held = block[None]
        for bit in range(n.bit_length() - 1):
            held = jnp.concatenate([held, swap(held, "seq", 1 << bit)], 0)
        return held
    by_2, by_4 = swap(block, "seq", 2), swap(block, "seq", 4)
    by_6 = jnp.concatenate([swap(by_2[:half], "seq", 4), swap(by_4[half:], "seq", 2)], 0)
    four = [block, by_2, by_4, by_6]
    return jnp.stack([part for held in four for part in (held, swap(held, "seq", 1))], 0)


def row_sum(blocks, dtype=jnp.bfloat16):
    n = lax.axis_size("seq")
    half = blocks.shape[1] // 2
    if n != 8 or half % 8:
        held = blocks.astype(dtype)
        for bit in range(n.bit_length() - 1):
            pairs = held.reshape((held.shape[0] // 2, 2) + held.shape[1:])
            came = swap(pairs[:, 1], "seq", 1 << bit)
            held = (pairs[:, 0].astype(F32) + came.astype(F32)).astype(dtype)
        return held[0].astype(F32)
    held = blocks.astype(dtype)
    one = [swap(held[m + 1], "seq", 1) for m in (6, 2, 4, 0)]
    by_6, by_2, by_4, own = (
        held[m].astype(F32) + came.astype(F32) for m, came in zip((6, 2, 4, 0), one)
    )
    by_6 = by_6.astype(dtype)
    to_4 = swap(by_6[:half], "seq", 2).astype(F32)
    to_2 = swap(by_6[half:], "seq", 4).astype(F32)
    by_4 = jnp.concatenate([by_4[:half] + to_4, by_4[half:]], 0).astype(dtype)
    by_2 = jnp.concatenate([by_2[:half], by_2[half:] + to_2], 0).astype(dtype)
    return own + swap(by_2, "seq", 2).astype(F32) + swap(by_4, "seq", 4).astype(F32)


def in_order(blocks):
    n = lax.axis_size("seq")
    here = lax.axis_index("seq")
    out = jnp.zeros_like(blocks)
    for m in range(n):
        out = lax.dynamic_update_index_in_dim(out, blocks[m], here ^ m, 0)
    return out


def by_place(blocks):
    return in_order(blocks)


def depth_blocks(block):
    n = lax.axis_size("fsdp")
    here = lax.axis_index("fsdp")
    up, down = [block], [block]
    for k in range(1, n):
        up.append(lax.ppermute(up[-1], "fsdp", [(i, i + 1) for i in range(k - 1, n - 1)]))
        down.append(lax.ppermute(down[-1], "fsdp", [(i, i - 1) for i in range(1, n - k + 1)]))
    laid = jnp.stack(up[:0:-1] + down, 0)
    return lax.dynamic_slice_in_dim(laid, n - 1 - here, n, 0)


def depth_sum(blocks):
    n = lax.axis_size("fsdp")
    here = lax.axis_index("fsdp")
    blocks = blocks.astype(jnp.bfloat16)

    def pick(index):
        return lax.dynamic_index_in_dim(blocks, jnp.clip(index, 0, n - 1), 0, False)

    up = down = None
    for k in range(1, n):
        rising, falling = pick(here + n - k), pick(here - n + k)
        if up is not None:
            rising = (rising.astype(F32) + up.astype(F32)).astype(jnp.bfloat16)
            falling = (falling.astype(F32) + down.astype(F32)).astype(jnp.bfloat16)
        up = lax.ppermute(rising, "fsdp", [(i, i + 1) for i in range(k)])
        down = lax.ppermute(falling, "fsdp", [(i, i - 1) for i in range(n - k, n)])
    return pick(here).astype(F32) + up.astype(F32) + down.astype(F32)


def pad_to(values, size, axis):
    widths = [(0, 0)] * values.ndim
    widths[axis] = (0, size - values.shape[axis])
    return jnp.pad(values, widths)


def norm_fwd(values, gains):
    inverse = lax.rsqrt(jnp.mean(values * values, -1, keepdims=True) + EPS)
    return (values * inverse * gains, inverse)


def norm_back(values, inverse, gains, grads):
    weighted = grads * gains
    mean_term = jnp.mean(values * weighted, -1, keepdims=True)
    return (
        inverse * weighted - values * inverse**3 * mean_term,
        jnp.sum(grads * values * inverse, 0),
    )


def silu_slope(values):
    sigmoid = jax.nn.sigmoid(values)
    return sigmoid * (1.0 + values * (1.0 - sigmoid))


def product(one, two, dims, exact=False, out=F32):
    return lax.dot_general(
        one,
        two,
        ((dims[:1], dims[1:]), ((), ())),
        preferred_element_type=F32,
        precision=HIGH if exact else None,
    ).astype(out)


def key_allowed(num_rows, position, blocks_back):
    row_ids = jnp.arange(num_rows)[:, None]
    col_ids = jnp.arange(num_rows)[None, :]
    pieces = [jnp.ones((num_rows, META), jnp.bool_)]
    for distance in range(blocks_back, 0, -1):
        reachable = position >= distance
        if distance == blocks_back:
            pieces.append((col_ids > row_ids) & reachable)
        else:
            pieces.append(jnp.broadcast_to(reachable, (num_rows, num_rows)))
    pieces.append(col_ids <= row_ids)
    return jnp.concatenate(pieces, 1)


def head_scores(query_part, key_part, allowed):
    scores = jnp.einsum(
        "tgd,kd->gtk", query_part, key_part, preferred_element_type=F32
    ) * HD ** (-0.5)
    return jnp.where(allowed[None], scores, -jnp.inf)


def shards(
    inputs, starts, norm_gain, in_weight, conv_weight, conv_bias, xproj_weight, dtproj_weight, dt_bias,
    log_decay, skip_gain, meta_tokens, attn_weight, mamba_weight, attn_gain, mamba_gain, ffn_gain,
    gate_weight, up_weight, down_weight, cotangent,
):
    low = jnp.bfloat16
    n, depth = lax.axis_size("seq"), lax.axis_size("fsdp")
    here = lax.axis_index("seq")
    tokens, width = inputs.shape[1:]
    rows = n * tokens
    q_cols, kv_cols = HQ * HD, HK * HD
    qkv_cols = q_cols + 2 * kv_cols
    group_size = HQ // HK
    inner = EI // n
    inner_pad = -(-inner // LANES) * LANES
    hidden_units = gate_weight.shape[1]
    units = hidden_units // n
    shard_rows = width // depth

    if n <= GAP:
        carries = jnp.array([0] + [1] * (n - 1), jnp.int32)
        position = here
    else:
        flags = lax.all_gather(starts[0, 0], "seq")
        carries = 1 - flags
        blocks = jnp.arange(n)
        position = here - jnp.max(jnp.where((flags == 1) & (blocks <= here), blocks, 0))
    info = jnp.concatenate([here.astype(jnp.int32)[None], carries])

    def own_cols(weight, base, total):
        chunk = total // (depth * n)
        return jnp.concatenate(
            [
                lax.dynamic_slice_in_dim(weight, base + j * (total // depth) + here * chunk, chunk, 1)
                for j in range(depth)
            ],
            1,
        )

    def own_rows(weight):
        chunk = weight.shape[0] // n
        return lax.dynamic_slice_in_dim(weight, here * chunk, chunk, 0)

    hidden_all = row_blocks(inputs[0])
    gain_rows = depth_blocks(jnp.stack([norm_gain, attn_gain, mamba_gain, ffn_gain], 0))
    gain_norm, gain_attn, gain_mamba, gain_ffn = (
        gain_rows[:, i].reshape(-1).astype(F32) for i in range(4)
    )
    own_in = jnp.concatenate(
        [own_cols(in_weight, qkv_cols, EI), own_cols(in_weight, qkv_cols + EI, EI)], 1
    )
    w_in = depth_blocks(own_in).reshape(width, 2 * inner)
    w_in = jnp.concatenate(
        [pad_to(w_in[:, :inner], inner_pad, 1), pad_to(w_in[:, inner:], inner_pad, 1)], 1
    )
    small = jnp.concatenate(
        [
            conv_weight, conv_bias[:, None], xproj_weight, dtproj_weight, dt_bias[:, None], log_decay,
            skip_gain[:, None],
        ],
        1,
    )
    small_cols = small.shape[1]
    small_full = depth_blocks(own_rows(small)).reshape(inner, small_cols)
    small_full = pad_to(small_full, inner_pad, 0).astype(F32)
    ends = np.cumsum([0, KC, 1, RDT + 2 * NS, RDT, 1, NS, 1])
    taps, bias, w_select, w_steps, b_steps, a_logs, skip = (
        small_full[:, a:b] for a, b in zip(ends[:-1], ends[1:])
    )
    taps_t, bias, b_steps, skip = taps.T, bias.T, b_steps.T, skip.T
    a_t = -jnp.exp(a_logs.T)

    piece = -(-shard_rows // (16 * n)) * 16
    attn_at = lambda m: jnp.minimum((here ^ m) * piece, shard_rows - piece)

    def gathered_rows(weight):
        own = lax.dynamic_slice_in_dim(weight, attn_at(0), piece, 0)
        parts = row_blocks(depth_blocks(own).reshape(depth * piece, -1))
        full = jnp.zeros((depth, shard_rows, weight.shape[1]), low)
        for m in range(n):
            full = lax.dynamic_update_slice_in_dim(
                full, parts[m].reshape(depth, piece, -1), attn_at(m), 1
            )
        return full.reshape(width, -1)

    w_qkv = gathered_rows(in_weight[:, :qkv_cols])
    w_q, w_kv = w_qkv[:, :q_cols], w_qkv[:, q_cols:]
    meta_rows = depth_blocks(meta_tokens).reshape(META, width)
    w_mamba = pad_to(depth_blocks(own_rows(mamba_weight)).reshape(inner, width), inner_pad, 0)
    w_attn = gathered_rows(attn_weight)
    w_gate = depth_blocks(own_cols(gate_weight, 0, hidden_units)).reshape(width, units)
    w_up = depth_blocks(own_cols(up_weight, 0, hidden_units)).reshape(width, units)
    w_down = depth_blocks(own_rows(down_weight)).reshape(units, width)
    grad_out_all = row_blocks(cotangent[0]).reshape(rows, width)

    hidden = inputs[0].astype(F32)
    normed_all, _ = norm_fwd(hidden_all.astype(F32), gain_norm)
    normed_all = normed_all.astype(low).reshape(rows, width)
    normed, inv_in = norm_fwd(hidden, gain_norm)
    normed = normed.astype(low)
    projected = product(normed_all, w_in, (1, 0), out=low)
    mixer_in, z_gate = projected[:, :inner_pad], projected[:, inner_pad:].astype(F32)
    conv_pre = conv_fwd(info, mixer_in, taps_t, bias, n)
    mixed = jax.nn.silu(conv_pre)
    part = product(w_select, mixed, (0, 1), exact=True)

    def all_sum(values):
        laid = values.reshape(values.shape[0], n, tokens).transpose(1, 0, 2)
        laid = pad_to(laid, -(-values.shape[0] // 16) * 16, 1)
        total = row_blocks(row_sum(laid, F32))
        return total.transpose(1, 0, 2).reshape(-1, rows)[: values.shape[0]]

    selected = all_sum(part)
    ranks, b_sel, c_sel = selected[:RDT], selected[RDT : RDT + NS], selected[RDT + NS :]
    dt_pre = product(ranks, w_steps, (0, 1), exact=True) + b_steps
    steps = jax.nn.softplus(dt_pre)
    y_scan, firsts = scan_fwd(info, steps, mixed, b_sel, c_sel, a_t, n)
    y_full = y_scan + skip * mixed
    silu_z = jax.nn.silu(z_gate)
    mamba_low = (y_full * silu_z).astype(low)
    mamba_out = row_sum(product(mamba_low, w_mamba, (1, 0), out=low).reshape(n, tokens, width))

    blocks_back = WIN // tokens
    queries = product(normed, w_q, (1, 0), out=low)
    keyvals_all = product(normed_all, w_kv, (1, 0), out=low).reshape(n, tokens, 2 * kv_cols)
    places = [((here - d) % n) ^ here for d in range(blocks_back, -1, -1)]
    window = [lax.dynamic_index_in_dim(keyvals_all, m, 0, False) for m in places]
    meta_float = meta_rows.astype(F32)
    meta_normed, meta_inv = norm_fwd(meta_float, gain_norm)
    meta_low = meta_normed.astype(low)
    meta_kv = product(meta_low, w_kv, (1, 0), out=low)
    allowed = key_allowed(tokens, position, blocks_back)
    all_kv = jnp.concatenate([meta_kv] + window, 0)
    n_keys = all_kv.shape[0]
    key_heads = all_kv[:, :kv_cols].reshape(n_keys, HK, HD).transpose(1, 0, 2)
    val_heads = all_kv[:, kv_cols:].reshape(n_keys, HK, HD).transpose(1, 0, 2)
    query_heads = queries.reshape(tokens, HK, group_size, HD).transpose(1, 0, 2, 3)

    def attend(pieces):
        query_part, key_part, val_part = pieces
        scores = head_scores(query_part, key_part, allowed)
        row_max = jnp.max(scores, -1, keepdims=True)
        weights_exp = jnp.exp(scores - row_max)
        row_total = jnp.sum(weights_exp, -1, keepdims=True)
        probabilities = (weights_exp / row_total).astype(low)
        context = jnp.einsum("gtk,kd->tgd", probabilities, val_part, preferred_element_type=F32)
        return (context, (row_max + jnp.log(row_total))[..., 0])

    contexts, log_norms = lax.map(attend, (query_heads, key_heads, val_heads))
    attended = contexts.transpose(1, 0, 2, 3).reshape(tokens, q_cols).astype(low)
    attn_out = product(attended, w_attn, (1, 0))

    attn_normed, attn_inv = norm_fwd(attn_out, gain_attn)
    mamba_normed, mamba_inv = norm_fwd(mamba_out, gain_mamba)
    middle = hidden + 0.5 * (attn_normed + mamba_normed)
    ffn_normed, ffn_inv = norm_fwd(middle, gain_ffn)
    ffn_all = row_blocks(ffn_normed.astype(low)).reshape(rows, width)
    gate_pre = product(ffn_all, w_gate, (1, 0))
    up_pre = product(ffn_all, w_up, (1, 0))
    grad_act = product(grad_out_all, w_down, (1, 1))
    silu_gate = jax.nn.silu(gate_pre)
    activated = (silu_gate * up_pre).astype(low)
    grad_gate = (grad_act * up_pre * silu_slope(gate_pre)).astype(low)
    grad_up = (grad_act * silu_gate).astype(low)
    grad_ffn_part = product(grad_gate, w_gate, (1, 1)) + product(grad_up, w_up, (1, 1))
    grad_ffn_in = row_sum(grad_ffn_part.astype(low).reshape(n, tokens, width))
    down_part = product(activated, w_down, (1, 0), out=low)
    layer_out = middle + row_sum(down_part.reshape(n, tokens, width))

    grad_out = cotangent[0].astype(F32)
    grad_mid_norm, grad_g_ffn = norm_back(middle, ffn_inv, gain_ffn, grad_ffn_in)
    grad_middle = grad_out + grad_mid_norm
    grad_attn_out, grad_g_attn = norm_back(attn_out, attn_inv, gain_attn, 0.5 * grad_middle)
    grad_mamba_out, grad_g_mamba = norm_back(mamba_out, mamba_inv, gain_mamba, 0.5 * grad_middle)
    grad_attn_low = grad_attn_out.astype(low)
    grad_mamba_all = row_blocks(grad_mamba_out.astype(low)).reshape(rows, width)

    grad_context = product(grad_attn_low, w_attn, (1, 1), out=low)
    grad_ctx_heads = grad_context.reshape(tokens, HK, group_size, HD).transpose(1, 0, 2, 3)

    def attend_back(pieces):
        query_part, key_part, val_part, norm_part, gctx_part = pieces
        scores = head_scores(query_part, key_part, allowed)
        probabilities = jnp.exp(scores - norm_part[..., None])
        grad_probs = jnp.einsum("tgd,kd->gtk", gctx_part, val_part, preferred_element_type=F32)
        grad_scores = (
            probabilities * (grad_probs - jnp.sum(probabilities * grad_probs, -1, keepdims=True))
        ).astype(low)
        scale = HD ** (-0.5)
        grad_query = jnp.einsum("gtk,kd->tgd", grad_scores, key_part, preferred_element_type=F32)
        grad_key = jnp.einsum("gtk,tgd->kd", grad_scores, query_part, preferred_element_type=F32)
        grad_val = jnp.einsum(
            "gtk,tgd->kd", probabilities.astype(low), gctx_part, preferred_element_type=F32
        )
        return (grad_query * scale, grad_key * scale, grad_val)

    grad_q_heads, grad_k_heads, grad_v_heads = lax.map(
        attend_back, (query_heads, key_heads, val_heads, log_norms, grad_ctx_heads)
    )
    grad_queries = grad_q_heads.transpose(1, 0, 2, 3).reshape(tokens, q_cols)
    grad_all_kv = jnp.concatenate(
        [
            grad_k_heads.transpose(1, 0, 2).reshape(n_keys, kv_cols),
            grad_v_heads.transpose(1, 0, 2).reshape(n_keys, kv_cols),
        ],
        1,
    )
    grad_meta_kv = grad_all_kv[:META]
    grad_kv_blocks = jnp.zeros((n, tokens, 2 * kv_cols), low)
    for at, m in enumerate(places):
        part = grad_all_kv[META + at * tokens : META + (at + 1) * tokens].astype(low)
        grad_kv_blocks = lax.dynamic_update_index_in_dim(grad_kv_blocks, part, m, 0)
    grad_keyvals = row_sum(grad_kv_blocks)
    grad_qkv = jnp.concatenate([grad_queries, grad_keyvals], 1).astype(low)
    grad_meta_low = product(grad_meta_kv, w_kv.astype(F32), (1, 1), exact=True)
    grad_meta, grad_g_meta = norm_back(meta_float, meta_inv, gain_norm, grad_meta_low)

    grad_mix = product(grad_mamba_all, w_mamba, (1, 1))
    grad_y = grad_mix * silu_z
    grad_z = (grad_mix * y_full * silu_slope(z_gate)).astype(low)
    grad_skip = jnp.sum(grad_y * mixed, 0, keepdims=True)
    grad_steps, grad_x, grad_b, grad_c, grad_a = scan_bwd(
        info, steps, mixed, b_sel, c_sel, grad_y, a_t, firsts, n
    )
    grad_dt_pre = grad_steps * jax.nn.sigmoid(dt_pre)
    grad_dt_bias = jnp.sum(grad_dt_pre, 0, keepdims=True)
    grad_ranks = product(w_steps, grad_dt_pre, (0, 1), exact=True)
    grad_selected = all_sum(jnp.concatenate([grad_ranks, grad_b, grad_c], 0))
    grad_w_steps = product(grad_dt_pre, ranks, (0, 1), exact=True)
    grad_w_select = product(mixed, grad_selected, (0, 1), exact=True)
    grad_mixed = grad_y * skip + grad_x + product(grad_selected, w_select, (0, 1), exact=True)
    grad_conv = grad_mixed * silu_slope(conv_pre)
    grad_mixer, grad_taps, grad_bias = conv_bwd(info, grad_conv, mixer_in, taps_t, n)

    grad_in = jnp.concatenate([grad_mixer, grad_z], 1)
    grad_normed = row_sum(product(grad_in, w_in, (1, 1), out=low).reshape(n, tokens, width))
    grad_normed = grad_normed + product(grad_qkv, w_qkv, (1, 1))
    grad_input_norm, grad_g_in = norm_back(hidden, inv_in, gain_norm, grad_normed)
    inputs_grad = (grad_middle + grad_input_norm)[None]

    def spread(part):
        return in_order(row_blocks(depth_sum(part).astype(low)))

    def spread_cols(grad):
        return spread(grad.astype(low).reshape(depth, shard_rows, -1))

    def laid_cols(parts, total):
        chunk = total // (depth * n)
        return (
            parts.reshape(n, shard_rows, -1, depth, chunk)
            .transpose(1, 2, 3, 0, 4)
            .reshape(shard_rows, -1)
            .astype(F32)
        )

    def spread_rows(grad):
        parts = spread(grad.astype(low).reshape(depth, grad.shape[0] // depth, -1))
        return parts.reshape(-1, parts.shape[-1]).astype(F32)

    def spread_own(grad):
        blocks = grad.astype(low).reshape(depth, shard_rows, -1)
        laid = jnp.stack(
            [
                lax.dynamic_slice_in_dim(blocks, attn_at(m), piece, 1).reshape(depth * piece, -1)
                for m in range(n)
            ],
            0,
        )
        own = depth_sum(row_sum(laid).reshape(depth, piece, -1)).astype(low)
        parts = row_blocks(own)
        full = jnp.zeros((shard_rows, grad.shape[1]), low)
        for m in range(n):
            full = lax.dynamic_update_slice_in_dim(full, parts[m], attn_at(m), 0)
        return full.astype(F32)

    grad_w_gate = laid_cols(spread_cols(product(ffn_all, grad_gate, (0, 0))), hidden_units)
    grad_w_up = laid_cols(spread_cols(product(ffn_all, grad_up, (0, 0))), hidden_units)
    grad_w_down = spread_rows(product(activated, grad_out_all, (0, 0)))
    grad_w_mamba = spread_rows(product(mamba_low, grad_mamba_all, (0, 0))[:inner])
    grad_w_attn = spread_own(product(attended, grad_attn_low, (0, 0)))
    grad_w_kv_meta = product(meta_low.astype(F32), grad_meta_kv, (0, 0), exact=True)
    grad_w_qkv = product(normed, grad_qkv, (0, 0)) + jnp.pad(grad_w_kv_meta, ((0, 0), (q_cols, 0)))
    grad_w_qkv = spread_own(grad_w_qkv)
    grad_w_in = product(normed_all, grad_in, (0, 0))
    grad_w_in = jnp.concatenate(
        [grad_w_in[:, :inner], grad_w_in[:, inner_pad : inner_pad + inner]], 1
    )
    grad_w_in = laid_cols(spread_cols(grad_w_in), EI)
    grad_w_proj = jnp.concatenate([grad_w_qkv, grad_w_in], 1)
    grad_small = jnp.concatenate(
        [
            grad_taps.T, grad_bias.T, grad_w_select, grad_w_steps, grad_dt_bias.T, (grad_a * a_t).T,
            grad_skip.T,
        ],
        1,
    )[:inner]
    grad_small = spread_rows(grad_small)
    grad_taps, grad_bias, grad_w_select, grad_w_steps, grad_dt_bias, grad_decay, grad_skip = (
        grad_small[:, a:b] for a, b in zip(ends[:-1], ends[1:])
    )

    gains = jnp.concatenate(
        [
            grad.astype(low).reshape(depth, -1, shard_rows)
            for grad in (grad_g_in + grad_g_meta, grad_g_attn, grad_g_mamba, grad_g_ffn)
        ],
        1,
    )
    meta_own = META // depth
    vector = jnp.concatenate(
        [
            grad_meta.astype(low).reshape(depth, meta_own * width),
            gains.reshape(depth, 4 * shard_rows),
        ],
        1,
    )
    vector = lax.psum_scatter(vector, "fsdp", scatter_dimension=0, tiled=True)
    vector = lax.psum(vector, "seq")[0].astype(F32)
    grad_meta = vector[: meta_own * width].reshape(meta_own, width)
    gains = vector[meta_own * width :].reshape(4, shard_rows)

    return (
        layer_out.astype(low)[None],
        inputs_grad,
        gains[0],
        grad_w_proj,
        grad_taps,
        grad_bias[:, 0],
        grad_w_select,
        grad_w_steps,
        grad_dt_bias[:, 0],
        grad_decay,
        grad_skip[:, 0],
        grad_meta,
        grad_w_attn,
        grad_w_mamba,
        gains[1],
        gains[2],
        gains[3],
        grad_w_gate,
        grad_w_up,
        grad_w_down,
    )


def solution(mesh):
    in_specs = (
        P("fsdp", "seq", None),
        P("fsdp", "seq"),
        P("fsdp"),
        P("fsdp", None),
        P("fsdp", None),
        P("fsdp"),
        P("fsdp", None),
        P("fsdp", None),
        P("fsdp"),
        P("fsdp", None),
        P("fsdp"),
        P("fsdp", None),
        P("fsdp", None),
        P("fsdp", None),
        P("fsdp"),
        P("fsdp"),
        P("fsdp"),
        P("fsdp", None),
        P("fsdp", None),
        P("fsdp", None),
        P("fsdp", "seq", None),
    )
    out_specs = (
        P("fsdp", "seq", None),
        P("fsdp", "seq", None),
        P("fsdp"),
        P("fsdp", None),
        P("fsdp", None),
        P("fsdp"),
        P("fsdp", None),
        P("fsdp", None),
        P("fsdp"),
        P("fsdp", None),
        P("fsdp"),
        P("fsdp", None),
        P("fsdp", None),
        P("fsdp", None),
        P("fsdp"),
        P("fsdp"),
        P("fsdp"),
        P("fsdp", None),
        P("fsdp", None),
        P("fsdp", None),
    )
    return jax.shard_map(shards, mesh=mesh, in_specs=in_specs, out_specs=out_specs, check_vma=False)
```

```python
import functools

import jax
import jax.numpy as jnp
import numpy as np
from jax import lax
from jax.experimental import pallas as pl
from jax.experimental.layout import Layout, with_layout_constraint
from jax.experimental.pallas import tpu as pltpu
from jax.sharding import PartitionSpec as P

HQ = 25
HK = 5
HD = 64
EI = 3200
NS = 16
KC = 4
RDT = 100
META = 128
WIN = 1024
GAP = 8
SMALL = 256
NEG = -jnp.inf

EPS = 1e-05
HIGH = lax.Precision.HIGHEST
LANES = 128
CHUNK = 128
F32 = jnp.float32
MESH = pl.DeviceIdType.MESH


def fold_rows(first, second, level):
    bit = (lax.broadcasted_iota(jnp.int32, first.shape, 0) >> level) & 1
    upper = bit == 0
    return jnp.where(upper, first, second) + pltpu.roll(
        jnp.where(upper, second, first), 8 - (1 << level), 0
    )


def fold_in(stack, part):
    level = 0
    while stack and stack[-1][0] == level:
        part = fold_rows(stack.pop()[1], part, level)
        level += 1
    stack.append((level, part))


def fold_in_down(stack, part):
    level = 0
    while stack and stack[-1][0] == level:
        part = fold_rows(part, stack.pop()[1], level)
        level += 1
    stack.append((level, part))


def halves(part):
    return part[:8] + part[8:]


def scan_fwd_body(info, dt_ref, x_ref, b_ref, c_ref, a_ref, y_ref, first_ref, state):
    block, piece = pl.program_id(0), pl.program_id(1)
    tiles = a_ref.shape[1] // LANES
    keep = jnp.where(piece == 0, info[1 + block], 1).astype(F32)

    @pl.when((block == 0) & (piece == 0))
    def _():
        state[...] = jnp.zeros_like(state)

    first = state[...] * keep
    first_ref[0] = first

    def cut(values, l):
        return values[:, l * LANES : (l + 1) * LANES]

    def group(g, carried):
        bt, ct, hs = carried
        stacks = [[] for _ in range(tiles)]
        hs = list(hs)
        for k in range(8):
            bk = jnp.broadcast_to(bt[:, k : k + 1], (NS, LANES))
            ck = jnp.broadcast_to(ct[:, k : k + 1], (NS, LANES))
            for l in range(tiles):
                lane = slice(l * LANES, (l + 1) * LANES)
                dtk = dt_ref[g, k : k + 1, lane]
                uk = dtk * x_ref[g, k : k + 1, lane]
                hs[l] = jnp.exp(dtk * cut(a_ref[...], l)) * hs[l] + uk * bk
                fold_in(stacks[l], halves(hs[l] * ck))
        for l in range(tiles):
            y_ref[g, :, l * LANES : (l + 1) * LANES] = stacks[l][0][1]
        return pltpu.roll(bt, LANES - 8, 1), pltpu.roll(ct, LANES - 8, 1), tuple(hs)

    start = tuple(cut(first, l) for l in range(tiles))
    _, _, hs = lax.fori_loop(0, CHUNK // 8, group, (b_ref[...], c_ref[...], start))
    for l in range(tiles):
        state[:, l * LANES : (l + 1) * LANES] = hs[l]


def scan_bwd_body(
    info, dt_ref, x_ref, b_ref, c_ref, gy_ref, a_ref, first_ref,
    gdt_ref, gx_ref, gb_ref, gc_ref, ga_ref, carry, states, decays, lanes_b, lanes_c,
):
    turn, piece = pl.program_id(0), pl.program_id(1)
    n_blocks, pieces = pl.num_programs(0), pl.num_programs(1)
    tiles = a_ref.shape[1] // LANES
    after = jnp.minimum(n_blocks - turn, n_blocks - 1)
    keep = jnp.where(piece == 0, info[1 + after], 1).astype(F32)

    @pl.when((turn == 0) & (piece == 0))
    def _():
        carry[...] = jnp.zeros_like(carry)
        ga_ref[...] = jnp.zeros_like(ga_ref)

    def cut(values, l):
        return values[:, l * LANES : (l + 1) * LANES]

    def again(g, carried):
        bt, hs = carried
        hs = list(hs)
        for k in range(8):
            bk = jnp.broadcast_to(bt[:, k : k + 1], (NS, LANES))
            for l in range(tiles):
                lane = slice(l * LANES, (l + 1) * LANES)
                dtk = dt_ref[g, k : k + 1, lane]
                uk = dtk * x_ref[g, k : k + 1, lane]
                decay = jnp.exp(dtk * cut(a_ref[...], l))
                hs[l] = decay * hs[l] + uk * bk
                decays[g * 8 + k, :, lane] = decay
                states[g * 8 + k + 1, :, lane] = hs[l]
        return pltpu.roll(bt, LANES - 8, 1), tuple(hs)

    states[0] = first_ref[0]
    start = tuple(cut(first_ref[0], l) for l in range(tiles))
    lax.fori_loop(0, CHUNK // 8, again, (b_ref[...], start))

    def group(turn_g, carried):
        bt, ct, gs = carried
        g = CHUNK // 8 - 1 - turn_g
        bt, ct = (pltpu.roll(v, 8, 1) for v in (bt, ct))
        gs = list(gs)
        logs, drives = [[] for _ in range(tiles)], [[] for _ in range(tiles)]
        sums = [None] * tiles
        for k in reversed(range(8)):
            t = g * 8 + k
            bk = jnp.broadcast_to(bt[:, k : k + 1], (NS, LANES))
            ck = jnp.broadcast_to(ct[:, k : k + 1], (NS, LANES))
            to_b = to_c = None
            for l in range(tiles):
                lane = slice(l * LANES, (l + 1) * LANES)
                gyk = gy_ref[g, k : k + 1, lane]
                dtk = dt_ref[g, k : k + 1, lane]
                uk = dtk * x_ref[g, k : k + 1, lane]
                grad = ck * gyk + gs[l]
                gs[l] = decays[t, :, lane] * grad
                log = gs[l] * states[t, :, lane]
                fold_in_down(logs[l], halves(log * cut(a_ref[...], l)))
                fold_in_down(drives[l], halves(grad * bk))
                part_b = grad * uk
                part_c = states[t + 1, :, lane] * gyk
                to_b = part_b if to_b is None else to_b + part_b
                to_c = part_c if to_c is None else to_c + part_c
                part_a = log * dtk
                sums[l] = part_a if sums[l] is None else sums[l] + part_a
            span = pl.ds(pl.multiple_of(t * NS, NS), NS)
            lanes_b[span, :] = to_b
            lanes_c[span, :] = to_c
        for l in range(tiles):
            lane = slice(l * LANES, (l + 1) * LANES)
            driven = drives[l][0][1]
            gdt_ref[g, :, lane] = logs[l][0][1] + driven * x_ref[g, :, lane]
            gx_ref[g, :, lane] = driven * dt_ref[g, :, lane]
            ga_ref[:, lane] += sums[l]
        return bt, ct, tuple(gs)

    held = tuple(carry[:, l * LANES : (l + 1) * LANES] * keep for l in range(tiles))
    _, _, gs = lax.fori_loop(0, CHUNK // 8, group, (b_ref[...], c_ref[...], held))
    for l in range(tiles):
        carry[:, l * LANES : (l + 1) * LANES] = gs[l]

    lane_ids = lax.broadcasted_iota(jnp.int32, (NS, LANES), 1)
    ones = jnp.ones((LANES, LANES), jnp.bfloat16)

    def lane_sums(values):
        high = values.astype(jnp.bfloat16)
        rest = (values - high.astype(F32)).astype(jnp.bfloat16)
        return jnp.dot(high, ones, preferred_element_type=F32) + jnp.dot(
            rest, ones, preferred_element_type=F32
        )

    def collect(g, carried):
        gbt, gct = carried
        span = pl.ds(pl.multiple_of(g * 8 * NS, 8 * NS), 8 * NS)
        sum_b, sum_c = lane_sums(lanes_b[span, :]), lane_sums(lanes_c[span, :])
        for k in range(8):
            here = lane_ids == g * 8 + k
            gbt = jnp.where(here, sum_b[k * NS : (k + 1) * NS], gbt)
            gct = jnp.where(here, sum_c[k * NS : (k + 1) * NS], gct)
        return gbt, gct

    zero = jnp.zeros((NS, LANES), F32)
    gbt, gct = lax.fori_loop(0, CHUNK // 8, collect, (zero, zero))
    gb_ref[...] = gbt
    gc_ref[...] = gct


def scan_fwd(info, dt, x, b_t, c_t, a_t, n_blocks):
    rows, width = dt.shape
    pieces = rows // n_blocks // CHUNK

    def at(i, j, info):
        return (i ^ info[0]) * pieces + j

    wide = pl.BlockSpec((CHUNK // 8, 8, width), lambda i, j, info: (at(i, j, info), 0, 0))
    tall = pl.BlockSpec((NS, CHUNK), lambda i, j, info: (0, at(i, j, info)))
    whole = pl.BlockSpec((NS, width), lambda i, j, info: (0, 0))
    dt, x = (v.reshape(-1, 8, width) for v in (dt, x))
    y, firsts = pl.pallas_call(
        scan_fwd_body,
        grid_spec=pltpu.PrefetchScalarGridSpec(
            num_scalar_prefetch=1,
            grid=(n_blocks, pieces),
            in_specs=[wide, wide, tall, tall, whole],
            out_specs=[
                wide,
                pl.BlockSpec((1, NS, width), lambda i, j, info: (i * pieces + j, 0, 0)),
            ],
            scratch_shapes=[pltpu.VMEM((NS, width), F32)],
        ),
        out_shape=[
            jax.ShapeDtypeStruct((rows // 8, 8, width), F32),
            jax.ShapeDtypeStruct((n_blocks * pieces, NS, width), F32),
        ],
        compiler_params=pltpu.CompilerParams(vmem_limit_bytes=32 * 2**20),
        cost_estimate=busy(36),
        name="scan_fwd",
    )(info, dt, x, b_t, c_t, a_t)
    return y.reshape(rows, width), firsts


def scan_bwd(info, dt, x, b_t, c_t, gy, a_t, firsts, n_blocks):
    rows, width = dt.shape
    pieces = rows // n_blocks // CHUNK

    def turned(i, j):
        return (n_blocks - 1 - i), (pieces - 1 - j)

    def at(i, j, info):
        i, j = turned(i, j)
        return (i ^ info[0]) * pieces + j

    wide = pl.BlockSpec((CHUNK // 8, 8, width), lambda i, j, info: (at(i, j, info), 0, 0))
    tall = pl.BlockSpec((NS, CHUNK), lambda i, j, info: (0, at(i, j, info)))
    whole = pl.BlockSpec((NS, width), lambda i, j, info: (0, 0))

    def first_at(i, j, info):
        i, j = turned(i, j)
        return (i * pieces + j, 0, 0)

    dt, x, gy = (v.reshape(-1, 8, width) for v in (dt, x, gy))
    gdt, gx, gb, gc, ga = pl.pallas_call(
        scan_bwd_body,
        grid_spec=pltpu.PrefetchScalarGridSpec(
            num_scalar_prefetch=1,
            grid=(n_blocks, pieces),
            in_specs=[wide, wide, tall, tall, wide, whole, pl.BlockSpec((1, NS, width), first_at)],
            out_specs=[wide, wide, tall, tall, whole],
            scratch_shapes=[
                pltpu.VMEM((NS, width), F32),
                pltpu.VMEM((CHUNK + 1, NS, width), F32),
                pltpu.VMEM((CHUNK, NS, width), F32),
                pltpu.VMEM((CHUNK * NS, LANES), F32),
                pltpu.VMEM((CHUNK * NS, LANES), F32),
            ],
        ),
        out_shape=[
            jax.ShapeDtypeStruct((rows // 8, 8, width), F32),
            jax.ShapeDtypeStruct((rows // 8, 8, width), F32),
            jax.ShapeDtypeStruct((NS, rows), F32),
            jax.ShapeDtypeStruct((NS, rows), F32),
            jax.ShapeDtypeStruct((NS, width), F32),
        ],
        compiler_params=pltpu.CompilerParams(vmem_limit_bytes=40 * 2**20),
        cost_estimate=busy(140),
        name="scan_bwd",
    )(info, dt, x, b_t, c_t, gy, a_t, firsts)
    return gdt.reshape(rows, width), gx.reshape(rows, width), gb, gc, ga


def conv_fwd_body(info, x_ref, taps_ref, bias_ref, out_ref, padded, *, taps):
    block = pl.program_id(0)
    rows = x_ref.shape[0]
    keep = info[1 + block].astype(F32)

    @pl.when(block == 0)
    def _():
        padded[...] = jnp.zeros_like(padded)

    padded[0:8, :] = padded[rows : rows + 8, :] * keep
    padded[8 : rows + 8, :] = x_ref[...].astype(F32)
    total = bias_ref[...] + taps_ref[0:1, :] * padded[8 - taps + 1 : 8 - taps + 1 + rows, :]
    for i in range(1, taps):
        total += taps_ref[i : i + 1, :] * padded[8 - taps + 1 + i : 8 - taps + 1 + i + rows, :]
    out_ref[...] = total


def conv_bwd_body(info, g_ref, x_ref, taps_ref, gx_ref, gw_ref, gb_ref, padded, *, taps):
    turn = pl.program_id(0)
    n_blocks = pl.num_programs(0)
    rows = x_ref.shape[0]
    after = jnp.minimum(n_blocks - turn, n_blocks - 1)
    keep = info[1 + after].astype(F32)

    @pl.when(turn == 0)
    def _():
        padded[...] = jnp.zeros_like(padded)
        gw_ref[...] = jnp.zeros_like(gw_ref)
        gb_ref[...] = jnp.zeros_like(gb_ref)

    padded[rows : rows + 8, :] = padded[0:8, :] * keep
    padded[0:rows, :] = g_ref[...]
    x = x_ref[...].astype(F32)
    total = None
    for i in range(taps):
        moved = padded[taps - 1 - i : taps - 1 - i + rows, :]
        part = taps_ref[i : i + 1, :] * moved
        total = part if total is None else total + part
        gw_ref[i : i + 1, :] += jnp.sum(x * moved, 0, keepdims=True)
    gx_ref[...] = total.astype(gx_ref.dtype)
    gb_ref[...] += jnp.sum(padded[0:rows, :], 0, keepdims=True)


def conv_fwd(info, x, taps_t, bias, n_blocks):
    rows, width = x.shape
    block = rows // n_blocks
    wide = pl.BlockSpec((block, width), lambda i, info: (i ^ info[0], 0))
    return pl.pallas_call(
        functools.partial(conv_fwd_body, taps=taps_t.shape[0]),
        grid_spec=pltpu.PrefetchScalarGridSpec(
            num_scalar_prefetch=1,
            grid=(n_blocks,),
            in_specs=[
                wide,
                pl.BlockSpec(taps_t.shape, lambda i, info: (0, 0)),
                pl.BlockSpec((1, width), lambda i, info: (0, 0)),
            ],
            out_specs=wide,
            scratch_shapes=[pltpu.VMEM((block + 8, width), F32)],
        ),
        out_shape=jax.ShapeDtypeStruct((rows, width), F32),
        compiler_params=pltpu.CompilerParams(vmem_limit_bytes=32 * 2**20),
        cost_estimate=busy(5),
        name="conv_fwd",
    )(info, x, taps_t, bias)


def conv_bwd(info, grad, x, taps_t, n_blocks):
    rows, width = x.shape
    block = rows // n_blocks
    wide = pl.BlockSpec((block, width), lambda i, info: ((n_blocks - 1 - i) ^ info[0], 0))
    taps_at = pl.BlockSpec(taps_t.shape, lambda i, info: (0, 0))
    one = pl.BlockSpec((1, width), lambda i, info: (0, 0))
    return pl.pallas_call(
        functools.partial(conv_bwd_body, taps=taps_t.shape[0]),
        grid_spec=pltpu.PrefetchScalarGridSpec(
            num_scalar_prefetch=1,
            grid=(n_blocks,),
            in_specs=[wide, wide, taps_at],
            out_specs=[wide, taps_at, one],
            scratch_shapes=[pltpu.VMEM((block + 8, width), F32)],
        ),
        out_shape=[
            jax.ShapeDtypeStruct((rows, width), jnp.bfloat16),
            jax.ShapeDtypeStruct(taps_t.shape, F32),
            jax.ShapeDtypeStruct((1, width), F32),
        ],
        compiler_params=pltpu.CompilerParams(vmem_limit_bytes=32 * 2**20),
        cost_estimate=busy(9),
        name="conv_bwd",
    )(info, grad, x, taps_t)


def busy(us):
    return pl.CostEstimate(flops=int(us * 1.1e9), bytes_accessed=0, transcendentals=0)


def on_seq(index):
    return {"seq": index}


def masks_of(n):
    return [1 << bit for bit in range(n.bit_length() - 1)]


def greet_seq(n):
    here = lax.axis_index("seq")
    barrier = pltpu.get_barrier_semaphore()
    masks = masks_of(n)
    for mask in masks:
        pl.semaphore_signal(barrier, inc=1, device_id=on_seq(here ^ mask), device_id_type=MESH)
    return len(masks)


def send_to(source, target, sems, at, mask):
    send, recv = sems
    here = lax.axis_index("seq")
    return pltpu.make_async_remote_copy(
        src_ref=source,
        dst_ref=target,
        send_sem=send.at[at],
        recv_sem=recv.at[at],
        device_id=on_seq(here ^ mask),
        device_id_type=MESH,
    )


def crossed(rows, n):
    return n == 8 and rows >= 64


def gather_start(src, out, sems, n):
    here = lax.axis_index("seq")
    if not crossed(src.shape[0], n):
        copies = []

        def bit_step(bit):
            def run():
                if bit:
                    copies[-1].wait_recv()
                size = 1 << bit
                span = pl.ds((here >> bit) << bit, size)
                copy = send_to(out.at[span], out.at[span], sems, bit, size)
                copy.start()
                copies.append(copy)

            return run

        def last():
            copies[-1].wait_recv()
            for copy in copies:
                copy.wait_send()

        return [bit_step(bit) for bit in range(n.bit_length() - 1)] + [last]

    half = -(-src.shape[0] // 32) * 16
    low, high = pl.ds(0, half), pl.ds(half, src.shape[0] - half)
    own = out.at[here]
    to_2, to_4, to_1 = (
        send_to(src, own, sems, 0, 2),
        send_to(src, own, sems, 1, 4),
        send_to(src, own, sems, 2, 1),
    )
    for copy in (to_2, to_4, to_1):
        copy.start()
    from_2, from_4, from_6 = out.at[here ^ 2], out.at[here ^ 4], out.at[here ^ 6]
    on_4 = send_to(from_2.at[low], from_2.at[low], sems, 3, 4)
    on_2 = send_to(from_4.at[high], from_4.at[high], sems, 4, 2)
    core_2, core_4, core_6 = (
        send_to(block, block, sems, 5 + i, 1) for i, block in enumerate((from_2, from_4, from_6))
    )

    def second():
        to_2.wait_recv()
        on_4.start()
        core_2.start()
        to_4.wait_recv()
        on_2.start()
        core_4.start()

    def third():
        on_4.wait_recv()
        on_2.wait_recv()
        core_6.start()

    def last():
        for copy in (to_1, core_2, core_4, core_6):
            copy.wait_recv()
        for copy in (to_2, to_4, to_1, on_4, on_2, core_2, core_4, core_6):
            copy.wait_send()

    return [second, third, last]


def gather_body(src, out, local, send, recv, *, n):
    here = lax.axis_index("seq")
    own = pltpu.make_async_copy(src, out.at[here], local)
    own.start()
    count = greet_seq(n)
    pl.semaphore_wait(pltpu.get_barrier_semaphore(), count)
    cross = crossed(src.shape[0], n)
    if not cross:
        own.wait()
    for step in gather_start(src, out, (send, recv), n):
        step()
    if cross:
        own.wait()


def seq_gather(block, call):
    n = lax.axis_size("seq")
    return pl.pallas_call(
        functools.partial(gather_body, n=n),
        out_shape=jax.ShapeDtypeStruct((n,) + block.shape, block.dtype),
        in_specs=[pl.BlockSpec(memory_space=pl.ANY)],
        out_specs=pl.BlockSpec(memory_space=pl.ANY),
        scratch_shapes=[
            pltpu.SemaphoreType.DMA(()),
            pltpu.SemaphoreType.DMA((8,)),
            pltpu.SemaphoreType.DMA((8,)),
        ],
        compiler_params=pltpu.CompilerParams(collective_id=call, has_side_effects=True),
        cost_estimate=busy(35),
        name="seq_gather",
    )(block)


def add_rows(out, one, two, start, size, step=16):
    def turn(i, _):
        rows = pl.ds(pl.multiple_of(start + i * step, step), step)
        out[rows, :] = (one[rows, :].astype(F32) + two[rows, :].astype(F32)).astype(out.dtype)
        return 0

    lax.fori_loop(0, size // step, turn, 0)


def reduce_steps(blocks, out, came, sums, ends, sems, n, at=0):
    here = lax.axis_index("seq")
    tokens = blocks.shape[1]
    if n != 8:
        held = blocks
        for k, bit in enumerate(reversed(range(n.bit_length() - 1))):
            size = 1 << bit
            first = (here >> bit) & 1
            other = pl.ds((1 - first) * size, size)
            copy = send_to(held.at[other], came.at[pl.ds(size, size)], sems, at + k, size)
            copy.start()
            copy.wait()
            for j in range(size):
                add_rows(
                    sums.at[size + j], held.at[first * size + j], came.at[size + j], 0, tokens
                )
            held = sums.at[pl.ds(size, size)]
        total = sums.at[1]

        def turn(i, _):
            rows = pl.ds(pl.multiple_of(i * 16, 16), 16)
            out[rows, :] = total[rows, :].astype(out.dtype)
            return 0

        lax.fori_loop(0, tokens // 16, turn, 0)
        return
    half = tokens // 2
    low, high = pl.ds(0, half), pl.ds(half, half)
    step = 16 if half % 16 == 0 else 8
    core = [
        send_to(blocks.at[here ^ (mask | 1)], came.at[i], sems, at + i, 1)
        for i, mask in enumerate((6, 2, 4, 0))
    ]
    for copy in core:
        copy.start()
    by_6, by_2, by_4 = (sums.at[i] for i in range(3))
    end_2, end_4, mid_2, mid_4 = ends.at[0], ends.at[1], ends.at[2], ends.at[3]
    dia_2 = send_to(by_6.at[low], mid_4.at[low], sems, at + 4, 2)
    dia_4 = send_to(by_6.at[high], mid_2.at[high], sems, at + 5, 4)
    x_low = send_to(by_2.at[low], end_2.at[low], sems, at + 6, 2)
    y_high = send_to(by_4.at[high], end_4.at[high], sems, at + 7, 4)
    x_high = send_to(by_2.at[high], end_2.at[high], sems, at + 8, 2)
    y_low = send_to(by_4.at[low], end_4.at[low], sems, at + 9, 4)
    core[0].wait_recv()
    add_rows(by_6, blocks.at[here ^ 6], came.at[0], 0, tokens, step)
    dia_2.start()
    dia_4.start()
    core[1].wait_recv()
    add_rows(by_2, blocks.at[here ^ 2], came.at[1], 0, tokens, step)
    x_low.start()
    core[2].wait_recv()
    add_rows(by_4, blocks.at[here ^ 4], came.at[2], 0, tokens, step)
    y_high.start()
    dia_4.wait_recv()
    add_rows(by_2, by_2, mid_2, half, half, step)
    x_high.start()
    dia_2.wait_recv()
    add_rows(by_4, by_4, mid_4, 0, half, step)
    y_low.start()
    core[3].wait_recv()
    add_rows(out, blocks.at[here], came.at[3], 0, tokens, step)
    x_low.wait_recv()
    x_high.wait_recv()
    add_rows(out, out, end_2, 0, tokens, step)
    y_high.wait_recv()
    y_low.wait_recv()
    add_rows(out, out, end_4, 0, tokens, step)
    for copy in core + [dia_2, dia_4, x_low, y_high, x_high, y_low]:
        copy.wait_send()


def reduce_body(blocks, out, came, sums, ends, send, recv, *, n):
    count = greet_seq(n)
    pl.semaphore_wait(pltpu.get_barrier_semaphore(), count)
    reduce_steps(blocks, out, came, sums, ends, (send, recv), n)


def reduce_scratch(n, rows, width, dtype):
    if n != 8:
        return [pltpu.VMEM((n, rows, width), dtype)] * 2 + [pltpu.VMEM((1, 8, 128), dtype)]
    return [
        pltpu.VMEM((4, rows, width), dtype),
        pltpu.VMEM((3, rows, width), dtype),
        pltpu.VMEM((4, rows, width), dtype),
    ]


def seq_reduce(blocks, call):
    n, rows, width = blocks.shape
    return pl.pallas_call(
        functools.partial(reduce_body, n=n),
        out_shape=jax.ShapeDtypeStruct((rows, width), F32),
        in_specs=[pl.BlockSpec(memory_space=pltpu.VMEM)],
        out_specs=pl.BlockSpec(memory_space=pltpu.VMEM),
        scratch_shapes=reduce_scratch(n, rows, width, blocks.dtype)
        + [pltpu.SemaphoreType.DMA((10,)), pltpu.SemaphoreType.DMA((10,))],
        compiler_params=pltpu.CompilerParams(
            collective_id=call, has_side_effects=True, vmem_limit_bytes=56 * 2**20
        ),
        cost_estimate=busy(blocks.size / 8e4),
        name="seq_reduce",
    )(blocks)


def total_body(blocks, out, total, came, sums, ends, send, recv, local, *, n):
    here = lax.axis_index("seq")
    count = greet_seq(n)
    pl.semaphore_wait(pltpu.get_barrier_semaphore(), count)
    reduce_steps(blocks, total, came, sums, ends, (send, recv), n)
    own = pltpu.make_async_copy(total, out.at[here], local)
    own.start()
    cross = crossed(total.shape[0], n)
    if not cross:
        own.wait()
    for step in gather_start(total, out, (send.at[pl.ds(10, 8)], recv.at[pl.ds(10, 8)]), n):
        step()
    if cross:
        own.wait()


def seq_total(blocks, call):
    n, rows, width = blocks.shape
    return pl.pallas_call(
        functools.partial(total_body, n=n),
        out_shape=jax.ShapeDtypeStruct(blocks.shape, F32),
        in_specs=[pl.BlockSpec(memory_space=pltpu.VMEM)],
        out_specs=pl.BlockSpec(memory_space=pltpu.VMEM),
        scratch_shapes=[pltpu.VMEM((rows, width), F32)]
        + reduce_scratch(n, rows, width, F32)
        + [
            pltpu.SemaphoreType.DMA((18,)),
            pltpu.SemaphoreType.DMA((18,)),
            pltpu.SemaphoreType.DMA(()),
        ],
        compiler_params=pltpu.CompilerParams(
            collective_id=call, has_side_effects=True, vmem_limit_bytes=40 * 2**20
        ),
        cost_estimate=busy(20),
        name="seq_total",
    )(blocks)


def line_steps(srcs, outs, send, recv, depth):
    here = lax.axis_index("fsdp")

    def passed(a, k, side):
        shard = here - (k - 1) if side == 0 else here + (k - 1)
        shard = jnp.clip(shard, 0, depth - 1)
        target = here + 1 if side == 0 else here - 1
        target = jnp.clip(target, 0, depth - 1)
        block = outs[a].at[shard]
        return pltpu.make_async_remote_copy(
            src_ref=srcs[a] if k == 1 else block,
            dst_ref=block,
            send_sem=send.at[a, side, k - 1],
            recv_sem=recv.at[a, side, k - 1],
            device_id={"fsdp": target},
            device_id_type=MESH,
        )

    def sends(k, side):
        if side == 0:
            return (here >= k - 1) & (here < depth - 1)
        return (here <= depth - k) & (here > 0)

    def gets(k, side):
        return here >= k if side == 0 else here <= depth - 1 - k

    def arrived(k):
        for side in range(2):

            @pl.when(gets(k, side))
            def _():
                for a in range(len(srcs)):
                    passed(a, k, side).wait_recv()

    def step(k):
        def run():
            if k > 1:
                arrived(k - 1)
            for side in range(2):

                @pl.when(sends(k, side))
                def _():
                    for a in range(len(srcs)):
                        passed(a, k, side).start()

        return run

    def last():
        arrived(depth - 1)
        for k in range(1, depth):
            for side in range(2):

                @pl.when(sends(k, side))
                def _():
                    for a in range(len(srcs)):
                        passed(a, k, side).wait_send()

    return [step(k) for k in range(1, depth)] + [last]


def first_body(*refs, n, depth, lines):
    block, srcs = refs[0], refs[1 : 1 + lines]
    gathered, outs = refs[1 + lines], refs[2 + lines : 2 + 2 * lines]
    local, send, recv, line_send, line_recv = refs[2 + 2 * lines :]
    here, level = lax.axis_index("seq"), lax.axis_index("fsdp")
    owns = [pltpu.make_async_copy(block, gathered.at[here], local.at[0])]
    for a in range(lines):
        owns.append(pltpu.make_async_copy(srcs[a], outs[a].at[level], local.at[a + 1]))
    for own in owns:
        own.start()
    count = greet_seq(n)
    barrier = pltpu.get_barrier_semaphore()
    for ready, other in ((level > 0, level - 1), (level < depth - 1, level + 1)):

        @pl.when(ready)
        def _():
            pl.semaphore_signal(
                barrier, inc=1, device_id={"fsdp": jnp.clip(other, 0, depth - 1)}, device_id_type=MESH
            )

    count = count + (level > 0).astype(jnp.int32) + (level < depth - 1).astype(jnp.int32)
    pl.semaphore_wait(barrier, count)
    cross = crossed(block.shape[0], n)
    if not cross:
        owns[0].wait()
    along = gather_start(block, gathered, (send, recv), n)
    line = line_steps(srcs, outs, line_send, line_recv, depth)
    for i in range(max(len(along), len(line))):
        if i < len(line):
            line[i]()
        if i < len(along):
            along[i]()
    if cross:
        owns[0].wait()
    for own in owns[1:]:
        own.wait()


def first_gather(block, arrays, call):
    n, depth = lax.axis_size("seq"), lax.axis_size("fsdp")
    lines = len(arrays)
    anywhere = pl.BlockSpec(memory_space=pl.ANY)
    return pl.pallas_call(
        functools.partial(first_body, n=n, depth=depth, lines=lines),
        out_shape=[jax.ShapeDtypeStruct((n,) + block.shape, block.dtype)]
        + [jax.ShapeDtypeStruct((depth,) + array.shape, array.dtype) for array in arrays],
        in_specs=[anywhere] * (1 + lines),
        out_specs=[anywhere] * (1 + lines),
        scratch_shapes=[
            pltpu.SemaphoreType.DMA((1 + lines,)),
            pltpu.SemaphoreType.DMA((8,)),
            pltpu.SemaphoreType.DMA((8,)),
            pltpu.SemaphoreType.DMA((lines, 2, depth - 1)),
            pltpu.SemaphoreType.DMA((lines, 2, depth - 1)),
        ],
        compiler_params=pltpu.CompilerParams(collective_id=call, has_side_effects=True),
        cost_estimate=busy(60),
        name="first_gather",
    )(block, *arrays)


def last_body(*refs, n, count):
    srcs, outs = refs[:count], refs[count : 2 * count]
    local, send, recv = refs[2 * count :]
    here = lax.axis_index("seq")
    owns = [pltpu.make_async_copy(srcs[a], outs[a].at[here], local.at[a]) for a in range(count)]
    for own in owns:
        own.start()
    peers = greet_seq(n)
    pl.semaphore_wait(pltpu.get_barrier_semaphore(), peers)
    cross = [crossed(src.shape[0], n) for src in srcs]
    for a in range(count):
        if not cross[a]:
            owns[a].wait()
    steps = [gather_start(srcs[a], outs[a], (send.at[a], recv.at[a]), n) for a in range(count)]
    for i in range(max(len(part) for part in steps)):
        for part in steps:
            if i < len(part):
                part[i]()
    for a in range(count):
        if cross[a]:
            owns[a].wait()


def last_gather(arrays, call):
    n = lax.axis_size("seq")
    count = len(arrays)
    anywhere = pl.BlockSpec(memory_space=pl.ANY)
    return pl.pallas_call(
        functools.partial(last_body, n=n, count=count),
        out_shape=[jax.ShapeDtypeStruct((n,) + array.shape, array.dtype) for array in arrays],
        in_specs=[anywhere] * count,
        out_specs=[anywhere] * count,
        scratch_shapes=[
            pltpu.SemaphoreType.DMA((count,)),
            pltpu.SemaphoreType.DMA((count, 8)),
            pltpu.SemaphoreType.DMA((count, 8)),
        ],
        compiler_params=pltpu.CompilerParams(collective_id=call, has_side_effects=True),
        cost_estimate=busy(60),
        name="last_gather",
    )(*arrays)


def lay_cols_body(*refs, n, depth, groups, chunk, padded, total, front):
    out = refs[-1]
    if front:
        out[:, :front] = refs[0][:, :front].astype(F32)
    parts = refs[len(refs) - 1 - groups : -1]
    for g, part in enumerate(parts):
        for s in range(n):
            values = part[s].astype(F32)
            for j in range(depth):
                at = front + g * total + j * (total // depth) + s * chunk
                out[:, at : at + chunk] = values[:, j * padded : j * padded + chunk]


def lay_cols(parts, chunk, padded, total, first=None, front=0):
    n, rows, width = parts[0].shape
    depth = total // (n * chunk)
    step = rows // 5
    ins = [] if first is None else [first]
    specs = [] if first is None else [pl.BlockSpec((step, first.shape[1]), lambda i: (i, 0))]
    return pl.pallas_call(
        functools.partial(
            lay_cols_body, n=n, depth=depth, groups=len(parts), chunk=chunk, padded=padded,
            total=total, front=front,
        ),
        grid=(5,),
        out_shape=jax.ShapeDtypeStruct((rows, front + len(parts) * total), F32),
        in_specs=specs + [pl.BlockSpec((n, step, width), lambda i: (0, i, 0))] * len(parts),
        out_specs=pl.BlockSpec((step, front + len(parts) * total), lambda i: (i, 0)),
        compiler_params=pltpu.CompilerParams(vmem_limit_bytes=48 * 2**20),
        cost_estimate=busy(10),
        name="lay_cols",
    )(*ins, *parts)


def lay_rows_body(parts, out, *, n, chunk):
    for s in range(n):
        out[s * chunk : (s + 1) * chunk, :] = parts[s, :chunk, :].astype(F32)


def lay_rows(parts, chunk):
    n, _, width = parts.shape
    return pl.pallas_call(
        functools.partial(lay_rows_body, n=n, chunk=chunk),
        out_shape=jax.ShapeDtypeStruct((n * chunk, width), F32),
        in_specs=[pl.BlockSpec(memory_space=pltpu.VMEM)],
        out_specs=pl.BlockSpec(memory_space=pltpu.VMEM),
        compiler_params=pltpu.CompilerParams(vmem_limit_bytes=48 * 2**20),
        cost_estimate=busy(4),
        name="lay_rows",
    )(parts)


def lay_places_body(info, own, other, *outs, n, depth, chunk, padded, groups, total, wide):
    here = info[0]
    for s in range(n):
        place = here ^ s
        mine = (place & 1) == 0
        values = jnp.where(mine, own[place >> 1], other[place >> 1]).astype(F32)
        for g in range(groups):
            for j in range(depth):
                at = j * (total // depth) + s * chunk
                first = g * wide + j * padded
                outs[g][:, at : at + chunk] = values[:, first : first + chunk]


def lay_places(own, other, here, chunk, padded, total, groups, wide):
    half, rows, width = own.shape
    n = 2 * half
    depth = total // (n * chunk)
    step = rows // 5
    part = pl.BlockSpec((half, step, width), lambda i, info: (0, i, 0))
    return pl.pallas_call(
        functools.partial(
            lay_places_body, n=n, depth=depth, chunk=chunk, padded=padded, groups=groups,
            total=total, wide=wide,
        ),
        grid_spec=pltpu.PrefetchScalarGridSpec(
            num_scalar_prefetch=1,
            grid=(5,),
            in_specs=[part, part],
            out_specs=[pl.BlockSpec((step, total), lambda i, info: (i, 0))] * groups,
        ),
        out_shape=[jax.ShapeDtypeStruct((rows, total), F32)] * groups,
        compiler_params=pltpu.CompilerParams(vmem_limit_bytes=56 * 2**20),
        cost_estimate=busy(10),
        name="lay_places",
    )(here, own, other)


def lay_row_places_body(info, own, other, out, *, n, chunk):
    here = info[0]
    for s in range(n):
        place = here ^ s
        mine = (place & 1) == 0
        values = jnp.where(mine, own[place >> 1], other[place >> 1])
        out[s * chunk : (s + 1) * chunk, :] = values[:chunk].astype(F32)


def lay_row_places(own, other, here, chunk):
    half, _, width = own.shape
    n = 2 * half
    whole = pl.BlockSpec(memory_space=pltpu.VMEM)
    return pl.pallas_call(
        functools.partial(lay_row_places_body, n=n, chunk=chunk),
        in_specs=[pl.BlockSpec(memory_space=pltpu.SMEM), whole, whole],
        out_specs=whole,
        out_shape=jax.ShapeDtypeStruct((n * chunk, width), F32),
        compiler_params=pltpu.CompilerParams(vmem_limit_bytes=48 * 2**20),
        cost_estimate=busy(6),
        name="lay_row_places",
    )(here, own, other)


def key_scores(k, q, allowed):
    scores = lax.dot_general(k, q, (((0,), (0,)), ((), ())), preferred_element_type=F32)
    return scores if allowed is None else jnp.where(allowed, scores, NEG)


def block_masks(position, back, rows):
    key = lax.broadcasted_iota(jnp.int32, (rows, rows), 0)
    query = lax.broadcasted_iota(jnp.int32, (rows, rows), 1)
    masks = []
    for distance in range(back, 0, -1):
        reached = jnp.broadcast_to(position >= distance, (rows, rows))
        masks.append((key > query) & reached if distance == back else reached)
    return masks + [key <= query]


def attend_body(info, q_ref, *refs, back):
    keys, values = refs[: back + 2], refs[back + 2 : 2 * back + 4]
    out_ref, norm_ref = refs[2 * back + 4 :]
    q = q_ref[...]
    masks = [None] + block_masks(info[1], back, q.shape[1])
    scores = [key_scores(k[...], q, mask) for k, mask in zip(keys, masks)]
    top = functools.reduce(jnp.maximum, (jnp.max(part, 0, keepdims=True) for part in scores))
    total = jnp.zeros_like(top)
    out = jnp.zeros(q.shape, F32)
    for part, v in zip(scores, values):
        weights = jnp.exp(part - top)
        total += jnp.sum(weights, 0, keepdims=True)
        out += jnp.dot(v[...], weights.astype(jnp.bfloat16), preferred_element_type=F32)
    out_ref[...] = out / total
    norm_ref[0] = jnp.broadcast_to(top + jnp.log(total), norm_ref.shape[1:])


def attend_back_body(info, q_ref, grad_ref, out_ref, norm_ref, *refs, back):
    count = back + 2
    keys, values = refs[:count], refs[count : 2 * count]
    gq_ref, gk_meta, gv_meta, gk_ref, gv_ref = refs[2 * count :]
    turn = pl.program_id(1)
    q, grad = q_ref[...], grad_ref[...]
    norm = norm_ref[0][0:1]
    shared = jnp.sum(grad.astype(F32) * out_ref[...], 0, keepdims=True)
    masks = [None] + block_masks(info[1], back, q.shape[1])

    @pl.when(turn == 0)
    def _():
        for ref in (gk_meta, gv_meta, gk_ref, gv_ref):
            ref[...] = jnp.zeros_like(ref)

    contract = (((1,), (1,)), ((), ()))
    gq = jnp.zeros(q.shape, F32)
    for i in range(count):
        k, v = keys[i][...], values[i][...]
        weights = jnp.exp(key_scores(k, q, masks[i]) - norm)
        grad_weights = lax.dot_general(
            v, grad, (((0,), (0,)), ((), ())), preferred_element_type=F32
        )
        grad_scores = (weights * (grad_weights - shared)).astype(jnp.bfloat16)
        gq += jnp.dot(k, grad_scores, preferred_element_type=F32)
        gk = lax.dot_general(q, grad_scores, contract, preferred_element_type=F32)
        gv = lax.dot_general(
            grad, weights.astype(jnp.bfloat16), contract, preferred_element_type=F32
        )
        if i == 0:
            gk_meta[...] += gk
            gv_meta[...] += gv
        else:
            gk_ref[i - 1] += gk
            gv_ref[i - 1] += gv
    gq_ref[...] = gq * HD ** (-0.5)


def attend_specs(heads, groups, tokens, meta, n, back):
    size = heads // groups
    head = pl.BlockSpec((HD, tokens), lambda g, j, info: (g * size + j, 0))

    def sides(first):
        specs = [pl.BlockSpec((HD, meta), lambda g, j, info: (first + g, 0))]
        for distance in range(back, -1, -1):
            specs.append(
                pl.BlockSpec(
                    (HD, tokens),
                    lambda g, j, info, distance=distance: (
                        first + g, lax.rem(info[0] - distance + n, n),
                    ),
                )
            )
        return specs

    norm = pl.BlockSpec((1, 8, tokens), lambda g, j, info: (g * size + j, 0, 0))
    return head, sides(0) + sides(groups), norm


def attend(info, q_t, kv_t, meta_t, heads, groups, n, back):
    tokens, meta = q_t.shape[1], meta_t.shape[1]
    head, kv, norm = attend_specs(heads, groups, tokens, meta, n, back)
    return pl.pallas_call(
        functools.partial(attend_body, back=back),
        grid_spec=pltpu.PrefetchScalarGridSpec(
            num_scalar_prefetch=1,
            grid=(groups, heads // groups),
            in_specs=[head] + kv,
            out_specs=[head, norm],
        ),
        out_shape=[
            jax.ShapeDtypeStruct(q_t.shape, F32),
            jax.ShapeDtypeStruct((heads, 8, tokens), F32),
        ],
        compiler_params=pltpu.CompilerParams(vmem_limit_bytes=40 * 2**20),
        cost_estimate=busy(25),
        name="attend",
    )(info, q_t, *(([meta_t] + [kv_t] * (back + 1)) * 2))


def attend_back(info, q_t, grad_t, out_t, norms, kv_t, meta_t, heads, groups, n, back):
    tokens, meta = q_t.shape[1], meta_t.shape[1]
    head, kv, norm = attend_specs(heads, groups, tokens, meta, n, back)
    cols = groups * HD
    window = pl.BlockSpec((back + 1, HD, tokens), lambda g, j, info: (0, g, 0))
    side = pl.BlockSpec((HD, meta), lambda g, j, info: (g, 0))
    return pl.pallas_call(
        functools.partial(attend_back_body, back=back),
        grid_spec=pltpu.PrefetchScalarGridSpec(
            num_scalar_prefetch=1,
            grid=(groups, heads // groups),
            in_specs=[head, head, head, norm] + kv,
            out_specs=[head, side, side, window, window],
        ),
        out_shape=[
            jax.ShapeDtypeStruct(q_t.shape, F32),
            jax.ShapeDtypeStruct((cols, meta), F32),
            jax.ShapeDtypeStruct((cols, meta), F32),
            jax.ShapeDtypeStruct((back + 1, cols, tokens), F32),
            jax.ShapeDtypeStruct((back + 1, cols, tokens), F32),
        ],
        compiler_params=pltpu.CompilerParams(vmem_limit_bytes=48 * 2**20),
        cost_estimate=busy(50),
        name="attend_back",
    )(info, q_t, grad_t, out_t, norms, *(([meta_t] + [kv_t] * (back + 1)) * 2))


def swap(values, mask):
    return lax.ppermute(values, "seq", [(i, i ^ mask) for i in range(lax.axis_size("seq"))])


def near_places(block):
    return [block] + [swap(block, mask) for mask in range(2, lax.axis_size("seq"), 2)]


def turned_sum(blocks):
    n = lax.axis_size("fsdp")
    here = lax.axis_index("fsdp")
    total = lax.dynamic_index_in_dim(blocks, here, 0, False)
    for k in range(1, n):
        part = lax.dynamic_index_in_dim(blocks, (here + k) % n, 0, False)
        total = total + lax.ppermute(part, "fsdp", [(i, (i + k) % n) for i in range(n)])
    return total


def in_rows(values):
    return with_layout_constraint(values, Layout(major_to_minor=(0, 1)))


def pad_to(values, size, axis):
    widths = [(0, 0)] * values.ndim
    widths[axis] = (0, size - values.shape[axis])
    return jnp.pad(values, widths)


def norm_fwd(values, gains):
    inverse = lax.rsqrt(jnp.mean(values * values, -1, keepdims=True) + EPS)
    return (values * inverse * gains, inverse)


def norm_back(values, inverse, gains, grads):
    weighted = grads * gains
    mean_term = jnp.mean(values * weighted, -1, keepdims=True)
    return (
        inverse * weighted - values * inverse**3 * mean_term,
        jnp.sum(grads * values * inverse, 0),
    )


def silu_slope(values):
    sigmoid = jax.nn.sigmoid(values)
    return sigmoid * (1.0 + values * (1.0 - sigmoid))


def product(one, two, dims, exact=False, out=F32):
    return lax.dot_general(
        one,
        two,
        ((dims[:1], dims[1:]), ((), ())),
        preferred_element_type=F32,
        precision=HIGH if exact else None,
    ).astype(out)


def shards(
    inputs, starts, norm_gain, in_weight, conv_weight, conv_bias, xproj_weight, dtproj_weight, dt_bias,
    log_decay, skip_gain, meta_tokens, attn_weight, mamba_weight, attn_gain, mamba_gain, ffn_gain,
    gate_weight, up_weight, down_weight, cotangent,
):
    low = jnp.bfloat16
    n, depth = lax.axis_size("seq"), lax.axis_size("fsdp")
    here = lax.axis_index("seq")
    tokens, width = inputs.shape[1:]
    rows = n * tokens
    q_cols, kv_cols = HQ * HD, HK * HD
    qkv_cols = q_cols + 2 * kv_cols
    group_size = HQ // HK
    inner = EI // n
    hidden_units = gate_weight.shape[1]
    units = hidden_units // n
    shard_rows = width // depth

    if n <= GAP:
        carries = jnp.array([0] + [1] * (n - 1), jnp.int32)
        position = here
    else:
        flags = lax.all_gather(starts[0, 0], "seq")
        carries = 1 - flags
        blocks = jnp.arange(n)
        position = here - jnp.max(jnp.where((flags == 1) & (blocks <= here), blocks, 0))
    info = jnp.concatenate([jnp.zeros((1,), jnp.int32), carries])

    def up_to(size, step):
        return -(-size // step) * step

    chunk, unit_chunk = inner // depth, units // depth
    chunk_pad, unit_pad = up_to(chunk, 16), up_to(unit_chunk, 16)
    channels, own_units = depth * chunk_pad, depth * unit_pad
    inner_pad, units_pad = up_to(channels, LANES), up_to(own_units, LANES)

    def own_cols(weight, base, total, padded, width, here=here):
        size = total // (depth * n)
        parts = [
            pad_to(
                lax.dynamic_slice_in_dim(weight, base + j * (total // depth) + here * size, size, 1),
                padded,
                1,
            )
            for j in range(depth)
        ]
        return pad_to(jnp.concatenate(parts, 1), width, 1)

    def own_rows(weight, padded, here=here):
        size = weight.shape[0] // n
        return pad_to(lax.dynamic_slice_in_dim(weight, here * size, size, 0), padded, 0)

    def along_depth(values):
        return lax.all_gather(values, "fsdp")

    small_cols = KC + RDT + 2 * NS + RDT + NS + 3
    small = jnp.concatenate(
        [
            conv_weight, conv_bias[:, None], xproj_weight, dtproj_weight, dt_bias[:, None], log_decay,
            skip_gain[:, None],
        ],
        1,
    )
    own_in = own_cols(in_weight, qkv_cols, EI, chunk_pad, inner_pad)
    own_z = own_cols(in_weight, qkv_cols + EI, EI, chunk_pad, inner_pad)
    gains = pad_to(jnp.stack([norm_gain, attn_gain, mamba_gain, ffn_gain], 0), 16, 0)
    hidden_all, w_in, small_full, gain_rows, meta_rows = first_gather(
        inputs[0],
        [jnp.concatenate([own_in, own_z], 1), own_rows(small, chunk_pad), gains, meta_tokens],
        1,
    )
    w_in = w_in.reshape(width, 2 * inner_pad)
    gain_norm, gain_attn, gain_mamba, gain_ffn = (
        gain_rows[:, i].reshape(-1).astype(F32) for i in range(4)
    )
    meta_rows = meta_rows.reshape(META, width)
    here_at = here.astype(jnp.int32)[None]

    small_full, later = lax.optimization_barrier((small_full, here))
    small_full = pad_to(small_full.reshape(channels, -1), inner_pad, 0).astype(F32)
    ends = np.cumsum([0, KC, 1, RDT + 2 * NS, RDT, 1, NS, 1])
    taps, bias, w_select, w_steps, b_steps, a_logs, skip = (
        small_full[:, a:b] for a, b in zip(ends[:-1], ends[1:])
    )
    taps_t, bias, b_steps, skip = taps.T, bias.T, b_steps.T, skip.T
    a_t = -jnp.exp(a_logs.T)

    piece = up_to(-(-shard_rows // n), 16)
    w_mamba = along_depth(own_rows(mamba_weight, chunk_pad, later)).reshape(channels, width)
    w_mamba = pad_to(w_mamba, inner_pad, 0)
    def attn_piece(weight):
        return lax.dynamic_slice_in_dim(pad_to(weight, n * piece, 0), later * piece, piece, 0)

    own_attn = along_depth(
        jnp.concatenate([attn_piece(in_weight[:, :qkv_cols]), attn_piece(attn_weight)], 1)
    )
    hidden = inputs[0].astype(F32)
    normed_all, _ = norm_fwd(hidden_all.astype(F32), gain_norm)
    normed_all = normed_all.astype(low).reshape(rows, width)
    normed, inv_in = norm_fwd(hidden, gain_norm)
    normed = normed.astype(low)
    mixer_in = product(normed_all, w_in[:, :inner_pad], (1, 0), out=low)
    z_gate = product(normed_all, w_in[:, inner_pad:], (1, 0), out=low).astype(F32)
    conv_pre = conv_fwd(info, mixer_in, taps_t, bias, n)
    mixed = jax.nn.silu(conv_pre)

    def all_sum(values, call):
        laid = values.reshape(values.shape[0], n, tokens).transpose(1, 0, 2)
        laid = pad_to(laid, up_to(values.shape[0], 16), 1)
        total = seq_total(laid, call)
        return total.transpose(1, 0, 2).reshape(-1, rows)[: values.shape[0]]

    part = product(w_select, mixed, (0, 1), exact=True)
    selected = all_sum(part, 2)
    selected, own_attn = lax.optimization_barrier((selected, own_attn))
    all_attn = lax.all_gather(own_attn, "seq").transpose(1, 0, 2, 3)
    all_attn = all_attn.reshape(depth, n * piece, -1)[:, :shard_rows].reshape(width, -1)
    w_qkv, w_attn = all_attn[:, :qkv_cols], all_attn[:, qkv_cols:]
    w_q, w_kv = w_qkv[:, :q_cols], w_qkv[:, q_cols:]
    ranks, b_sel, c_sel = selected[:RDT], selected[RDT : RDT + NS], selected[RDT + NS :]
    dt_pre = product(ranks, w_steps, (0, 1), exact=True) + b_steps
    steps = jax.nn.softplus(dt_pre)
    steps, last, last_cotangent = lax.optimization_barrier((steps, later, cotangent))
    y_scan, firsts = scan_fwd(info, steps, mixed, b_sel, c_sel, a_t, n)
    w_units = along_depth(
        jnp.concatenate(
            [
                own_cols(gate_weight, 0, hidden_units, unit_pad, units_pad, last),
                own_cols(up_weight, 0, hidden_units, unit_pad, units_pad, last),
            ],
            1,
        )
    ).reshape(width, 2 * units_pad)
    w_down = along_depth(own_rows(down_weight, unit_pad, last)).reshape(own_units, width)
    w_down = pad_to(w_down, units_pad, 0)
    grad_out_all = lax.all_gather(last_cotangent[0], "seq").reshape(rows, width)
    y_full = y_scan + skip * mixed
    silu_z = jax.nn.silu(z_gate)
    mamba_low = (y_full * silu_z).astype(low)
    mamba_out = seq_reduce(
        in_rows(product(mamba_low, w_mamba, (1, 0), out=low)).reshape(n, tokens, width), 3
    )

    blocks_back = WIN // tokens
    attend_at = jnp.stack([here, position]).astype(jnp.int32)
    heads = (HQ, HK, n, blocks_back)
    queries = product(w_q, normed, (0, 1), out=low) * HD ** (-0.5)
    keyvals = product(w_kv, normed_all, (0, 1), out=low)
    meta_float = meta_rows.astype(F32)
    meta_normed, meta_inv = norm_fwd(meta_float, gain_norm)
    meta_low = meta_normed.astype(low)
    meta_kv = product(w_kv, meta_low, (0, 1), out=low)
    contexts, log_norms = attend(attend_at, queries, keyvals, meta_kv, *heads)
    attended = contexts.astype(low)
    attn_out = product(attended, w_attn, (0, 0))

    attn_normed, attn_inv = norm_fwd(attn_out, gain_attn)
    mamba_normed, mamba_inv = norm_fwd(mamba_out, gain_mamba)
    middle = hidden + 0.5 * (attn_normed + mamba_normed)
    ffn_normed, ffn_inv = norm_fwd(middle, gain_ffn)
    ffn_all = seq_gather(ffn_normed.astype(low), 4).reshape(rows, width)
    both_pre = product(ffn_all, w_units, (1, 0))
    gate_pre, up_pre = both_pre[:, :units_pad], both_pre[:, units_pad:]
    grad_act = product(grad_out_all, w_down, (1, 1))
    silu_gate = jax.nn.silu(gate_pre)
    activated = (silu_gate * up_pre).astype(low)
    grad_units = jnp.concatenate(
        [
            (grad_act * up_pre * silu_slope(gate_pre)).astype(low),
            (grad_act * silu_gate).astype(low),
        ],
        1,
    )
    grad_ffn_part = in_rows(product(grad_units, w_units, (1, 1), out=low))
    down_part = product(activated, w_down, (1, 0), out=low)
    grad_w_units = product(ffn_all, grad_units, (0, 0), out=low)
    grad_w_down = product(activated, grad_out_all, (0, 0), out=low)[:own_units]
    grad_ffn_part, grad_w_units, grad_w_down, down_part = lax.optimization_barrier(
        (grad_ffn_part, grad_w_units, grad_w_down, down_part)
    )
    grad_ffn_in = seq_reduce(grad_ffn_part.reshape(n, tokens, width), 5)

    def depth_sum(part):
        return lax.psum_scatter(part, "fsdp", scatter_dimension=0, tiled=True)

    own_w_units, own_w_down = depth_sum(grad_w_units), depth_sum(grad_w_down)
    down_sum = lax.psum_scatter(down_part, "seq", scatter_dimension=0, tiled=True)
    grad_out = cotangent[0].astype(F32)
    grad_mid_norm, grad_g_ffn = norm_back(middle, ffn_inv, gain_ffn, grad_ffn_in)
    grad_middle = grad_out + grad_mid_norm
    grad_attn_out, grad_g_attn = norm_back(attn_out, attn_inv, gain_attn, 0.5 * grad_middle)
    grad_mamba_out, grad_g_mamba = norm_back(mamba_out, mamba_inv, gain_mamba, 0.5 * grad_middle)
    grad_attn_low = grad_attn_out.astype(low)
    grad_context = product(w_attn, grad_attn_low, (1, 1), out=low)
    grad_queries, grad_k_meta, grad_v_meta, grad_keys, grad_values = attend_back(
        attend_at, queries, grad_context, contexts, log_norms, keyvals, meta_kv, *heads
    )
    grad_queries, own_w_units, own_w_down = lax.optimization_barrier(
        (grad_queries, own_w_units, own_w_down)
    )
    grad_meta_kv = jnp.concatenate([grad_k_meta, grad_v_meta], 0)
    grad_kv_blocks = lax.dynamic_update_slice_in_dim(
        jnp.zeros((blocks_back + n, 2 * kv_cols, tokens), low),
        jnp.concatenate([grad_keys, grad_values], 1).astype(low),
        here,
        0,
    )[blocks_back:]
    grad_keyvals = seq_reduce(grad_kv_blocks, 7)
    grad_qkv = jnp.concatenate([grad_queries, grad_keyvals], 0).astype(low)
    grad_meta_low = product(grad_meta_kv, w_kv.astype(F32), (0, 1), exact=True)
    grad_meta, grad_g_meta = norm_back(meta_float, meta_inv, gain_norm, grad_meta_low)

    meta_high = grad_meta_kv.astype(low)
    meta_rest = (grad_meta_kv - meta_high.astype(F32)).astype(low)
    qkv_pad, attn_pad = up_to(qkv_cols, LANES), up_to(width, LANES)
    meta_side = ((q_cols, qkv_pad - qkv_cols), (0, 0))
    grad_w_qkv = product(
        jnp.concatenate([normed, meta_low, meta_low], 0),
        jnp.concatenate(
            [pad_to(grad_qkv, qkv_pad, 0), jnp.pad(meta_high, meta_side), jnp.pad(meta_rest, meta_side)],
            1,
        ),
        (0, 1),
        out=low,
    )
    grad_w_attn = product(attended, pad_to(grad_attn_low, attn_pad, 1), (1, 0), out=low)
    grad_attn = jnp.concatenate([grad_w_qkv, grad_w_attn], 1).reshape(depth, shard_rows, -1)
    meta_own = META // depth
    grad_gains = jnp.stack([grad_g_attn, grad_g_mamba, grad_g_ffn], 0).astype(low)
    grad_gains = grad_gains.reshape(3, depth, shard_rows).transpose(1, 0, 2)
    spare = jnp.concatenate(
        [grad_meta.astype(low).reshape(depth, meta_own, width), pad_to(grad_gains, width, 2)], 1
    )
    spare = pad_to(spare, up_to(meta_own + 3, 16), 1)
    piece = up_to(-(-(shard_rows + spare.shape[1]) // n), 16)
    grad_attn = jnp.concatenate([grad_attn, pad_to(spare, qkv_pad + attn_pad, 2)], 1)
    grad_attn = pad_to(grad_attn, n * piece, 1)
    grad_attn = grad_attn.reshape(depth, n, piece, -1).transpose(1, 0, 2, 3)
    grad_attn = grad_attn.reshape(n * depth * piece, -1)

    grad_mamba_all = seq_gather(grad_mamba_out.astype(low), 6).reshape(rows, width)
    grad_w_mamba = product(mamba_low, grad_mamba_all, (0, 0), out=low)[:channels]
    grad_mix = product(grad_mamba_all, w_mamba, (1, 1))
    grad_y = grad_mix * silu_z
    grad_z = (grad_mix * y_full * silu_slope(z_gate)).astype(low)
    grad_w_z = product(normed_all, grad_z, (0, 0), out=low)
    grad_y, grad_w_z, grad_w_mamba, grad_attn, own_w_units, own_w_down, down_sum = (
        lax.optimization_barrier(
            (grad_y, grad_w_z, grad_w_mamba, grad_attn, own_w_units, own_w_down, down_sum)
        )
    )
    own_z, own_mamba = depth_sum(grad_w_z), depth_sum(grad_w_mamba)
    grad_attn = lax.psum_scatter(grad_attn, "seq", scatter_dimension=0, tiled=True)
    near_units, near_down = near_places(own_w_units), near_places(own_w_down)
    grad_skip = jnp.sum(grad_y * mixed, 0, keepdims=True)
    grad_steps, grad_x, grad_b, grad_c, grad_a = scan_bwd(
        info, steps, mixed, b_sel, c_sel, grad_y, a_t, firsts, n
    )
    grad_steps, near_units, near_down, own_z, own_mamba = lax.optimization_barrier(
        (grad_steps, near_units, near_down, own_z, own_mamba)
    )
    near_units, near_down = jnp.stack(near_units, 0), jnp.stack(near_down, 0)
    all_w_units, all_w_down = (near_units, swap(near_units, 1)), (near_down, swap(near_down, 1))
    grad_dt_pre = grad_steps * jax.nn.sigmoid(dt_pre)
    grad_dt_bias = jnp.sum(grad_dt_pre, 0, keepdims=True)
    grad_ranks = product(w_steps, grad_dt_pre, (0, 1), exact=True)
    grad_selected = all_sum(jnp.concatenate([grad_ranks, grad_b, grad_c], 0), 8)
    grad_selected, grad_attn = lax.optimization_barrier((grad_selected, grad_attn))
    own_attn = depth_sum(grad_attn)
    grad_w_steps = product(grad_dt_pre, ranks, (0, 1), exact=True)
    grad_w_select = product(mixed, grad_selected, (0, 1), exact=True)
    grad_mixed = grad_y * skip + grad_x + product(grad_selected, w_select, (0, 1), exact=True)
    grad_conv = grad_mixed * silu_slope(conv_pre)
    grad_mixer, grad_taps, grad_bias = conv_bwd(info, grad_conv, mixer_in, taps_t, n)

    grad_w_x = product(normed_all, grad_mixer, (0, 0), out=low)
    grad_small = jnp.concatenate(
        [
            grad_taps.T, grad_bias.T, grad_w_select, grad_w_steps, grad_dt_bias.T, (grad_a * a_t).T,
            grad_skip.T,
        ],
        1,
    )[:channels].astype(low)
    grad_in = jnp.concatenate([grad_mixer, grad_z], 1)
    grad_in, grad_w_x, grad_small = lax.optimization_barrier((grad_in, grad_w_x, grad_small))
    own_x, own_small = depth_sum(grad_w_x), depth_sum(grad_small)
    grad_normed = in_rows(product(grad_in, w_in, (1, 1), out=low)).reshape(n, tokens, width)
    grad_normed = seq_reduce(grad_normed, 9)
    layer_out = middle + down_sum.astype(F32)
    grad_normed = grad_normed + product(grad_qkv, w_qkv, (0, 1))
    grad_input_norm, grad_g_in = norm_back(hidden, inv_in, gain_norm, grad_normed)
    inputs_grad = (grad_middle + grad_input_norm)[None]
    grad_g_in = turned_sum((grad_g_in + grad_g_meta).reshape(depth, shard_rows))
    own_small = jnp.concatenate(
        [
            pad_to(own_small, SMALL, 1),
            pad_to(pad_to(grad_g_in[None], 2 * SMALL, 1).reshape(2, SMALL), 16, 0).astype(low),
        ],
        0,
    )

    all_small, all_x, all_z, all_mamba, all_attn = last_gather(
        [own_small, own_x, own_z, own_mamba, own_attn], 10
    )
    all_gain = all_small[:, chunk_pad : chunk_pad + 2].reshape(n, -1)[:, :shard_rows].astype(F32)
    all_small = all_small[:, :chunk_pad]
    grad_w_gate, grad_w_up = lay_places(
        *all_w_units, here_at, unit_chunk, unit_pad, hidden_units, 2, units_pad
    )
    grad_w_down = lay_row_places(*all_w_down, here_at, unit_chunk)
    grad_w_mamba = lay_rows(all_mamba, chunk)
    grad_attn = all_attn.reshape(n * piece, -1)
    grad_w_attn = grad_attn[:shard_rows, qkv_pad : qkv_pad + width].astype(F32)
    gains = grad_attn[shard_rows + meta_own : shard_rows + meta_own + 3, :shard_rows].astype(F32)
    grad_meta = grad_attn[shard_rows : shard_rows + meta_own, :width].astype(F32)
    grad_w_proj = lay_cols([all_x, all_z], chunk, chunk_pad, EI, grad_attn[:shard_rows], qkv_cols)
    grad_small = lay_rows(all_small, chunk)[:, :small_cols]
    grad_taps, grad_bias, grad_w_select, grad_w_steps, grad_dt_bias, grad_decay, grad_skip = (
        grad_small[:, a:b] for a, b in zip(ends[:-1], ends[1:])
    )

    return (
        layer_out.astype(low)[None],
        inputs_grad,
        jnp.sum(all_gain, 0),
        grad_w_proj,
        grad_taps,
        grad_bias[:, 0],
        grad_w_select,
        grad_w_steps,
        grad_dt_bias[:, 0],
        grad_decay,
        grad_skip[:, 0],
        grad_meta,
        grad_w_attn,
        grad_w_mamba,
        gains[0],
        gains[1],
        gains[2],
        grad_w_gate,
        grad_w_up,
        grad_w_down,
    )


def solution(mesh):
    in_specs = (
        P("fsdp", "seq", None),
        P("fsdp", "seq"),
        P("fsdp"),
        P("fsdp", None),
        P("fsdp", None),
        P("fsdp"),
        P("fsdp", None),
        P("fsdp", None),
        P("fsdp"),
        P("fsdp", None),
        P("fsdp"),
        P("fsdp", None),
        P("fsdp", None),
        P("fsdp", None),
        P("fsdp"),
        P("fsdp"),
        P("fsdp"),
        P("fsdp", None),
        P("fsdp", None),
        P("fsdp", None),
        P("fsdp", "seq", None),
    )
    out_specs = (
        P("fsdp", "seq", None),
        P("fsdp", "seq", None),
        P("fsdp"),
        P("fsdp", None),
        P("fsdp", None),
        P("fsdp"),
        P("fsdp", None),
        P("fsdp", None),
        P("fsdp"),
        P("fsdp", None),
        P("fsdp"),
        P("fsdp", None),
        P("fsdp", None),
        P("fsdp", None),
        P("fsdp"),
        P("fsdp"),
        P("fsdp"),
        P("fsdp", None),
        P("fsdp", None),
        P("fsdp", None),
    )
    return jax.shard_map(shards, mesh=mesh, in_specs=in_specs, out_specs=out_specs, check_vma=False)
```

```python
import functools

import jax
import jax.numpy as jnp
import numpy as np
from jax import lax
from jax.experimental import pallas as pl
from jax.experimental.layout import Layout, with_layout_constraint
from jax.experimental.pallas import tpu as pltpu
from jax.sharding import PartitionSpec as P

HQ = 25
HK = 5
HD = 64
EI = 3200
NS = 16
KC = 4
RDT = 100
META = 128
WIN = 1024
GAP = 8
STEP = 2048
LOG2E = 1.4426950408889634
NEG = -jnp.inf

EPS = 1e-05
HIGH = lax.Precision.HIGHEST
LANES = 128
CHUNK = 128
F32 = jnp.float32
MESH = pl.DeviceIdType.MESH


def fold_rows(first, second, level):
    bit = (lax.broadcasted_iota(jnp.int32, first.shape, 0) >> level) & 1
    upper = bit == 0
    return jnp.where(upper, first, second) + pltpu.roll(
        jnp.where(upper, second, first), 8 - (1 << level), 0
    )


def fold_in(stack, part):
    level = 0
    while stack and stack[-1][0] == level:
        part = fold_rows(stack.pop()[1], part, level)
        level += 1
    stack.append((level, part))


def fold_in_down(stack, part):
    level = 0
    while stack and stack[-1][0] == level:
        part = fold_rows(part, stack.pop()[1], level)
        level += 1
    stack.append((level, part))


def halves(part):
    return part[:8] + part[8:]


def scan_fwd_body(info, dt_ref, x_ref, b_ref, c_ref, a_ref, y_ref, first_ref, state):
    block, piece = pl.program_id(0), pl.program_id(1)
    tiles = a_ref.shape[1] // LANES
    keep = jnp.where(piece == 0, info[1 + block], 1).astype(F32)

    @pl.when((block == 0) & (piece == 0))
    def _():
        state[...] = jnp.zeros_like(state)

    first = state[...] * keep
    first_ref[0] = first
    a2 = a_ref[...] * LOG2E

    def cut(values, l):
        return values[:, l * LANES : (l + 1) * LANES]

    def group(g, carried):
        bt, ct, hs = carried
        stacks = [[] for _ in range(tiles)]
        hs = list(hs)
        for k in range(8):
            bk = jnp.broadcast_to(bt[:, k : k + 1], (NS, LANES))
            ck = jnp.broadcast_to(ct[:, k : k + 1], (NS, LANES))
            for l in range(tiles):
                lane = slice(l * LANES, (l + 1) * LANES)
                dtk = dt_ref[g, k : k + 1, lane]
                uk = dtk * x_ref[g, k : k + 1, lane]
                hs[l] = jnp.exp2(dtk * cut(a2, l)) * hs[l] + uk * bk
                fold_in(stacks[l], halves(hs[l] * ck))
        for l in range(tiles):
            y_ref[g, :, l * LANES : (l + 1) * LANES] = stacks[l][0][1]
        return pltpu.roll(bt, LANES - 8, 1), pltpu.roll(ct, LANES - 8, 1), tuple(hs)

    start = tuple(cut(first, l) for l in range(tiles))
    _, _, hs = lax.fori_loop(0, CHUNK // 8, group, (b_ref[...], c_ref[...], start))
    for l in range(tiles):
        state[:, l * LANES : (l + 1) * LANES] = hs[l]


def spread_lanes(bc_ref, wide, both):
    rows = lax.broadcasted_iota(jnp.int32, (NS, LANES), 0)
    lanes = lax.broadcasted_iota(jnp.int32, (NS, LANES), 1)
    own = (lanes % NS == rows) & (lanes < 4 * NS)

    def lay(g, _):
        for k in range(8):
            span = pl.ds(pl.multiple_of((g * 8 + k) * NS, NS), NS)
            wide[span, :] = jnp.where(own, bc_ref[g, k : k + 1, :], 0.0).astype(jnp.bfloat16)
        return 0

    lax.fori_loop(0, CHUNK // 8, lay, 0)
    source = lax.broadcasted_iota(jnp.int32, (LANES, 2 * LANES), 0)
    target = lax.broadcasted_iota(jnp.int32, (LANES, 2 * LANES), 1)
    ones = (source // (2 * NS) == target // LANES).astype(jnp.bfloat16)

    def multiply(i, _):
        span = pl.ds(pl.multiple_of(i * STEP, STEP), STEP)
        both[span, :] = jnp.dot(wide[span, :], ones, preferred_element_type=F32)
        return 0

    lax.fori_loop(0, CHUNK * NS // STEP, multiply, 0)


def scan_bwd_body(
    info, dt_ref, x_ref, bc_ref, gy_ref, a_ref, first_ref,
    gdt_ref, gx_ref, gb_ref, gc_ref, ga_ref, carry, states, decays, wide, both, lanes_c,
):
    turn, piece = pl.program_id(0), pl.program_id(1)
    n_blocks, pieces = pl.num_programs(0), pl.num_programs(1)
    tiles = a_ref.shape[1] // LANES
    after = jnp.minimum(n_blocks - turn, n_blocks - 1)
    keep = jnp.where(piece == 0, info[1 + after], 1).astype(F32)
    lanes_b = wide

    @pl.when((turn == 0) & (piece == 0))
    def _():
        carry[...] = jnp.zeros_like(carry)
        ga_ref[...] = jnp.zeros_like(ga_ref)

    def cut(values, l):
        return values[:, l * LANES : (l + 1) * LANES]

    spread_lanes(bc_ref, wide, both)
    a2 = a_ref[...] * LOG2E

    def again(g, hs):
        hs = list(hs)
        for k in range(8):
            span = pl.ds(pl.multiple_of((g * 8 + k) * NS, NS), NS)
            bk = both[span, :LANES]
            for l in range(tiles):
                lane = slice(l * LANES, (l + 1) * LANES)
                dtk = dt_ref[g, k : k + 1, lane]
                uk = dtk * x_ref[g, k : k + 1, lane]
                decay = jnp.exp2(dtk * cut(a2, l))
                hs[l] = decay * hs[l] + uk * bk
                decays[g * 8 + k, :, lane] = decay
                states[g * 8 + k + 1, :, lane] = hs[l]
        return tuple(hs)

    states[0] = first_ref[0]
    lax.fori_loop(0, CHUNK // 8, again, tuple(cut(first_ref[0], l) for l in range(tiles)))

    def group(turn_g, gs):
        g = CHUNK // 8 - 1 - turn_g
        gs = list(gs)
        logs, drives = [[] for _ in range(tiles)], [[] for _ in range(tiles)]
        sums = [None] * tiles
        for k in reversed(range(8)):
            t = g * 8 + k
            span = pl.ds(pl.multiple_of(t * NS, NS), NS)
            bk, ck = both[span, :LANES], both[span, LANES:]
            to_b = to_c = None
            for l in range(tiles):
                lane = slice(l * LANES, (l + 1) * LANES)
                gyk = gy_ref[g, k : k + 1, lane]
                dtk = dt_ref[g, k : k + 1, lane]
                uk = dtk * x_ref[g, k : k + 1, lane]
                grad = ck * gyk + gs[l]
                gs[l] = decays[t, :, lane] * grad
                log = gs[l] * states[t, :, lane]
                fold_in_down(logs[l], halves(log * cut(a_ref[...], l)))
                fold_in_down(drives[l], halves(grad * bk))
                part_b = grad * uk
                part_c = states[t + 1, :, lane] * gyk
                to_b = part_b if to_b is None else to_b + part_b
                to_c = part_c if to_c is None else to_c + part_c
                part_a = log * dtk
                sums[l] = part_a if sums[l] is None else sums[l] + part_a
            lanes_b[span, :] = to_b.astype(jnp.bfloat16)
            lanes_c[span, :] = to_c.astype(jnp.bfloat16)
        for l in range(tiles):
            lane = slice(l * LANES, (l + 1) * LANES)
            driven = drives[l][0][1]
            gdt_ref[g, :, lane] = logs[l][0][1] + driven * x_ref[g, :, lane]
            gx_ref[g, :, lane] = driven * dt_ref[g, :, lane]
            ga_ref[:, lane] += sums[l]
        return tuple(gs)

    held = tuple(carry[:, l * LANES : (l + 1) * LANES] * keep for l in range(tiles))
    gs = lax.fori_loop(0, CHUNK // 8, group, held)
    for l in range(tiles):
        carry[:, l * LANES : (l + 1) * LANES] = gs[l]

    lane_ids = lax.broadcasted_iota(jnp.int32, (NS, LANES), 1)
    ones = jnp.ones((LANES, LANES), jnp.bfloat16)

    def collect(i, carried):
        gbt, gct = carried
        span = pl.ds(pl.multiple_of(i * STEP, STEP), STEP)
        sum_b = jnp.dot(lanes_b[span, :], ones, preferred_element_type=F32)
        sum_c = jnp.dot(lanes_c[span, :], ones, preferred_element_type=F32)
        for k in range(STEP // NS):
            here = lane_ids == i * (STEP // NS) + k
            gbt = jnp.where(here, sum_b[k * NS : (k + 1) * NS], gbt)
            gct = jnp.where(here, sum_c[k * NS : (k + 1) * NS], gct)
        return gbt, gct

    zero = jnp.zeros((NS, LANES), F32)
    gbt, gct = lax.fori_loop(0, CHUNK * NS // STEP, collect, (zero, zero))
    gb_ref[...] = gbt
    gc_ref[...] = gct


def state_weights(b_t, c_t):
    parts = []
    for values in (b_t.T, c_t.T):
        high = lax.reduce_precision(values, 8, 7)
        parts += [high, values - high]
    return jnp.pad(jnp.concatenate(parts, 1), ((0, 0), (0, LANES - 4 * NS)))


def scan_fwd(info, dt, x, b_t, c_t, a_t, n_blocks):
    rows, width = dt.shape
    pieces = rows // n_blocks // CHUNK

    def at(i, j, info):
        return (i ^ info[0]) * pieces + j

    wide = pl.BlockSpec((CHUNK // 8, 8, width), lambda i, j, info: (at(i, j, info), 0, 0))
    tall = pl.BlockSpec((NS, CHUNK), lambda i, j, info: (0, at(i, j, info)))
    whole = pl.BlockSpec((NS, width), lambda i, j, info: (0, 0))
    dt, x = (v.reshape(-1, 8, width) for v in (dt, x))
    y, firsts = pl.pallas_call(
        scan_fwd_body,
        grid_spec=pltpu.PrefetchScalarGridSpec(
            num_scalar_prefetch=1,
            grid=(n_blocks, pieces),
            in_specs=[wide, wide, tall, tall, whole],
            out_specs=[
                wide,
                pl.BlockSpec((1, NS, width), lambda i, j, info: (i * pieces + j, 0, 0)),
            ],
            scratch_shapes=[pltpu.VMEM((NS, width), F32)],
        ),
        out_shape=[
            jax.ShapeDtypeStruct((rows // 8, 8, width), F32),
            jax.ShapeDtypeStruct((n_blocks * pieces, NS, width), F32),
        ],
        compiler_params=pltpu.CompilerParams(vmem_limit_bytes=32 * 2**20),
        cost_estimate=busy(36),
        name="scan_fwd",
    )(info, dt, x, b_t, c_t, a_t)
    return y.reshape(rows, width), firsts


def scan_bwd(info, dt, x, bc, gy, a_t, firsts, n_blocks):
    rows, width = dt.shape
    pieces = rows // n_blocks // CHUNK

    def at(i, j):
        return (n_blocks - 1 - i) * pieces + pieces - 1 - j

    wide = pl.BlockSpec((CHUNK // 8, 8, width), lambda i, j, info: (at(i, j), 0, 0))
    tall = pl.BlockSpec((CHUNK // 8, 8, LANES), lambda i, j, info: (at(i, j), 0, 0))
    turned = pl.BlockSpec((NS, CHUNK), lambda i, j, info: (0, at(i, j)))
    whole = pl.BlockSpec((NS, width), lambda i, j, info: (0, 0))
    first = pl.BlockSpec((1, NS, width), lambda i, j, info: (at(i, j), 0, 0))
    gdt, gx, gb, gc, ga = pl.pallas_call(
        scan_bwd_body,
        grid_spec=pltpu.PrefetchScalarGridSpec(
            num_scalar_prefetch=1,
            grid=(n_blocks, pieces),
            in_specs=[wide, wide, tall, wide, whole, first],
            out_specs=[wide, wide, turned, turned, whole],
            scratch_shapes=[
                pltpu.VMEM((NS, width), F32),
                pltpu.VMEM((CHUNK + 1, NS, width), F32),
                pltpu.VMEM((CHUNK, NS, width), F32),
                pltpu.VMEM((CHUNK * NS, LANES), jnp.bfloat16),
                pltpu.VMEM((CHUNK * NS, 2 * LANES), F32),
                pltpu.VMEM((CHUNK * NS, LANES), jnp.bfloat16),
            ],
        ),
        out_shape=[
            jax.ShapeDtypeStruct((rows // 8, 8, width), F32),
            jax.ShapeDtypeStruct((rows // 8, 8, width), F32),
            jax.ShapeDtypeStruct((NS, rows), F32),
            jax.ShapeDtypeStruct((NS, rows), F32),
            jax.ShapeDtypeStruct((NS, width), F32),
        ],
        compiler_params=pltpu.CompilerParams(vmem_limit_bytes=40 * 2**20),
        cost_estimate=busy(90),
        name="scan_bwd",
    )(
        info, dt.reshape(-1, 8, width), x.reshape(-1, 8, width), bc.reshape(-1, 8, LANES),
        gy.reshape(-1, 8, width), a_t, firsts,
    )
    return gdt.reshape(rows, width), gx.reshape(rows, width), gb, gc, ga


def conv_fwd_body(info, x_ref, taps_ref, bias_ref, out_ref, padded, *, taps):
    block = pl.program_id(0)
    rows = x_ref.shape[0]
    keep = info[1 + block].astype(F32)

    @pl.when(block == 0)
    def _():
        padded[...] = jnp.zeros_like(padded)

    padded[0:8, :] = padded[rows : rows + 8, :] * keep
    padded[8 : rows + 8, :] = x_ref[...].astype(F32)
    total = bias_ref[...] + taps_ref[0:1, :] * padded[8 - taps + 1 : 8 - taps + 1 + rows, :]
    for i in range(1, taps):
        total += taps_ref[i : i + 1, :] * padded[8 - taps + 1 + i : 8 - taps + 1 + i + rows, :]
    out_ref[...] = total


def conv_bwd_body(info, g_ref, x_ref, taps_ref, gx_ref, gw_ref, gb_ref, padded, *, taps):
    turn = pl.program_id(0)
    n_blocks = pl.num_programs(0)
    rows = x_ref.shape[0]
    after = jnp.minimum(n_blocks - turn, n_blocks - 1)
    keep = info[1 + after].astype(F32)

    @pl.when(turn == 0)
    def _():
        padded[...] = jnp.zeros_like(padded)
        gw_ref[...] = jnp.zeros_like(gw_ref)
        gb_ref[...] = jnp.zeros_like(gb_ref)

    padded[rows : rows + 8, :] = padded[0:8, :] * keep
    padded[0:rows, :] = g_ref[...]
    x = x_ref[...].astype(F32)
    total = None
    for i in range(taps):
        moved = padded[taps - 1 - i : taps - 1 - i + rows, :]
        part = taps_ref[i : i + 1, :] * moved
        total = part if total is None else total + part
        gw_ref[i : i + 1, :] += jnp.sum(x * moved, 0, keepdims=True)
    gx_ref[...] = total.astype(gx_ref.dtype)
    gb_ref[...] += jnp.sum(padded[0:rows, :], 0, keepdims=True)


def conv_fwd(info, x, taps_t, bias, n_blocks):
    rows, width = x.shape
    block = rows // n_blocks
    wide = pl.BlockSpec((block, width), lambda i, info: (i ^ info[0], 0))
    return pl.pallas_call(
        functools.partial(conv_fwd_body, taps=taps_t.shape[0]),
        grid_spec=pltpu.PrefetchScalarGridSpec(
            num_scalar_prefetch=1,
            grid=(n_blocks,),
            in_specs=[
                wide,
                pl.BlockSpec(taps_t.shape, lambda i, info: (0, 0)),
                pl.BlockSpec((1, width), lambda i, info: (0, 0)),
            ],
            out_specs=wide,
            scratch_shapes=[pltpu.VMEM((block + 8, width), F32)],
        ),
        out_shape=jax.ShapeDtypeStruct((rows, width), F32),
        compiler_params=pltpu.CompilerParams(vmem_limit_bytes=32 * 2**20),
        cost_estimate=busy(5),
        name="conv_fwd",
    )(info, x, taps_t, bias)


def conv_bwd(info, grad, x, taps_t, n_blocks):
    rows, width = x.shape
    block = rows // n_blocks
    wide = pl.BlockSpec((block, width), lambda i, info: ((n_blocks - 1 - i) ^ info[0], 0))
    taps_at = pl.BlockSpec(taps_t.shape, lambda i, info: (0, 0))
    one = pl.BlockSpec((1, width), lambda i, info: (0, 0))
    return pl.pallas_call(
        functools.partial(conv_bwd_body, taps=taps_t.shape[0]),
        grid_spec=pltpu.PrefetchScalarGridSpec(
            num_scalar_prefetch=1,
            grid=(n_blocks,),
            in_specs=[wide, wide, taps_at],
            out_specs=[wide, taps_at, one],
            scratch_shapes=[pltpu.VMEM((block + 8, width), F32)],
        ),
        out_shape=[
            jax.ShapeDtypeStruct((rows, width), jnp.bfloat16),
            jax.ShapeDtypeStruct(taps_t.shape, F32),
            jax.ShapeDtypeStruct((1, width), F32),
        ],
        compiler_params=pltpu.CompilerParams(vmem_limit_bytes=32 * 2**20),
        cost_estimate=busy(9),
        name="conv_bwd",
    )(info, grad, x, taps_t)


def busy(us):
    return pl.CostEstimate(flops=int(us * 1.1e9), bytes_accessed=0, transcendentals=0)


def on_seq(index):
    return {"seq": index}


def masks_of(n):
    return [1 << bit for bit in range(n.bit_length() - 1)]


def greet_seq(n):
    here = lax.axis_index("seq")
    barrier = pltpu.get_barrier_semaphore()
    masks = masks_of(n)
    for mask in masks:
        pl.semaphore_signal(barrier, inc=1, device_id=on_seq(here ^ mask), device_id_type=MESH)
    return len(masks)


def send_to(source, target, sems, at, mask):
    send, recv = sems
    here = lax.axis_index("seq")
    return pltpu.make_async_remote_copy(
        src_ref=source,
        dst_ref=target,
        send_sem=send.at[at],
        recv_sem=recv.at[at],
        device_id=on_seq(here ^ mask),
        device_id_type=MESH,
    )


def crossed(rows, n):
    return n == 8 and rows >= 64


def gather_start(src, out, sems, n):
    here = lax.axis_index("seq")
    if not crossed(src.shape[0], n):
        copies = []

        def bit_step(bit):
            def run():
                if bit:
                    copies[-1].wait_recv()
                size = 1 << bit
                span = pl.ds((here >> bit) << bit, size)
                copy = send_to(out.at[span], out.at[span], sems, bit, size)
                copy.start()
                copies.append(copy)

            return run

        def last():
            copies[-1].wait_recv()
            for copy in copies:
                copy.wait_send()

        return [bit_step(bit) for bit in range(n.bit_length() - 1)] + [last]

    half = -(-src.shape[0] // 32) * 16
    low, high = pl.ds(0, half), pl.ds(half, src.shape[0] - half)
    own = out.at[here]
    to_2, to_4, to_1 = (
        send_to(src, own, sems, 0, 2),
        send_to(src, own, sems, 1, 4),
        send_to(src, own, sems, 2, 1),
    )
    for copy in (to_2, to_4, to_1):
        copy.start()
    from_2, from_4, from_6 = out.at[here ^ 2], out.at[here ^ 4], out.at[here ^ 6]
    on_4 = send_to(from_2.at[low], from_2.at[low], sems, 3, 4)
    on_2 = send_to(from_4.at[high], from_4.at[high], sems, 4, 2)
    core_2, core_4, core_6 = (
        send_to(block, block, sems, 5 + i, 1) for i, block in enumerate((from_2, from_4, from_6))
    )

    def second():
        to_2.wait_recv()
        on_4.start()
        core_2.start()
        to_4.wait_recv()
        on_2.start()
        core_4.start()

    def third():
        on_4.wait_recv()
        on_2.wait_recv()
        core_6.start()

    def last():
        for copy in (to_1, core_2, core_4, core_6):
            copy.wait_recv()
        for copy in (to_2, to_4, to_1, on_4, on_2, core_2, core_4, core_6):
            copy.wait_send()

    return [second, third, last]


def gather_body(src, out, local, send, recv, *, n):
    here = lax.axis_index("seq")
    own = pltpu.make_async_copy(src, out.at[here], local)
    own.start()
    count = greet_seq(n)
    pl.semaphore_wait(pltpu.get_barrier_semaphore(), count)
    cross = crossed(src.shape[0], n)
    if not cross:
        own.wait()
    for step in gather_start(src, out, (send, recv), n):
        step()
    if cross:
        own.wait()


def seq_gather(block, call):
    n = lax.axis_size("seq")
    return pl.pallas_call(
        functools.partial(gather_body, n=n),
        out_shape=jax.ShapeDtypeStruct((n,) + block.shape, block.dtype),
        in_specs=[pl.BlockSpec(memory_space=pl.ANY)],
        out_specs=pl.BlockSpec(memory_space=pl.ANY),
        scratch_shapes=[
            pltpu.SemaphoreType.DMA(()),
            pltpu.SemaphoreType.DMA((8,)),
            pltpu.SemaphoreType.DMA((8,)),
        ],
        compiler_params=pltpu.CompilerParams(collective_id=call, has_side_effects=True),
        cost_estimate=busy(35),
        name="seq_gather",
    )(block)


def add_rows(out, one, two, start, size, step=16):
    def turn(i, _):
        rows = pl.ds(pl.multiple_of(start + i * step, step), step)
        out[rows, :] = (one[rows, :].astype(F32) + two[rows, :].astype(F32)).astype(out.dtype)
        return 0

    lax.fori_loop(0, size // step, turn, 0)


def reduce_steps(blocks, out, came, sums, ends, sems, n, at=0):
    here = lax.axis_index("seq")
    tokens = blocks.shape[1]
    if n != 8:
        held = blocks
        for k, bit in enumerate(reversed(range(n.bit_length() - 1))):
            size = 1 << bit
            first = (here >> bit) & 1
            other = pl.ds((1 - first) * size, size)
            copy = send_to(held.at[other], came.at[pl.ds(size, size)], sems, at + k, size)
            copy.start()
            copy.wait()
            for j in range(size):
                add_rows(
                    sums.at[size + j], held.at[first * size + j], came.at[size + j], 0, tokens
                )
            held = sums.at[pl.ds(size, size)]
        total = sums.at[1]

        def turn(i, _):
            rows = pl.ds(pl.multiple_of(i * 16, 16), 16)
            out[rows, :] = total[rows, :].astype(out.dtype)
            return 0

        lax.fori_loop(0, tokens // 16, turn, 0)
        return
    half = tokens // 2
    low, high = pl.ds(0, half), pl.ds(half, half)
    step = 16 if half % 16 == 0 else 8
    core = [
        send_to(blocks.at[here ^ (mask | 1)], came.at[i], sems, at + i, 1)
        for i, mask in enumerate((6, 2, 4, 0))
    ]
    for copy in core:
        copy.start()
    by_6, by_2, by_4 = (sums.at[i] for i in range(3))
    end_2, end_4, mid_2, mid_4 = ends.at[0], ends.at[1], ends.at[2], ends.at[3]
    dia_2 = send_to(by_6.at[low], mid_4.at[low], sems, at + 4, 2)
    dia_4 = send_to(by_6.at[high], mid_2.at[high], sems, at + 5, 4)
    x_low = send_to(by_2.at[low], end_2.at[low], sems, at + 6, 2)
    y_high = send_to(by_4.at[high], end_4.at[high], sems, at + 7, 4)
    x_high = send_to(by_2.at[high], end_2.at[high], sems, at + 8, 2)
    y_low = send_to(by_4.at[low], end_4.at[low], sems, at + 9, 4)
    core[0].wait_recv()
    add_rows(by_6, blocks.at[here ^ 6], came.at[0], 0, tokens, step)
    dia_2.start()
    dia_4.start()
    core[1].wait_recv()
    add_rows(by_2, blocks.at[here ^ 2], came.at[1], 0, tokens, step)
    x_low.start()
    core[2].wait_recv()
    add_rows(by_4, blocks.at[here ^ 4], came.at[2], 0, tokens, step)
    y_high.start()
    dia_4.wait_recv()
    add_rows(by_2, by_2, mid_2, half, half, step)
    x_high.start()
    dia_2.wait_recv()
    add_rows(by_4, by_4, mid_4, 0, half, step)
    y_low.start()
    core[3].wait_recv()
    add_rows(out, blocks.at[here], came.at[3], 0, tokens, step)
    x_low.wait_recv()
    x_high.wait_recv()
    add_rows(out, out, end_2, 0, tokens, step)
    y_high.wait_recv()
    y_low.wait_recv()
    add_rows(out, out, end_4, 0, tokens, step)
    for copy in core + [dia_2, dia_4, x_low, y_high, x_high, y_low]:
        copy.wait_send()


def reduce_body(blocks, out, came, sums, ends, send, recv, *, n):
    count = greet_seq(n)
    pl.semaphore_wait(pltpu.get_barrier_semaphore(), count)
    reduce_steps(blocks, out, came, sums, ends, (send, recv), n)


def reduce_scratch(n, rows, width, dtype):
    if n != 8:
        return [pltpu.VMEM((n, rows, width), dtype)] * 2 + [pltpu.VMEM((1, 8, 128), dtype)]
    return [
        pltpu.VMEM((4, rows, width), dtype),
        pltpu.VMEM((3, rows, width), dtype),
        pltpu.VMEM((4, rows, width), dtype),
    ]


def seq_reduce(blocks, call):
    n, rows, width = blocks.shape
    return pl.pallas_call(
        functools.partial(reduce_body, n=n),
        out_shape=jax.ShapeDtypeStruct((rows, width), F32),
        in_specs=[pl.BlockSpec(memory_space=pltpu.VMEM)],
        out_specs=pl.BlockSpec(memory_space=pltpu.VMEM),
        scratch_shapes=reduce_scratch(n, rows, width, blocks.dtype)
        + [pltpu.SemaphoreType.DMA((10,)), pltpu.SemaphoreType.DMA((10,))],
        compiler_params=pltpu.CompilerParams(
            collective_id=call, has_side_effects=True, vmem_limit_bytes=56 * 2**20
        ),
        cost_estimate=busy(blocks.size / 8e4),
        name="seq_reduce",
    )(blocks)


def total_body(blocks, out, total, came, sums, ends, send, recv, local, *, n):
    here = lax.axis_index("seq")
    count = greet_seq(n)
    pl.semaphore_wait(pltpu.get_barrier_semaphore(), count)
    reduce_steps(blocks, total, came, sums, ends, (send, recv), n)
    own = pltpu.make_async_copy(total, out.at[here], local)
    own.start()
    cross = crossed(total.shape[0], n)
    if not cross:
        own.wait()
    for step in gather_start(total, out, (send.at[pl.ds(10, 8)], recv.at[pl.ds(10, 8)]), n):
        step()
    if cross:
        own.wait()


def seq_total(blocks, call):
    n, rows, width = blocks.shape
    return pl.pallas_call(
        functools.partial(total_body, n=n),
        out_shape=jax.ShapeDtypeStruct(blocks.shape, F32),
        in_specs=[pl.BlockSpec(memory_space=pltpu.VMEM)],
        out_specs=pl.BlockSpec(memory_space=pltpu.VMEM),
        scratch_shapes=[pltpu.VMEM((rows, width), F32)]
        + reduce_scratch(n, rows, width, F32)
        + [
            pltpu.SemaphoreType.DMA((18,)),
            pltpu.SemaphoreType.DMA((18,)),
            pltpu.SemaphoreType.DMA(()),
        ],
        compiler_params=pltpu.CompilerParams(
            collective_id=call, has_side_effects=True, vmem_limit_bytes=40 * 2**20
        ),
        cost_estimate=busy(20),
        name="seq_total",
    )(blocks)


def line_steps(srcs, outs, send, recv, depth):
    here = lax.axis_index("fsdp")

    def passed(a, k, side):
        shard = here - (k - 1) if side == 0 else here + (k - 1)
        shard = jnp.clip(shard, 0, depth - 1)
        target = here + 1 if side == 0 else here - 1
        target = jnp.clip(target, 0, depth - 1)
        block = outs[a].at[shard]
        return pltpu.make_async_remote_copy(
            src_ref=srcs[a] if k == 1 else block,
            dst_ref=block,
            send_sem=send.at[a, side, k - 1],
            recv_sem=recv.at[a, side, k - 1],
            device_id={"fsdp": target},
            device_id_type=MESH,
        )

    def sends(k, side):
        if side == 0:
            return (here >= k - 1) & (here < depth - 1)
        return (here <= depth - k) & (here > 0)

    def gets(k, side):
        return here >= k if side == 0 else here <= depth - 1 - k

    def arrived(k):
        for side in range(2):

            @pl.when(gets(k, side))
            def _():
                for a in range(len(srcs)):
                    passed(a, k, side).wait_recv()

    def step(k):
        def run():
            if k > 1:
                arrived(k - 1)
            for side in range(2):

                @pl.when(sends(k, side))
                def _():
                    for a in range(len(srcs)):
                        passed(a, k, side).start()

        return run

    def last():
        arrived(depth - 1)
        for k in range(1, depth):
            for side in range(2):

                @pl.when(sends(k, side))
                def _():
                    for a in range(len(srcs)):
                        passed(a, k, side).wait_send()

    return [step(k) for k in range(1, depth)] + [last]


def first_body(*refs, n, depth, blocks, lines):
    srcs, refs = refs[: blocks + lines], refs[blocks + lines :]
    outs = refs[: blocks + lines]
    local, send, recv, line_send, line_recv = refs[blocks + lines :]
    here, level = lax.axis_index("seq"), lax.axis_index("fsdp")
    owns = []
    for a in range(blocks + lines):
        place = outs[a].at[here if a < blocks else level]
        owns.append(pltpu.make_async_copy(srcs[a], place, local.at[a]))
        owns[-1].start()
    count = greet_seq(n)
    barrier = pltpu.get_barrier_semaphore()
    for ready, other in ((level > 0, level - 1), (level < depth - 1, level + 1)):

        @pl.when(ready)
        def _():
            pl.semaphore_signal(
                barrier, inc=1, device_id={"fsdp": jnp.clip(other, 0, depth - 1)}, device_id_type=MESH
            )

    count = count + (level > 0).astype(jnp.int32) + (level < depth - 1).astype(jnp.int32)
    pl.semaphore_wait(barrier, count)
    cross = crossed(srcs[0].shape[0], n)
    if not cross:
        for own in owns[:blocks]:
            own.wait()
    line = line_steps(srcs[blocks:], outs[blocks:], line_send, line_recv, depth)
    line.pop(0)()
    turns = []
    for a in range(blocks):
        along = gather_start(srcs[a], outs[a], (send.at[a], recv.at[a]), n)
        turns += [(2 * i + 2 * a, step) for i, step in enumerate(along)]
    turns += [(2 * i + 0.5, step) for i, step in enumerate(line)]
    for _, step in sorted(turns, key=lambda turn: turn[0]):
        step()
    if cross:
        for own in owns[:blocks]:
            own.wait()
    for own in owns[blocks:]:
        own.wait()


def first_gather(blocks, arrays, call):
    n, depth = lax.axis_size("seq"), lax.axis_size("fsdp")
    count, lines = len(blocks), len(arrays)
    anywhere = pl.BlockSpec(memory_space=pl.ANY)
    return pl.pallas_call(
        functools.partial(first_body, n=n, depth=depth, blocks=count, lines=lines),
        out_shape=[jax.ShapeDtypeStruct((n,) + block.shape, block.dtype) for block in blocks]
        + [jax.ShapeDtypeStruct((depth,) + array.shape, array.dtype) for array in arrays],
        in_specs=[anywhere] * (count + lines),
        out_specs=[anywhere] * (count + lines),
        scratch_shapes=[
            pltpu.SemaphoreType.DMA((count + lines,)),
            pltpu.SemaphoreType.DMA((count, 8)),
            pltpu.SemaphoreType.DMA((count, 8)),
            pltpu.SemaphoreType.DMA((lines, 2, depth - 1)),
            pltpu.SemaphoreType.DMA((lines, 2, depth - 1)),
        ],
        compiler_params=pltpu.CompilerParams(collective_id=call, has_side_effects=True),
        cost_estimate=busy(60),
        name="first_gather",
    )(*blocks, *arrays)


def last_body(*refs, n, count):
    srcs, outs = refs[:count], refs[count : 2 * count]
    local, send, recv = refs[2 * count :]
    here = lax.axis_index("seq")
    owns = [pltpu.make_async_copy(srcs[a], outs[a].at[here], local.at[a]) for a in range(count)]
    for own in owns:
        own.start()
    peers = greet_seq(n)
    pl.semaphore_wait(pltpu.get_barrier_semaphore(), peers)
    cross = [crossed(src.shape[0], n) for src in srcs]
    for a in range(count):
        if not cross[a]:
            owns[a].wait()
    steps = [gather_start(srcs[a], outs[a], (send.at[a], recv.at[a]), n) for a in range(count)]
    for i in range(max(len(part) for part in steps)):
        for part in steps:
            if i < len(part):
                part[i]()
    for a in range(count):
        if cross[a]:
            owns[a].wait()


def last_gather(arrays, call):
    n = lax.axis_size("seq")
    count = len(arrays)
    anywhere = pl.BlockSpec(memory_space=pl.ANY)
    return pl.pallas_call(
        functools.partial(last_body, n=n, count=count),
        out_shape=[jax.ShapeDtypeStruct((n,) + array.shape, array.dtype) for array in arrays],
        in_specs=[anywhere] * count,
        out_specs=[anywhere] * count,
        scratch_shapes=[
            pltpu.SemaphoreType.DMA((count,)),
            pltpu.SemaphoreType.DMA((count, 8)),
            pltpu.SemaphoreType.DMA((count, 8)),
        ],
        compiler_params=pltpu.CompilerParams(collective_id=call, has_side_effects=True),
        cost_estimate=busy(60),
        name="last_gather",
    )(*arrays)


def lay_cols_body(*refs, n, depth, groups, chunk, padded, total, front):
    out = refs[-1]
    if front:
        out[:, :front] = refs[0][:, :front].astype(F32)
    parts = refs[len(refs) - 1 - groups : -1]
    for g, part in enumerate(parts):
        for s in range(n):
            values = part[s].astype(F32)
            for j in range(depth):
                at = front + g * total + j * (total // depth) + s * chunk
                out[:, at : at + chunk] = values[:, j * padded : j * padded + chunk]


def lay_cols(parts, chunk, padded, total, first=None, front=0):
    n, rows, _ = parts[0][0].shape
    depth = total // (n * chunk)
    width = depth * padded
    turns = 1 if rows % 40 else 5
    step = rows // turns
    ins = [] if first is None else [first]
    specs = [] if first is None else [pl.BlockSpec((step, first.shape[1]), lambda i: (i, 0))]
    for _, block in parts:
        specs.append(pl.BlockSpec((n, step, width), lambda i, block=block: (0, i, block)))
    return pl.pallas_call(
        functools.partial(
            lay_cols_body, n=n, depth=depth, groups=len(parts), chunk=chunk, padded=padded,
            total=total, front=front,
        ),
        grid=(turns,),
        out_shape=jax.ShapeDtypeStruct((rows, front + len(parts) * total), F32),
        in_specs=specs,
        out_specs=pl.BlockSpec((step, front + len(parts) * total), lambda i: (i, 0)),
        compiler_params=pltpu.CompilerParams(vmem_limit_bytes=48 * 2**20),
        cost_estimate=busy(8),
        name="lay_cols",
    )(*ins, *(array for array, _ in parts))


def lay_rows_body(parts, out, *, n, chunk):
    for s in range(n):
        out[s * chunk : (s + 1) * chunk, :] = parts[s, :chunk, :].astype(F32)


def lay_rows(parts, chunk):
    n, _, width = parts.shape
    return pl.pallas_call(
        functools.partial(lay_rows_body, n=n, chunk=chunk),
        out_shape=jax.ShapeDtypeStruct((n * chunk, width), F32),
        in_specs=[pl.BlockSpec(memory_space=pltpu.VMEM)],
        out_specs=pl.BlockSpec(memory_space=pltpu.VMEM),
        compiler_params=pltpu.CompilerParams(vmem_limit_bytes=48 * 2**20),
        cost_estimate=busy(4),
        name="lay_rows",
    )(parts)


def lay_rows_turned_body(parts, out, *, n, chunk):
    for s in range(n):
        out[:, s * chunk : (s + 1) * chunk] = parts[s].astype(F32).T[:, :chunk]


def lay_rows_turned(parts, chunk):
    n, padded, width = parts.shape
    return pl.pallas_call(
        functools.partial(lay_rows_turned_body, n=n, chunk=chunk),
        grid=(-(-width // LANES),),
        in_specs=[pl.BlockSpec((n, padded, LANES), lambda i: (0, 0, i))],
        out_specs=pl.BlockSpec((LANES, n * chunk), lambda i: (i, 0)),
        out_shape=jax.ShapeDtypeStruct((width, n * chunk), F32),
        compiler_params=pltpu.CompilerParams(vmem_limit_bytes=48 * 2**20),
        cost_estimate=busy(8),
        name="lay_rows_turned",
    )(parts)


def key_scores(k, q, allowed):
    scores = lax.dot_general(k, q, (((0,), (0,)), ((), ())), preferred_element_type=F32)
    return scores if allowed is None else jnp.where(allowed, scores, NEG)


def block_masks(position, back, rows):
    key = lax.broadcasted_iota(jnp.int32, (rows, rows), 0)
    query = lax.broadcasted_iota(jnp.int32, (rows, rows), 1)
    masks = []
    for distance in range(back, 0, -1):
        reached = jnp.broadcast_to(position >= distance, (rows, rows))
        masks.append((key > query) & reached if distance == back else reached)
    return masks + [key <= query]


def attend_body(info, q_ref, *refs, back):
    keys, values = refs[: back + 2], refs[back + 2 : 2 * back + 4]
    out_ref, norm_ref = refs[2 * back + 4 :]
    q = q_ref[...]
    masks = [None] + block_masks(info[1], back, q.shape[1])
    scores = [key_scores(k[...], q, mask) for k, mask in zip(keys, masks)]
    top = functools.reduce(jnp.maximum, (jnp.max(part, 0, keepdims=True) for part in scores))
    total = jnp.zeros_like(top)
    out = jnp.zeros(q.shape, F32)
    for part, v in zip(scores, values):
        weights = jnp.exp(part - top)
        total += jnp.sum(weights, 0, keepdims=True)
        out += jnp.dot(v[...], weights.astype(jnp.bfloat16), preferred_element_type=F32)
    out_ref[...] = out / total
    norm_ref[0] = jnp.broadcast_to(top + jnp.log(total), norm_ref.shape[1:])


def attend_back_body(info, q_ref, grad_ref, out_ref, norm_ref, *refs, back):
    count = back + 2
    keys, values = refs[:count], refs[count : 2 * count]
    gq_ref, gk_meta, gv_meta, gk_ref, gv_ref = refs[2 * count :]
    turn = pl.program_id(1)
    q, grad = q_ref[...], grad_ref[...]
    norm = norm_ref[0][0:1]
    shared = jnp.sum(grad.astype(F32) * out_ref[...], 0, keepdims=True)
    masks = [None] + block_masks(info[1], back, q.shape[1])

    @pl.when(turn == 0)
    def _():
        for ref in (gk_meta, gv_meta, gk_ref, gv_ref):
            ref[...] = jnp.zeros_like(ref)

    contract = (((1,), (1,)), ((), ()))
    gq = jnp.zeros(q.shape, F32)
    for i in range(count):
        k, v = keys[i][...], values[i][...]
        weights = jnp.exp(key_scores(k, q, masks[i]) - norm)
        grad_weights = lax.dot_general(
            v, grad, (((0,), (0,)), ((), ())), preferred_element_type=F32
        )
        grad_scores = (weights * (grad_weights - shared)).astype(jnp.bfloat16)
        gq += jnp.dot(k, grad_scores, preferred_element_type=F32)
        gk = lax.dot_general(q, grad_scores, contract, preferred_element_type=F32)
        gv = lax.dot_general(
            grad, weights.astype(jnp.bfloat16), contract, preferred_element_type=F32
        )
        if i == 0:
            gk_meta[...] += gk
            gv_meta[...] += gv
        else:
            gk_ref[i - 1] += gk
            gv_ref[i - 1] += gv
    gq_ref[...] = gq * HD ** (-0.5)


def attend_specs(heads, groups, tokens, meta, n, back):
    size = heads // groups
    head = pl.BlockSpec((HD, tokens), lambda g, j, info: (g * size + j, 0))

    def sides(first):
        specs = [pl.BlockSpec((HD, meta), lambda g, j, info: (first + g, 0))]
        for distance in range(back, -1, -1):
            specs.append(
                pl.BlockSpec(
                    (HD, tokens),
                    lambda g, j, info, distance=distance: (
                        first + g, lax.rem(info[0] - distance + n, n),
                    ),
                )
            )
        return specs

    norm = pl.BlockSpec((1, 8, tokens), lambda g, j, info: (g * size + j, 0, 0))
    return head, sides(0) + sides(groups), norm


def attend(info, q_t, kv_t, meta_t, heads, groups, n, back):
    tokens, meta = q_t.shape[1], meta_t.shape[1]
    head, kv, norm = attend_specs(heads, groups, tokens, meta, n, back)
    return pl.pallas_call(
        functools.partial(attend_body, back=back),
        grid_spec=pltpu.PrefetchScalarGridSpec(
            num_scalar_prefetch=1,
            grid=(groups, heads // groups),
            in_specs=[head] + kv,
            out_specs=[head, norm],
        ),
        out_shape=[
            jax.ShapeDtypeStruct(q_t.shape, F32),
            jax.ShapeDtypeStruct((heads, 8, tokens), F32),
        ],
        compiler_params=pltpu.CompilerParams(vmem_limit_bytes=40 * 2**20),
        cost_estimate=busy(25),
        name="attend",
    )(info, q_t, *(([meta_t] + [kv_t] * (back + 1)) * 2))


def attend_back(info, q_t, grad_t, out_t, norms, kv_t, meta_t, heads, groups, n, back):
    tokens, meta = q_t.shape[1], meta_t.shape[1]
    head, kv, norm = attend_specs(heads, groups, tokens, meta, n, back)
    cols = groups * HD
    window = pl.BlockSpec((back + 1, HD, tokens), lambda g, j, info: (0, g, 0))
    side = pl.BlockSpec((HD, meta), lambda g, j, info: (g, 0))
    return pl.pallas_call(
        functools.partial(attend_back_body, back=back),
        grid_spec=pltpu.PrefetchScalarGridSpec(
            num_scalar_prefetch=1,
            grid=(groups, heads // groups),
            in_specs=[head, head, head, norm] + kv,
            out_specs=[head, side, side, window, window],
        ),
        out_shape=[
            jax.ShapeDtypeStruct(q_t.shape, F32),
            jax.ShapeDtypeStruct((cols, meta), F32),
            jax.ShapeDtypeStruct((cols, meta), F32),
            jax.ShapeDtypeStruct((back + 1, cols, tokens), F32),
            jax.ShapeDtypeStruct((back + 1, cols, tokens), F32),
        ],
        compiler_params=pltpu.CompilerParams(vmem_limit_bytes=48 * 2**20),
        cost_estimate=busy(50),
        name="attend_back",
    )(info, q_t, grad_t, out_t, norms, *(([meta_t] + [kv_t] * (back + 1)) * 2))


def turned_sum(blocks):
    n = lax.axis_size("fsdp")
    here = lax.axis_index("fsdp")
    total = lax.dynamic_index_in_dim(blocks, here, 0, False).astype(F32)
    for k in range(1, n):
        part = lax.dynamic_index_in_dim(blocks, (here + k) % n, 0, False)
        total = total + lax.ppermute(part, "fsdp", [(i, (i + k) % n) for i in range(n)]).astype(F32)
    return total


def in_rows(values):
    return with_layout_constraint(values, Layout(major_to_minor=(0, 1)))


def pad_to(values, size, axis):
    widths = [(0, 0)] * values.ndim
    widths[axis] = (0, size - values.shape[axis])
    return jnp.pad(values, widths)


def norm_fwd(values, gains):
    inverse = lax.rsqrt(jnp.mean(values * values, -1, keepdims=True) + EPS)
    return (values * inverse * gains, inverse)


def norm_back(values, inverse, gains, grads):
    weighted = grads * gains
    mean_term = jnp.mean(values * weighted, -1, keepdims=True)
    return (
        inverse * weighted - values * inverse**3 * mean_term,
        jnp.sum(grads * values * inverse, 0),
    )


def silu_slope(values):
    sigmoid = jax.nn.sigmoid(values)
    return sigmoid * (1.0 + values * (1.0 - sigmoid))


def product(one, two, dims, exact=False, out=F32):
    return lax.dot_general(
        one,
        two,
        ((dims[:1], dims[1:]), ((), ())),
        preferred_element_type=F32,
        precision=lax.Precision.HIGH if exact else None,
    ).astype(out)


def shards(
    inputs, starts, norm_gain, in_weight, conv_weight, conv_bias, xproj_weight, dtproj_weight, dt_bias,
    log_decay, skip_gain, meta_tokens, attn_weight, mamba_weight, attn_gain, mamba_gain, ffn_gain,
    gate_weight, up_weight, down_weight, cotangent,
):
    low = jnp.bfloat16
    n, depth = lax.axis_size("seq"), lax.axis_size("fsdp")
    here = lax.axis_index("seq")
    tokens, width = inputs.shape[1:]
    rows = n * tokens
    q_cols, kv_cols = HQ * HD, HK * HD
    qkv_cols = q_cols + 2 * kv_cols
    group_size = HQ // HK
    inner = EI // n
    hidden_units = gate_weight.shape[1]
    units = hidden_units // n
    shard_rows = width // depth

    if n <= GAP:
        carries = jnp.array([0] + [1] * (n - 1), jnp.int32)
        position = here
    else:
        flags = lax.all_gather(starts[0, 0], "seq")
        carries = 1 - flags
        blocks = jnp.arange(n)
        position = here - jnp.max(jnp.where((flags == 1) & (blocks <= here), blocks, 0))
    info = jnp.concatenate([jnp.zeros((1,), jnp.int32), carries])

    def up_to(size, step):
        return -(-size // step) * step

    chunk, unit_chunk = inner // depth, units // depth
    inner_pad = up_to(depth * up_to(chunk, 16), LANES)
    units_pad = up_to(depth * up_to(unit_chunk, 16), LANES)
    chunk_pad, unit_pad = inner_pad // depth, units_pad // depth

    def own_cols(weight, base, total, padded, here=here):
        size = total // (depth * n)
        parts = [
            pad_to(
                lax.dynamic_slice_in_dim(weight, base + j * (total // depth) + here * size, size, 1),
                padded,
                1,
            )
            for j in range(depth)
        ]
        return jnp.concatenate(parts, 1)

    def own_rows(weight, padded, here=here):
        size = weight.shape[0] // n
        return pad_to(lax.dynamic_slice_in_dim(weight, here * size, size, 0), padded, 0)

    def along_depth(values):
        return lax.all_gather(values, "fsdp")

    small = jnp.concatenate(
        [
            conv_weight.T, conv_bias[None], xproj_weight.T, dtproj_weight.T, dt_bias[None], log_decay.T,
            skip_gain[None],
        ],
        0,
    )
    small_rows = up_to(small.shape[0], 16)
    small = pad_to(lax.dynamic_slice_in_dim(small, here * chunk, chunk, 1), chunk_pad, 1)
    own_in = own_cols(in_weight, qkv_cols, EI, chunk_pad)
    own_z = own_cols(in_weight, qkv_cols + EI, EI, chunk_pad)
    gains = pad_to(jnp.stack([norm_gain, attn_gain, mamba_gain, ffn_gain], 0), 16, 0)
    hidden_all, grad_out_all, w_in, small_full, gain_rows, meta_rows = first_gather(
        [inputs[0], cotangent[0]],
        [jnp.concatenate([own_in, own_z], 1), pad_to(small, small_rows, 0), gains, meta_tokens],
        1,
    )
    w_in = w_in.reshape(width, 2 * inner_pad)
    gain_norm, gain_attn, gain_mamba, gain_ffn = (
        gain_rows[:, i].reshape(-1).astype(F32) for i in range(4)
    )
    meta_rows = meta_rows.reshape(META, width)

    small_full, later = lax.optimization_barrier((small_full, here))
    small_full = small_full.transpose(1, 0, 2).reshape(small_rows, inner_pad).astype(F32)
    ends = np.cumsum([0, KC, 1, RDT + 2 * NS, RDT, 1, NS, 1])
    taps_t, bias, select_t, steps_t, b_steps, a_logs, skip = (
        small_full[a:b] for a, b in zip(ends[:-1], ends[1:])
    )
    a_t = -jnp.exp(a_logs)

    piece = up_to(-(-shard_rows // n), 8)

    def attn_piece(weight, cols):
        first = jnp.minimum(later * piece, shard_rows - piece)
        part = lax.dynamic_slice(weight, (first, 0), (piece, cols))
        return lax.dynamic_slice_in_dim(pad_to(part, 2 * piece, 0), later * piece - first, piece, 0)

    own_attn = along_depth(
        jnp.concatenate([attn_piece(in_weight, qkv_cols), attn_piece(attn_weight, width)], 1)
    )
    w_mamba = along_depth(own_rows(mamba_weight, chunk_pad, later)).reshape(inner_pad, width)

    hidden = inputs[0].astype(F32)
    normed_all, _ = norm_fwd(hidden_all.astype(F32), gain_norm)
    normed_all = normed_all.astype(low).reshape(rows, width)
    normed, inv_in = norm_fwd(hidden, gain_norm)
    normed = normed.astype(low)
    mixer_in = product(normed_all, w_in[:, :inner_pad], (1, 0), out=low)
    z_gate = product(normed_all, w_in[:, inner_pad:], (1, 0), out=low).astype(F32)
    conv_pre = conv_fwd(info, mixer_in, taps_t, bias, n)
    mixed = jax.nn.silu(conv_pre)

    def all_sum(values, call):
        laid = values.reshape(values.shape[0], n, tokens).transpose(1, 0, 2)
        laid = pad_to(laid, up_to(values.shape[0], 16), 1)
        total = seq_total(laid, call)
        return total.transpose(1, 0, 2).reshape(-1, rows)[: values.shape[0]]

    part = product(select_t, mixed, (1, 1), exact=True)
    selected = all_sum(part, 2)
    selected, own_attn = lax.optimization_barrier((selected, own_attn))
    all_attn = lax.all_gather(own_attn, "seq").transpose(1, 0, 2, 3)
    all_attn = all_attn.reshape(depth, n * piece, -1)[:, :shard_rows].reshape(width, -1)
    w_qkv, w_attn = all_attn[:, :qkv_cols], all_attn[:, qkv_cols:]
    w_q, w_kv = w_qkv[:, :q_cols], w_qkv[:, q_cols:]
    ranks, b_sel, c_sel = selected[:RDT], selected[RDT : RDT + NS], selected[RDT + NS :]
    dt_pre = product(ranks, steps_t, (0, 0), exact=True) + b_steps
    steps = jax.nn.softplus(dt_pre)
    steps, last = lax.optimization_barrier((steps, later))
    y_scan, firsts = scan_fwd(info, steps, mixed, b_sel, c_sel, a_t, n)
    w_units = along_depth(
        jnp.concatenate(
            [
                own_cols(gate_weight, 0, hidden_units, unit_pad, last),
                own_cols(up_weight, 0, hidden_units, unit_pad, last),
            ],
            1,
        )
    ).reshape(width, 2 * units_pad)
    w_down = along_depth(own_rows(down_weight, unit_pad, last)).reshape(units_pad, width)
    grad_out_all = grad_out_all.reshape(rows, width)
    y_full = y_scan + skip * mixed
    silu_z = jax.nn.silu(z_gate)
    mamba_low = (y_full * silu_z).astype(low)
    mamba_out = seq_reduce(
        in_rows(product(mamba_low, w_mamba, (1, 0), out=low)).reshape(n, tokens, width), 3
    )

    blocks_back = WIN // tokens
    attend_at = jnp.stack([here, position]).astype(jnp.int32)
    heads = (HQ, HK, n, blocks_back)
    queries = product(w_q, normed, (0, 1), out=low) * HD ** (-0.5)
    keyvals = product(w_kv, normed_all, (0, 1), out=low)
    meta_float = meta_rows.astype(F32)
    meta_normed, meta_inv = norm_fwd(meta_float, gain_norm)
    meta_low = meta_normed.astype(low)
    meta_kv = product(w_kv, meta_low, (0, 1), out=low)
    contexts, log_norms = attend(attend_at, queries, keyvals, meta_kv, *heads)
    attended = contexts.astype(low)
    attn_out = product(attended, w_attn, (0, 0))

    attn_normed, attn_inv = norm_fwd(attn_out, gain_attn)
    mamba_normed, mamba_inv = norm_fwd(mamba_out, gain_mamba)
    middle = hidden + 0.5 * (attn_normed + mamba_normed)
    ffn_normed, ffn_inv = norm_fwd(middle, gain_ffn)
    ffn_all = seq_gather(ffn_normed.astype(low), 4).reshape(rows, width)
    both_pre = product(ffn_all, w_units, (1, 0))
    gate_pre, up_pre = both_pre[:, :units_pad], both_pre[:, units_pad:]
    grad_act = product(grad_out_all, w_down, (1, 1))
    silu_gate = jax.nn.silu(gate_pre)
    activated = (silu_gate * up_pre).astype(low)
    grad_units = jnp.concatenate(
        [
            (grad_act * up_pre * silu_slope(gate_pre)).astype(low),
            (grad_act * silu_gate).astype(low),
        ],
        1,
    )
    grad_ffn_part = in_rows(product(grad_units, w_units, (1, 1), out=low))
    down_part = product(activated, w_down, (1, 0), out=low)
    grad_w_units = product(ffn_all, grad_units, (0, 0), out=low)
    grad_w_down = product(activated, grad_out_all, (0, 0), out=low)
    grad_ffn_part, grad_w_units, grad_w_down, down_part = lax.optimization_barrier(
        (grad_ffn_part, grad_w_units, grad_w_down, down_part)
    )
    grad_ffn_in = seq_reduce(grad_ffn_part.reshape(n, tokens, width), 5)

    def depth_sum(part):
        return lax.psum_scatter(part, "fsdp", scatter_dimension=0, tiled=True)

    own_w_units, own_w_down = depth_sum(grad_w_units), depth_sum(grad_w_down)
    down_sum = lax.psum_scatter(down_part, "seq", scatter_dimension=0, tiled=True)

    grad_out = cotangent[0].astype(F32)
    grad_mid_norm, grad_g_ffn = norm_back(middle, ffn_inv, gain_ffn, grad_ffn_in)
    grad_middle = grad_out + grad_mid_norm
    grad_attn_out, grad_g_attn = norm_back(attn_out, attn_inv, gain_attn, 0.5 * grad_middle)
    grad_mamba_out, grad_g_mamba = norm_back(mamba_out, mamba_inv, gain_mamba, 0.5 * grad_middle)
    grad_attn_low = grad_attn_out.astype(low)

    grad_context = product(w_attn, grad_attn_low, (1, 1), out=low)
    grad_queries, grad_k_meta, grad_v_meta, grad_keys, grad_values = attend_back(
        attend_at, queries, grad_context, contexts, log_norms, keyvals, meta_kv, *heads
    )
    grad_queries, own_w_units, own_w_down = lax.optimization_barrier(
        (grad_queries, own_w_units, own_w_down)
    )
    grad_meta_kv = jnp.concatenate([grad_k_meta, grad_v_meta], 0)
    grad_kv_blocks = lax.dynamic_update_slice_in_dim(
        jnp.zeros((blocks_back + n, 2 * kv_cols, tokens), low),
        jnp.concatenate([grad_keys, grad_values], 1).astype(low),
        here,
        0,
    )[blocks_back:]
    grad_keyvals = seq_reduce(grad_kv_blocks, 7)
    grad_qkv = jnp.concatenate([grad_queries, grad_keyvals], 0).astype(low)
    grad_meta_low = product(grad_meta_kv, w_kv.astype(F32), (0, 1), exact=True)
    grad_meta, grad_g_meta = norm_back(meta_float, meta_inv, gain_norm, grad_meta_low)

    meta_high = grad_meta_kv.astype(low)
    meta_rest = (grad_meta_kv - lax.reduce_precision(grad_meta_kv, 8, 7)).astype(low)
    qkv_pad, attn_pad = up_to(qkv_cols, LANES), up_to(width, LANES)
    meta_side = ((q_cols, qkv_pad - qkv_cols), (0, 0))
    grad_w_qkv = product(
        jnp.concatenate([normed, meta_low, meta_low], 0),
        jnp.concatenate(
            [pad_to(grad_qkv, qkv_pad, 0), jnp.pad(meta_high, meta_side), jnp.pad(meta_rest, meta_side)],
            1,
        ),
        (0, 1),
        out=low,
    )
    grad_w_attn = product(attended, pad_to(grad_attn_low, attn_pad, 1), (1, 0), out=low)
    grad_attn = jnp.concatenate([grad_w_qkv, grad_w_attn], 1).reshape(depth, shard_rows, -1)
    meta_own = META // depth
    grad_gains = jnp.stack([grad_g_attn, grad_g_mamba, grad_g_ffn], 0).astype(low)
    grad_gains = grad_gains.reshape(3, depth, shard_rows).transpose(1, 0, 2)
    spare = jnp.concatenate(
        [grad_meta.astype(low).reshape(depth, meta_own, width), pad_to(grad_gains, width, 2)], 1
    )
    spare = pad_to(spare, up_to(meta_own + 3, 16), 1)
    piece = up_to(-(-(shard_rows + spare.shape[1]) // n), 8)
    grad_attn = jnp.concatenate([grad_attn, pad_to(spare, qkv_pad + attn_pad, 2)], 1)
    grad_attn = pad_to(grad_attn, n * piece, 1)
    grad_attn = grad_attn.reshape(depth, n, piece, -1).transpose(1, 0, 2, 3)
    grad_attn = grad_attn.reshape(n * depth * piece, -1)

    grad_mamba_low, grad_attn = lax.optimization_barrier((grad_mamba_out.astype(low), grad_attn))
    grad_mamba_all = seq_gather(grad_mamba_low, 6).reshape(rows, width)
    grad_attn = lax.psum_scatter(grad_attn, "seq", scatter_dimension=0, tiled=True)
    grad_w_mamba = product(mamba_low, grad_mamba_all, (0, 0), out=low)
    grad_mix = product(grad_mamba_all, w_mamba, (1, 1))
    grad_y = grad_mix * silu_z
    grad_z = (grad_mix * y_full * silu_slope(z_gate)).astype(low)
    grad_w_z = product(normed_all, grad_z, (0, 0), out=low)
    grad_y, grad_w_z, grad_w_mamba, down_sum = lax.optimization_barrier(
        (grad_y, grad_w_z, grad_w_mamba, down_sum)
    )
    own_mamba, own_z = depth_sum(grad_w_mamba), depth_sum(grad_w_z)
    grad_skip = jnp.sum(grad_y * mixed, 0, keepdims=True)
    grad_steps, grad_x, grad_b, grad_c, grad_a = scan_bwd(
        info, steps, mixed, state_weights(b_sel, c_sel), grad_y, a_t, firsts, n
    )
    grad_dt_pre = grad_steps * jax.nn.sigmoid(dt_pre)
    grad_dt_bias = jnp.sum(grad_dt_pre, 0, keepdims=True)
    grad_ranks = product(steps_t, grad_dt_pre, (1, 1), exact=True)
    grad_selected = all_sum(jnp.concatenate([grad_ranks, grad_b, grad_c], 0), 8)
    grad_selected, grad_attn = lax.optimization_barrier((grad_selected, grad_attn))
    own_attn = depth_sum(grad_attn)
    grad_w_steps = product(ranks, grad_dt_pre, (1, 0), exact=True)
    grad_w_select = product(grad_selected, mixed, (1, 0), exact=True)
    grad_mixed = grad_y * skip + grad_x + product(grad_selected, select_t, (0, 0), exact=True)
    grad_conv = grad_mixed * silu_slope(conv_pre)
    grad_mixer, grad_taps, grad_bias = conv_bwd(info, grad_conv, mixer_in, taps_t, n)

    grad_mixer, own_mamba, own_z = lax.optimization_barrier((grad_mixer, own_mamba, own_z))

    grad_w_x = product(normed_all, grad_mixer, (0, 0), out=low)
    grad_small = jnp.concatenate(
        [grad_taps, grad_bias, grad_w_select, grad_w_steps, grad_dt_bias, grad_a * a_t, grad_skip], 0
    )
    grad_small = pad_to(grad_small, small_rows, 0).astype(low)
    grad_in = jnp.concatenate([grad_mixer, grad_z], 1)
    grad_in, grad_w_x, grad_small, own_w_units, own_w_down = lax.optimization_barrier(
        (grad_in, grad_w_x, grad_small, own_w_units, own_w_down)
    )
    own_x = depth_sum(grad_w_x)
    all_w_units, all_w_down = lax.all_gather(own_w_units, "seq"), lax.all_gather(own_w_down, "seq")
    own_small = turned_sum(grad_small.reshape(small_rows, depth, chunk_pad).transpose(1, 0, 2))
    grad_normed = in_rows(product(grad_in, w_in, (1, 1), out=low)).reshape(n, tokens, width)
    grad_normed = seq_reduce(grad_normed, 9)
    layer_out = middle + down_sum.astype(F32)
    grad_normed = grad_normed + product(grad_qkv, w_qkv, (0, 1))
    grad_input_norm, grad_g_in = norm_back(hidden, inv_in, gain_norm, grad_normed)
    inputs_grad = (grad_middle + grad_input_norm)[None]
    gain_rows = up_to(-(-width // chunk_pad), 16)
    grad_g_in = pad_to((grad_g_in + grad_g_meta)[None], gain_rows * chunk_pad, 1)
    grad_g_in = grad_g_in.reshape(gain_rows, chunk_pad)
    own_small = jnp.concatenate([own_small, grad_g_in], 0).astype(low)

    all_small, all_x, all_z, all_mamba, all_attn = last_gather(
        [own_small, own_x, own_z, own_mamba, pad_to(own_attn, up_to(piece, 16), 0)], 10
    )
    all_gain = jnp.sum(all_small[:, small_rows:].astype(F32), 0).reshape(-1)[:width]
    all_gain = turned_sum(all_gain.reshape(depth, shard_rows))
    grad_w_mamba = lay_rows(all_mamba, chunk)
    all_attn = all_attn[:, :piece]
    grad_attn = all_attn.reshape(n * piece, -1)
    grad_w_attn = grad_attn[:shard_rows, qkv_pad : qkv_pad + width].astype(F32)
    gains = grad_attn[shard_rows + meta_own : shard_rows + meta_own + 3, :shard_rows].astype(F32)
    grad_meta = grad_attn[shard_rows : shard_rows + meta_own, :width].astype(F32)
    grad_w_proj = lay_cols(
        [(all_x, 0), (all_z, 0)], chunk, chunk_pad, EI, grad_attn[:shard_rows], qkv_cols
    )
    grad_w_proj, all_w_units, all_w_down = lax.optimization_barrier(
        (grad_w_proj, all_w_units, all_w_down)
    )
    unit_cols = (unit_chunk, unit_pad, hidden_units)
    grad_w_gate = lay_cols([(all_w_units, 0)], *unit_cols)
    grad_w_up = lay_cols([(all_w_units, 1)], *unit_cols)
    grad_w_down = lay_rows_turned(all_w_down, unit_chunk).T
    grad_small = lay_cols([(all_small[:, :small_rows], 0)], chunk, chunk_pad, EI // depth)
    grad_taps, grad_bias, grad_w_select, grad_w_steps, grad_dt_bias, grad_decay, grad_skip = (
        grad_small[a:b].T for a, b in zip(ends[:-1], ends[1:])
    )

    return (
        layer_out.astype(low)[None],
        inputs_grad,
        all_gain,
        grad_w_proj,
        grad_taps,
        grad_bias[:, 0],
        grad_w_select,
        grad_w_steps,
        grad_dt_bias[:, 0],
        grad_decay,
        grad_skip[:, 0],
        grad_meta,
        grad_w_attn,
        grad_w_mamba,
        gains[0],
        gains[1],
        gains[2],
        grad_w_gate,
        grad_w_up,
        grad_w_down,
    )


def solution(mesh):
    in_specs = (
        P("fsdp", "seq", None),
        P("fsdp", "seq"),
        P("fsdp"),
        P("fsdp", None),
        P("fsdp", None),
        P("fsdp"),
        P("fsdp", None),
        P("fsdp", None),
        P("fsdp"),
        P("fsdp", None),
        P("fsdp"),
        P("fsdp", None),
        P("fsdp", None),
        P("fsdp", None),
        P("fsdp"),
        P("fsdp"),
        P("fsdp"),
        P("fsdp", None),
        P("fsdp", None),
        P("fsdp", None),
        P("fsdp", "seq", None),
    )
    out_specs = (
        P("fsdp", "seq", None),
        P("fsdp", "seq", None),
        P("fsdp"),
        P("fsdp", None),
        P("fsdp", None),
        P("fsdp"),
        P("fsdp", None),
        P("fsdp", None),
        P("fsdp"),
        P("fsdp", None),
        P("fsdp"),
        P("fsdp", None),
        P("fsdp", None),
        P("fsdp", None),
        P("fsdp"),
        P("fsdp"),
        P("fsdp"),
        P("fsdp", None),
        P("fsdp", None),
        P("fsdp", None),
    )
    return jax.shard_map(shards, mesh=mesh, in_specs=in_specs, out_specs=out_specs, check_vma=False)
```

```python
import functools

import jax
import jax.numpy as jnp
import numpy as np
from jax import lax
from jax.experimental import pallas as pl
from jax.experimental.layout import Layout, with_layout_constraint
from jax.experimental.pallas import tpu as pltpu
from jax.sharding import PartitionSpec as P

HQ = 25
HK = 5
HD = 64
EI = 3200
NS = 16
KC = 4
RDT = 100
META = 128
WIN = 1024
GAP = 8
STEP = 2048
LOG2E = 1.4426950408889634
NEG = -jnp.inf

EPS = 1e-05
HIGH = lax.Precision.HIGHEST
LANES = 128
CHUNK = 128
F32 = jnp.float32
MESH = pl.DeviceIdType.MESH


def fold_rows(first, second, level):
    bit = (lax.broadcasted_iota(jnp.int32, first.shape, 0) >> level) & 1
    upper = bit == 0
    return jnp.where(upper, first, second) + pltpu.roll(
        jnp.where(upper, second, first), 8 - (1 << level), 0
    )


def fold_in(stack, part):
    level = 0
    while stack and stack[-1][0] == level:
        part = fold_rows(stack.pop()[1], part, level)
        level += 1
    stack.append((level, part))


def fold_in_down(stack, part):
    level = 0
    while stack and stack[-1][0] == level:
        part = fold_rows(part, stack.pop()[1], level)
        level += 1
    stack.append((level, part))


def halves(part):
    return part[:8] + part[8:]


def scan_fwd_body(info, dt_ref, x_ref, b_ref, c_ref, a_ref, y_ref, first_ref, state):
    block, piece = pl.program_id(0), pl.program_id(1)
    tiles = a_ref.shape[1] // LANES
    keep = jnp.where(piece == 0, info[1 + block], 1).astype(F32)

    @pl.when((block == 0) & (piece == 0))
    def _():
        state[...] = jnp.zeros_like(state)

    first = state[...] * keep
    first_ref[0] = first
    a2 = a_ref[...] * LOG2E

    def cut(values, l):
        return values[:, l * LANES : (l + 1) * LANES]

    def group(g, carried):
        bt, ct, hs = carried
        stacks = [[] for _ in range(tiles)]
        hs = list(hs)
        for k in range(8):
            bk = jnp.broadcast_to(bt[:, k : k + 1], (NS, LANES))
            ck = jnp.broadcast_to(ct[:, k : k + 1], (NS, LANES))
            for l in range(tiles):
                lane = slice(l * LANES, (l + 1) * LANES)
                dtk = dt_ref[g, k : k + 1, lane]
                uk = dtk * x_ref[g, k : k + 1, lane]
                hs[l] = jnp.exp2(dtk * cut(a2, l)) * hs[l] + uk * bk
                fold_in(stacks[l], halves(hs[l] * ck))
        for l in range(tiles):
            y_ref[g, :, l * LANES : (l + 1) * LANES] = stacks[l][0][1]
        return pltpu.roll(bt, LANES - 8, 1), pltpu.roll(ct, LANES - 8, 1), tuple(hs)

    start = tuple(cut(first, l) for l in range(tiles))
    _, _, hs = lax.fori_loop(0, CHUNK // 8, group, (b_ref[...], c_ref[...], start))
    for l in range(tiles):
        state[:, l * LANES : (l + 1) * LANES] = hs[l]


def spread_lanes(bc_ref, wide, both):
    rows = lax.broadcasted_iota(jnp.int32, (NS, LANES), 0)
    lanes = lax.broadcasted_iota(jnp.int32, (NS, LANES), 1)
    own = (lanes % NS == rows) & (lanes < 4 * NS)

    def lay(g, _):
        for k in range(8):
            span = pl.ds(pl.multiple_of((g * 8 + k) * NS, NS), NS)
            wide[span, :] = jnp.where(own, bc_ref[g, k : k + 1, :], 0.0).astype(jnp.bfloat16)
        return 0

    lax.fori_loop(0, CHUNK // 8, lay, 0)
    source = lax.broadcasted_iota(jnp.int32, (LANES, 2 * LANES), 0)
    target = lax.broadcasted_iota(jnp.int32, (LANES, 2 * LANES), 1)
    ones = (source // (2 * NS) == target // LANES).astype(jnp.bfloat16)

    def multiply(i, _):
        span = pl.ds(pl.multiple_of(i * STEP, STEP), STEP)
        both[span, :] = jnp.dot(wide[span, :], ones, preferred_element_type=F32)
        return 0

    lax.fori_loop(0, CHUNK * NS // STEP, multiply, 0)


def scan_bwd_body(
    info, dt_ref, x_ref, bc_ref, gy_ref, a_ref, first_ref,
    gdt_ref, gx_ref, gb_ref, gc_ref, ga_ref, carry, states, decays, wide, both, lanes_c,
):
    turn, piece = pl.program_id(0), pl.program_id(1)
    n_blocks, pieces = pl.num_programs(0), pl.num_programs(1)
    tiles = a_ref.shape[1] // LANES
    after = jnp.minimum(n_blocks - turn, n_blocks - 1)
    keep = jnp.where(piece == 0, info[1 + after], 1).astype(F32)
    lanes_b = wide

    @pl.when((turn == 0) & (piece == 0))
    def _():
        carry[...] = jnp.zeros_like(carry)
        ga_ref[...] = jnp.zeros_like(ga_ref)

    def cut(values, l):
        return values[:, l * LANES : (l + 1) * LANES]

    spread_lanes(bc_ref, wide, both)
    a2 = a_ref[...] * LOG2E

    def again(g, hs):
        hs = list(hs)
        for k in range(8):
            span = pl.ds(pl.multiple_of((g * 8 + k) * NS, NS), NS)
            bk = both[span, :LANES]
            for l in range(tiles):
                lane = slice(l * LANES, (l + 1) * LANES)
                dtk = dt_ref[g, k : k + 1, lane]
                uk = dtk * x_ref[g, k : k + 1, lane]
                decay = jnp.exp2(dtk * cut(a2, l))
                hs[l] = decay * hs[l] + uk * bk
                decays[g * 8 + k, :, lane] = decay
                states[g * 8 + k + 1, :, lane] = hs[l]
        return tuple(hs)

    states[0] = first_ref[0]
    lax.fori_loop(0, CHUNK // 8, again, tuple(cut(first_ref[0], l) for l in range(tiles)))

    def group(turn_g, gs):
        g = CHUNK // 8 - 1 - turn_g
        gs = list(gs)
        logs, drives = [[] for _ in range(tiles)], [[] for _ in range(tiles)]
        sums = [None] * tiles
        for k in reversed(range(8)):
            t = g * 8 + k
            span = pl.ds(pl.multiple_of(t * NS, NS), NS)
            bk, ck = both[span, :LANES], both[span, LANES:]
            to_b = to_c = None
            for l in range(tiles):
                lane = slice(l * LANES, (l + 1) * LANES)
                gyk = gy_ref[g, k : k + 1, lane]
                dtk = dt_ref[g, k : k + 1, lane]
                uk = dtk * x_ref[g, k : k + 1, lane]
                grad = ck * gyk + gs[l]
                gs[l] = decays[t, :, lane] * grad
                log = gs[l] * states[t, :, lane]
                fold_in_down(logs[l], halves(log * cut(a_ref[...], l)))
                fold_in_down(drives[l], halves(grad * bk))
                part_b = grad * uk
                part_c = states[t + 1, :, lane] * gyk
                to_b = part_b if to_b is None else to_b + part_b
                to_c = part_c if to_c is None else to_c + part_c
                part_a = log * dtk
                sums[l] = part_a if sums[l] is None else sums[l] + part_a
            lanes_b[span, :] = to_b.astype(jnp.bfloat16)
            lanes_c[span, :] = to_c.astype(jnp.bfloat16)
        for l in range(tiles):
            lane = slice(l * LANES, (l + 1) * LANES)
            driven = drives[l][0][1]
            gdt_ref[g, :, lane] = logs[l][0][1] + driven * x_ref[g, :, lane]
            gx_ref[g, :, lane] = driven * dt_ref[g, :, lane]
            ga_ref[:, lane] += sums[l]
        return tuple(gs)

    held = tuple(carry[:, l * LANES : (l + 1) * LANES] * keep for l in range(tiles))
    gs = lax.fori_loop(0, CHUNK // 8, group, held)
    for l in range(tiles):
        carry[:, l * LANES : (l + 1) * LANES] = gs[l]

    lane_ids = lax.broadcasted_iota(jnp.int32, (NS, LANES), 1)
    ones = jnp.ones((LANES, LANES), jnp.bfloat16)

    def collect(i, carried):
        gbt, gct = carried
        span = pl.ds(pl.multiple_of(i * STEP, STEP), STEP)
        sum_b = jnp.dot(lanes_b[span, :], ones, preferred_element_type=F32)
        sum_c = jnp.dot(lanes_c[span, :], ones, preferred_element_type=F32)
        for k in range(STEP // NS):
            here = lane_ids == i * (STEP // NS) + k
            gbt = jnp.where(here, sum_b[k * NS : (k + 1) * NS], gbt)
            gct = jnp.where(here, sum_c[k * NS : (k + 1) * NS], gct)
        return gbt, gct

    zero = jnp.zeros((NS, LANES), F32)
    gbt, gct = lax.fori_loop(0, CHUNK * NS // STEP, collect, (zero, zero))
    gb_ref[...] = gbt
    gc_ref[...] = gct


def state_weights(b_t, c_t):
    parts = []
    for values in (b_t.T, c_t.T):
        high = lax.reduce_precision(values, 8, 7)
        parts += [high, values - high]
    return jnp.pad(jnp.concatenate(parts, 1), ((0, 0), (0, LANES - 4 * NS)))


def scan_fwd(info, dt, x, b_t, c_t, a_t, n_blocks):
    rows, width = dt.shape
    pieces = rows // n_blocks // CHUNK

    def at(i, j, info):
        return (i ^ info[0]) * pieces + j

    wide = pl.BlockSpec((CHUNK // 8, 8, width), lambda i, j, info: (at(i, j, info), 0, 0))
    tall = pl.BlockSpec((NS, CHUNK), lambda i, j, info: (0, at(i, j, info)))
    whole = pl.BlockSpec((NS, width), lambda i, j, info: (0, 0))
    dt, x = (v.reshape(-1, 8, width) for v in (dt, x))
    y, firsts = pl.pallas_call(
        scan_fwd_body,
        grid_spec=pltpu.PrefetchScalarGridSpec(
            num_scalar_prefetch=1,
            grid=(n_blocks, pieces),
            in_specs=[wide, wide, tall, tall, whole],
            out_specs=[
                wide,
                pl.BlockSpec((1, NS, width), lambda i, j, info: (i * pieces + j, 0, 0)),
            ],
            scratch_shapes=[pltpu.VMEM((NS, width), F32)],
        ),
        out_shape=[
            jax.ShapeDtypeStruct((rows // 8, 8, width), F32),
            jax.ShapeDtypeStruct((n_blocks * pieces, NS, width), F32),
        ],
        compiler_params=pltpu.CompilerParams(vmem_limit_bytes=32 * 2**20),
        cost_estimate=busy(36),
        name="scan_fwd",
    )(info, dt, x, b_t, c_t, a_t)
    return y.reshape(rows, width), firsts


def scan_bwd(info, dt, x, bc, gy, a_t, firsts, n_blocks):
    rows, width = dt.shape
    pieces = rows // n_blocks // CHUNK

    def at(i, j):
        return (n_blocks - 1 - i) * pieces + pieces - 1 - j

    wide = pl.BlockSpec((CHUNK // 8, 8, width), lambda i, j, info: (at(i, j), 0, 0))
    tall = pl.BlockSpec((CHUNK // 8, 8, LANES), lambda i, j, info: (at(i, j), 0, 0))
    turned = pl.BlockSpec((NS, CHUNK), lambda i, j, info: (0, at(i, j)))
    whole = pl.BlockSpec((NS, width), lambda i, j, info: (0, 0))
    first = pl.BlockSpec((1, NS, width), lambda i, j, info: (at(i, j), 0, 0))
    gdt, gx, gb, gc, ga = pl.pallas_call(
        scan_bwd_body,
        grid_spec=pltpu.PrefetchScalarGridSpec(
            num_scalar_prefetch=1,
            grid=(n_blocks, pieces),
            in_specs=[wide, wide, tall, wide, whole, first],
            out_specs=[wide, wide, turned, turned, whole],
            scratch_shapes=[
                pltpu.VMEM((NS, width), F32),
                pltpu.VMEM((CHUNK + 1, NS, width), F32),
                pltpu.VMEM((CHUNK, NS, width), F32),
                pltpu.VMEM((CHUNK * NS, LANES), jnp.bfloat16),
                pltpu.VMEM((CHUNK * NS, 2 * LANES), F32),
                pltpu.VMEM((CHUNK * NS, LANES), jnp.bfloat16),
            ],
        ),
        out_shape=[
            jax.ShapeDtypeStruct((rows // 8, 8, width), F32),
            jax.ShapeDtypeStruct((rows // 8, 8, width), F32),
            jax.ShapeDtypeStruct((NS, rows), F32),
            jax.ShapeDtypeStruct((NS, rows), F32),
            jax.ShapeDtypeStruct((NS, width), F32),
        ],
        compiler_params=pltpu.CompilerParams(vmem_limit_bytes=40 * 2**20),
        cost_estimate=busy(90),
        name="scan_bwd",
    )(
        info, dt.reshape(-1, 8, width), x.reshape(-1, 8, width), bc.reshape(-1, 8, LANES),
        gy.reshape(-1, 8, width), a_t, firsts,
    )
    return gdt.reshape(rows, width), gx.reshape(rows, width), gb, gc, ga


def conv_fwd_body(info, x_ref, taps_ref, bias_ref, out_ref, mixed_ref, padded, *, taps):
    block = pl.program_id(0)
    rows = x_ref.shape[0]
    keep = info[1 + block].astype(F32)

    @pl.when(block == 0)
    def _():
        padded[...] = jnp.zeros_like(padded)

    padded[0:8, :] = padded[rows : rows + 8, :] * keep
    padded[8 : rows + 8, :] = x_ref[...].astype(F32)
    total = bias_ref[...] + taps_ref[0:1, :] * padded[8 - taps + 1 : 8 - taps + 1 + rows, :]
    for i in range(1, taps):
        total += taps_ref[i : i + 1, :] * padded[8 - taps + 1 + i : 8 - taps + 1 + i + rows, :]
    out_ref[...] = total
    mixed_ref[...] = jax.nn.silu(total)


def conv_bwd_body(info, g_ref, x_ref, z_ref, taps_ref, gx_ref, gw_ref, gb_ref, padded, *, taps):
    turn = pl.program_id(0)
    n_blocks = pl.num_programs(0)
    rows = x_ref.shape[0]
    after = jnp.minimum(n_blocks - turn, n_blocks - 1)
    keep = info[1 + after].astype(F32)

    @pl.when(turn == 0)
    def _():
        padded[...] = jnp.zeros_like(padded)
        gw_ref[...] = jnp.zeros_like(gw_ref)
        gb_ref[...] = jnp.zeros_like(gb_ref)

    padded[rows : rows + 8, :] = padded[0:8, :] * keep
    padded[0:rows, :] = g_ref[...]
    x = x_ref[...].astype(F32)
    total = None
    for i in range(taps):
        moved = padded[taps - 1 - i : taps - 1 - i + rows, :]
        part = taps_ref[i : i + 1, :] * moved
        total = part if total is None else total + part
        gw_ref[i : i + 1, :] += jnp.sum(x * moved, 0, keepdims=True)
    width = x.shape[1]
    gx_ref[:, :width] = total.astype(gx_ref.dtype)
    gx_ref[:, width:] = z_ref[...]
    gb_ref[...] += jnp.sum(padded[0:rows, :], 0, keepdims=True)


def conv_fwd(info, x, taps_t, bias, n_blocks):
    rows, width = x.shape
    block = rows // n_blocks
    wide = pl.BlockSpec((block, width), lambda i, info: (i ^ info[0], 0))
    return pl.pallas_call(
        functools.partial(conv_fwd_body, taps=taps_t.shape[0]),
        grid_spec=pltpu.PrefetchScalarGridSpec(
            num_scalar_prefetch=1,
            grid=(n_blocks,),
            in_specs=[
                wide,
                pl.BlockSpec(taps_t.shape, lambda i, info: (0, 0)),
                pl.BlockSpec((1, width), lambda i, info: (0, 0)),
            ],
            out_specs=[wide, wide],
            scratch_shapes=[pltpu.VMEM((block + 8, width), F32)],
        ),
        out_shape=[jax.ShapeDtypeStruct((rows, width), F32)] * 2,
        compiler_params=pltpu.CompilerParams(vmem_limit_bytes=32 * 2**20),
        cost_estimate=busy(5),
        name="conv_fwd",
    )(info, x, taps_t, bias)


def conv_bwd(info, grad, x, grad_z, taps_t, n_blocks):
    rows, width = x.shape
    block = rows // n_blocks
    wide = pl.BlockSpec((block, width), lambda i, info: ((n_blocks - 1 - i) ^ info[0], 0))
    both = pl.BlockSpec((block, 2 * width), lambda i, info: ((n_blocks - 1 - i) ^ info[0], 0))
    taps_at = pl.BlockSpec(taps_t.shape, lambda i, info: (0, 0))
    one = pl.BlockSpec((1, width), lambda i, info: (0, 0))
    return pl.pallas_call(
        functools.partial(conv_bwd_body, taps=taps_t.shape[0]),
        grid_spec=pltpu.PrefetchScalarGridSpec(
            num_scalar_prefetch=1,
            grid=(n_blocks,),
            in_specs=[wide, wide, wide, taps_at],
            out_specs=[both, taps_at, one],
            scratch_shapes=[pltpu.VMEM((block + 8, width), F32)],
        ),
        out_shape=[
            jax.ShapeDtypeStruct((rows, 2 * width), jnp.bfloat16),
            jax.ShapeDtypeStruct(taps_t.shape, F32),
            jax.ShapeDtypeStruct((1, width), F32),
        ],
        compiler_params=pltpu.CompilerParams(vmem_limit_bytes=32 * 2**20),
        cost_estimate=busy(9),
        name="conv_bwd",
    )(info, grad, x, grad_z, taps_t)


def busy(us):
    return pl.CostEstimate(flops=int(us * 1.1e9), bytes_accessed=0, transcendentals=0)


def on_seq(index):
    return {"seq": index}


def masks_of(n):
    return [1 << bit for bit in range(n.bit_length() - 1)]


def greet_seq(n):
    here = lax.axis_index("seq")
    barrier = pltpu.get_barrier_semaphore()
    masks = masks_of(n)
    for mask in masks:
        pl.semaphore_signal(barrier, inc=1, device_id=on_seq(here ^ mask), device_id_type=MESH)
    return len(masks)


def send_to(source, target, sems, at, mask):
    send, recv = sems
    here = lax.axis_index("seq")
    return pltpu.make_async_remote_copy(
        src_ref=source,
        dst_ref=target,
        send_sem=send.at[at],
        recv_sem=recv.at[at],
        device_id=on_seq(here ^ mask),
        device_id_type=MESH,
    )


def crossed(rows, n):
    return n == 8 and rows >= 64


def gather_start(src, out, sems, n):
    here = lax.axis_index("seq")
    if not crossed(src.shape[0], n):
        copies = []

        def bit_step(bit):
            def run():
                if bit:
                    copies[-1].wait_recv()
                size = 1 << bit
                span = pl.ds((here >> bit) << bit, size)
                copy = send_to(out.at[span], out.at[span], sems, bit, size)
                copy.start()
                copies.append(copy)

            return run

        def last():
            copies[-1].wait_recv()
            for copy in copies:
                copy.wait_send()

        return [bit_step(bit) for bit in range(n.bit_length() - 1)] + [last]

    half = -(-src.shape[0] // 32) * 16
    low, high = pl.ds(0, half), pl.ds(half, src.shape[0] - half)
    own = out.at[here]
    to_2, to_4, to_1 = (
        send_to(src, own, sems, 0, 2),
        send_to(src, own, sems, 1, 4),
        send_to(src, own, sems, 2, 1),
    )
    for copy in (to_2, to_4, to_1):
        copy.start()
    from_2, from_4, from_6 = out.at[here ^ 2], out.at[here ^ 4], out.at[here ^ 6]
    on_4 = send_to(from_2.at[low], from_2.at[low], sems, 3, 4)
    on_2 = send_to(from_4.at[high], from_4.at[high], sems, 4, 2)
    core_2, core_4, core_6 = (
        send_to(block, block, sems, 5 + i, 1) for i, block in enumerate((from_2, from_4, from_6))
    )

    def second():
        to_2.wait_recv()
        on_4.start()
        core_2.start()
        to_4.wait_recv()
        on_2.start()
        core_4.start()

    def third():
        on_4.wait_recv()
        on_2.wait_recv()
        core_6.start()

    def last():
        for copy in (to_1, core_2, core_4, core_6):
            copy.wait_recv()
        for copy in (to_2, to_4, to_1, on_4, on_2, core_2, core_4, core_6):
            copy.wait_send()

    return [second, third, last]


def gather_body(src, out, local, send, recv, *, n):
    here = lax.axis_index("seq")
    own = pltpu.make_async_copy(src, out.at[here], local)
    own.start()
    count = greet_seq(n)
    pl.semaphore_wait(pltpu.get_barrier_semaphore(), count)
    cross = crossed(src.shape[0], n)
    if not cross:
        own.wait()
    for step in gather_start(src, out, (send, recv), n):
        step()
    if cross:
        own.wait()


def seq_gather(block, call):
    n = lax.axis_size("seq")
    return pl.pallas_call(
        functools.partial(gather_body, n=n),
        out_shape=jax.ShapeDtypeStruct((n,) + block.shape, block.dtype),
        in_specs=[pl.BlockSpec(memory_space=pl.ANY)],
        out_specs=pl.BlockSpec(memory_space=pl.ANY),
        scratch_shapes=[
            pltpu.SemaphoreType.DMA(()),
            pltpu.SemaphoreType.DMA((8,)),
            pltpu.SemaphoreType.DMA((8,)),
        ],
        compiler_params=pltpu.CompilerParams(collective_id=call, has_side_effects=True),
        cost_estimate=busy(35),
        name="seq_gather",
    )(block)


def add_rows(out, one, two, start, size, step=16):
    def turn(i, _):
        rows = pl.ds(pl.multiple_of(start + i * step, step), step)
        out[rows, :] = (one[rows, :].astype(F32) + two[rows, :].astype(F32)).astype(out.dtype)
        return 0

    lax.fori_loop(0, size // step, turn, 0)


def reduce_steps(blocks, out, came, sums, ends, sems, n, at=0):
    here = lax.axis_index("seq")
    tokens = blocks.shape[1]
    if n != 8:
        held = blocks
        for k, bit in enumerate(reversed(range(n.bit_length() - 1))):
            size = 1 << bit
            first = (here >> bit) & 1
            other = pl.ds((1 - first) * size, size)
            copy = send_to(held.at[other], came.at[pl.ds(size, size)], sems, at + k, size)
            copy.start()
            copy.wait()
            for j in range(size):
                add_rows(
                    sums.at[size + j], held.at[first * size + j], came.at[size + j], 0, tokens
                )
            held = sums.at[pl.ds(size, size)]
        total = sums.at[1]

        def turn(i, _):
            rows = pl.ds(pl.multiple_of(i * 16, 16), 16)
            out[rows, :] = total[rows, :].astype(out.dtype)
            return 0

        lax.fori_loop(0, tokens // 16, turn, 0)
        return
    half = tokens // 2
    low, high = pl.ds(0, half), pl.ds(half, half)
    step = 16 if half % 16 == 0 else 8
    core = [
        send_to(blocks.at[here ^ (mask | 1)], came.at[i], sems, at + i, 1)
        for i, mask in enumerate((6, 2, 4, 0))
    ]
    for copy in core:
        copy.start()
    by_6, by_2, by_4 = (sums.at[i] for i in range(3))
    end_2, end_4, mid_2, mid_4 = ends.at[0], ends.at[1], ends.at[2], ends.at[3]
    dia_2 = send_to(by_6.at[low], mid_4.at[low], sems, at + 4, 2)
    dia_4 = send_to(by_6.at[high], mid_2.at[high], sems, at + 5, 4)
    x_low = send_to(by_2.at[low], end_2.at[low], sems, at + 6, 2)
    y_high = send_to(by_4.at[high], end_4.at[high], sems, at + 7, 4)
    x_high = send_to(by_2.at[high], end_2.at[high], sems, at + 8, 2)
    y_low = send_to(by_4.at[low], end_4.at[low], sems, at + 9, 4)
    core[0].wait_recv()
    add_rows(by_6, blocks.at[here ^ 6], came.at[0], 0, tokens, step)
    dia_2.start()
    dia_4.start()
    core[1].wait_recv()
    add_rows(by_2, blocks.at[here ^ 2], came.at[1], 0, tokens, step)
    x_low.start()
    core[2].wait_recv()
    add_rows(by_4, blocks.at[here ^ 4], came.at[2], 0, tokens, step)
    y_high.start()
    dia_4.wait_recv()
    add_rows(by_2, by_2, mid_2, half, half, step)
    x_high.start()
    dia_2.wait_recv()
    add_rows(by_4, by_4, mid_4, 0, half, step)
    y_low.start()
    core[3].wait_recv()
    add_rows(out, blocks.at[here], came.at[3], 0, tokens, step)
    x_low.wait_recv()
    x_high.wait_recv()
    add_rows(out, out, end_2, 0, tokens, step)
    y_high.wait_recv()
    y_low.wait_recv()
    add_rows(out, out, end_4, 0, tokens, step)
    for copy in core + [dia_2, dia_4, x_low, y_high, x_high, y_low]:
        copy.wait_send()


def reduce_body(blocks, out, came, sums, ends, send, recv, *, n):
    count = greet_seq(n)
    pl.semaphore_wait(pltpu.get_barrier_semaphore(), count)
    reduce_steps(blocks, out, came, sums, ends, (send, recv), n)


def reduce_scratch(n, rows, width, dtype):
    if n != 8:
        return [pltpu.VMEM((n, rows, width), dtype)] * 2 + [pltpu.VMEM((1, 8, 128), dtype)]
    return [
        pltpu.VMEM((4, rows, width), dtype),
        pltpu.VMEM((3, rows, width), dtype),
        pltpu.VMEM((4, rows, width), dtype),
    ]


def seq_reduce(blocks, call):
    n, rows, width = blocks.shape
    return pl.pallas_call(
        functools.partial(reduce_body, n=n),
        out_shape=jax.ShapeDtypeStruct((rows, width), F32),
        in_specs=[pl.BlockSpec(memory_space=pltpu.VMEM)],
        out_specs=pl.BlockSpec(memory_space=pltpu.VMEM),
        scratch_shapes=reduce_scratch(n, rows, width, blocks.dtype)
        + [pltpu.SemaphoreType.DMA((10,)), pltpu.SemaphoreType.DMA((10,))],
        compiler_params=pltpu.CompilerParams(
            collective_id=call, has_side_effects=True, vmem_limit_bytes=56 * 2**20
        ),
        cost_estimate=busy(blocks.size / 8e4),
        name="seq_reduce",
    )(blocks)


def total_body(blocks, out, total, came, sums, ends, send, recv, local, *, n):
    here = lax.axis_index("seq")
    count = greet_seq(n)
    pl.semaphore_wait(pltpu.get_barrier_semaphore(), count)
    reduce_steps(blocks, total, came, sums, ends, (send, recv), n)
    own = pltpu.make_async_copy(total, out.at[here], local)
    own.start()
    cross = crossed(total.shape[0], n)
    if not cross:
        own.wait()
    for step in gather_start(total, out, (send.at[pl.ds(10, 8)], recv.at[pl.ds(10, 8)]), n):
        step()
    if cross:
        own.wait()


def seq_total(blocks, call):
    n, rows, width = blocks.shape
    return pl.pallas_call(
        functools.partial(total_body, n=n),
        out_shape=jax.ShapeDtypeStruct(blocks.shape, F32),
        in_specs=[pl.BlockSpec(memory_space=pltpu.VMEM)],
        out_specs=pl.BlockSpec(memory_space=pltpu.VMEM),
        scratch_shapes=[pltpu.VMEM((rows, width), F32)]
        + reduce_scratch(n, rows, width, F32)
        + [
            pltpu.SemaphoreType.DMA((18,)),
            pltpu.SemaphoreType.DMA((18,)),
            pltpu.SemaphoreType.DMA(()),
        ],
        compiler_params=pltpu.CompilerParams(
            collective_id=call, has_side_effects=True, vmem_limit_bytes=40 * 2**20
        ),
        cost_estimate=busy(20),
        name="seq_total",
    )(blocks)


def line_steps(srcs, outs, send, recv, depth):
    here = lax.axis_index("fsdp")

    def passed(a, k, side):
        shard = here - (k - 1) if side == 0 else here + (k - 1)
        shard = jnp.clip(shard, 0, depth - 1)
        target = here + 1 if side == 0 else here - 1
        target = jnp.clip(target, 0, depth - 1)
        block = outs[a].at[shard]
        return pltpu.make_async_remote_copy(
            src_ref=srcs[a] if k == 1 else block,
            dst_ref=block,
            send_sem=send.at[a, side, k - 1],
            recv_sem=recv.at[a, side, k - 1],
            device_id={"fsdp": target},
            device_id_type=MESH,
        )

    def sends(k, side):
        if side == 0:
            return (here >= k - 1) & (here < depth - 1)
        return (here <= depth - k) & (here > 0)

    def gets(k, side):
        return here >= k if side == 0 else here <= depth - 1 - k

    def arrived(k):
        for side in range(2):

            @pl.when(gets(k, side))
            def _():
                for a in range(len(srcs)):
                    passed(a, k, side).wait_recv()

    def step(k):
        def run():
            if k > 1:
                arrived(k - 1)
            for side in range(2):

                @pl.when(sends(k, side))
                def _():
                    for a in range(len(srcs)):
                        passed(a, k, side).start()

        return run

    def last():
        arrived(depth - 1)
        for k in range(1, depth):
            for side in range(2):

                @pl.when(sends(k, side))
                def _():
                    for a in range(len(srcs)):
                        passed(a, k, side).wait_send()

    return [step(k) for k in range(1, depth)] + [last]


def first_body(*refs, n, depth, blocks, lines):
    srcs, refs = refs[: blocks + lines], refs[blocks + lines :]
    outs = refs[: blocks + lines]
    local, send, recv, line_send, line_recv = refs[blocks + lines :]
    here, level = lax.axis_index("seq"), lax.axis_index("fsdp")
    owns = []
    for a in range(blocks + lines):
        place = outs[a].at[here if a < blocks else level]
        owns.append(pltpu.make_async_copy(srcs[a], place, local.at[a]))
        owns[-1].start()
    count = greet_seq(n)
    barrier = pltpu.get_barrier_semaphore()
    for ready, other in ((level > 0, level - 1), (level < depth - 1, level + 1)):

        @pl.when(ready)
        def _():
            pl.semaphore_signal(
                barrier, inc=1, device_id={"fsdp": jnp.clip(other, 0, depth - 1)}, device_id_type=MESH
            )

    count = count + (level > 0).astype(jnp.int32) + (level < depth - 1).astype(jnp.int32)
    pl.semaphore_wait(barrier, count)
    cross = crossed(srcs[0].shape[0], n)
    if not cross:
        for own in owns[:blocks]:
            own.wait()
    line = line_steps(srcs[blocks:], outs[blocks:], line_send, line_recv, depth)
    line.pop(0)()
    turns = []
    for a in range(blocks):
        along = gather_start(srcs[a], outs[a], (send.at[a], recv.at[a]), n)
        turns += [(2 * i + 2 * a, step) for i, step in enumerate(along)]
    turns += [(2 * i + 0.5, step) for i, step in enumerate(line)]
    for _, step in sorted(turns, key=lambda turn: turn[0]):
        step()
    if cross:
        for own in owns[:blocks]:
            own.wait()
    for own in owns[blocks:]:
        own.wait()


def first_gather(blocks, arrays, call):
    n, depth = lax.axis_size("seq"), lax.axis_size("fsdp")
    count, lines = len(blocks), len(arrays)
    anywhere = pl.BlockSpec(memory_space=pl.ANY)
    return pl.pallas_call(
        functools.partial(first_body, n=n, depth=depth, blocks=count, lines=lines),
        out_shape=[jax.ShapeDtypeStruct((n,) + block.shape, block.dtype) for block in blocks]
        + [jax.ShapeDtypeStruct((depth,) + array.shape, array.dtype) for array in arrays],
        in_specs=[anywhere] * (count + lines),
        out_specs=[anywhere] * (count + lines),
        scratch_shapes=[
            pltpu.SemaphoreType.DMA((count + lines,)),
            pltpu.SemaphoreType.DMA((count, 8)),
            pltpu.SemaphoreType.DMA((count, 8)),
            pltpu.SemaphoreType.DMA((lines, 2, depth - 1)),
            pltpu.SemaphoreType.DMA((lines, 2, depth - 1)),
        ],
        compiler_params=pltpu.CompilerParams(collective_id=call, has_side_effects=True),
        cost_estimate=busy(60),
        name="first_gather",
    )(*blocks, *arrays)


def last_body(*refs, n, count):
    srcs, outs = refs[:count], refs[count : 2 * count]
    local, send, recv = refs[2 * count :]
    here = lax.axis_index("seq")
    owns = [pltpu.make_async_copy(srcs[a], outs[a].at[here], local.at[a]) for a in range(count)]
    for own in owns:
        own.start()
    peers = greet_seq(n)
    pl.semaphore_wait(pltpu.get_barrier_semaphore(), peers)
    cross = [crossed(src.shape[0], n) for src in srcs]
    for a in range(count):
        if not cross[a]:
            owns[a].wait()
    steps = [gather_start(srcs[a], outs[a], (send.at[a], recv.at[a]), n) for a in range(count)]
    for i in range(max(len(part) for part in steps)):
        for part in steps:
            if i < len(part):
                part[i]()
    for a in range(count):
        if cross[a]:
            owns[a].wait()


def last_gather(arrays, call):
    n = lax.axis_size("seq")
    count = len(arrays)
    anywhere = pl.BlockSpec(memory_space=pl.ANY)
    return pl.pallas_call(
        functools.partial(last_body, n=n, count=count),
        out_shape=[jax.ShapeDtypeStruct((n,) + array.shape, array.dtype) for array in arrays],
        in_specs=[anywhere] * count,
        out_specs=[anywhere] * count,
        scratch_shapes=[
            pltpu.SemaphoreType.DMA((count,)),
            pltpu.SemaphoreType.DMA((count, 8)),
            pltpu.SemaphoreType.DMA((count, 8)),
        ],
        compiler_params=pltpu.CompilerParams(collective_id=call, has_side_effects=True),
        cost_estimate=busy(60),
        name="last_gather",
    )(*arrays)


def lay_cols_body(*refs, n, depth, groups, chunk, padded, total, front):
    out = refs[-1]
    if front:
        out[:, :front] = refs[0][:, :front].astype(F32)
    parts = refs[len(refs) - 1 - groups : -1]
    for g, part in enumerate(parts):
        for s in range(n):
            values = part[s].astype(F32)
            for j in range(depth):
                at = front + g * total + j * (total // depth) + s * chunk
                out[:, at : at + chunk] = values[:, j * padded : j * padded + chunk]


def lay_cols(parts, chunk, padded, total, first=None, front=0):
    n, rows, _ = parts[0][0].shape
    depth = total // (n * chunk)
    width = depth * padded
    turns = 1 if rows % 40 else 5
    step = rows // turns
    ins = [] if first is None else [first]
    specs = [] if first is None else [pl.BlockSpec((step, first.shape[1]), lambda i: (i, 0))]
    for _, block in parts:
        specs.append(pl.BlockSpec((n, step, width), lambda i, block=block: (0, i, block)))
    return pl.pallas_call(
        functools.partial(
            lay_cols_body, n=n, depth=depth, groups=len(parts), chunk=chunk, padded=padded,
            total=total, front=front,
        ),
        grid=(turns,),
        out_shape=jax.ShapeDtypeStruct((rows, front + len(parts) * total), F32),
        in_specs=specs,
        out_specs=pl.BlockSpec((step, front + len(parts) * total), lambda i: (i, 0)),
        compiler_params=pltpu.CompilerParams(vmem_limit_bytes=48 * 2**20),
        cost_estimate=busy(8),
        name="lay_cols",
    )(*ins, *(array for array, _ in parts))


def lay_rows_body(parts, out, *, n, chunk):
    for s in range(n):
        out[s * chunk : (s + 1) * chunk, :] = parts[s, :chunk, :].astype(F32)


def lay_rows(parts, chunk):
    n, _, width = parts.shape
    return pl.pallas_call(
        functools.partial(lay_rows_body, n=n, chunk=chunk),
        out_shape=jax.ShapeDtypeStruct((n * chunk, width), F32),
        in_specs=[pl.BlockSpec(memory_space=pltpu.VMEM)],
        out_specs=pl.BlockSpec(memory_space=pltpu.VMEM),
        compiler_params=pltpu.CompilerParams(vmem_limit_bytes=48 * 2**20),
        cost_estimate=busy(4),
        name="lay_rows",
    )(parts)


def lay_rows_turned_body(parts, out, *, n, chunk):
    for s in range(n):
        out[:, s * chunk : (s + 1) * chunk] = parts[s].astype(F32).T[:, :chunk]


def lay_rows_turned(parts, chunk):
    n, padded, width = parts.shape
    return pl.pallas_call(
        functools.partial(lay_rows_turned_body, n=n, chunk=chunk),
        grid=(-(-width // LANES),),
        in_specs=[pl.BlockSpec((n, padded, LANES), lambda i: (0, 0, i))],
        out_specs=pl.BlockSpec((LANES, n * chunk), lambda i: (i, 0)),
        out_shape=jax.ShapeDtypeStruct((width, n * chunk), F32),
        compiler_params=pltpu.CompilerParams(vmem_limit_bytes=48 * 2**20),
        cost_estimate=busy(8),
        name="lay_rows_turned",
    )(parts)


def key_scores(k, q, allowed):
    scores = lax.dot_general(k, q, (((0,), (0,)), ((), ())), preferred_element_type=F32)
    return scores if allowed is None else jnp.where(allowed, scores, NEG)


def block_masks(position, back, rows):
    key = lax.broadcasted_iota(jnp.int32, (rows, rows), 0)
    query = lax.broadcasted_iota(jnp.int32, (rows, rows), 1)
    masks = []
    for distance in range(back, 0, -1):
        reached = jnp.broadcast_to(position >= distance, (rows, rows))
        masks.append((key > query) & reached if distance == back else reached)
    return masks + [key <= query]


def attend_body(info, q_ref, *refs, back):
    keys, values = refs[: back + 2], refs[back + 2 : 2 * back + 4]
    out_ref, norm_ref = refs[2 * back + 4 :]
    q = q_ref[...]
    masks = [None] + block_masks(info[1], back, q.shape[1])
    scores = [key_scores(k[...], q, mask) for k, mask in zip(keys, masks)]
    top = functools.reduce(jnp.maximum, (jnp.max(part, 0, keepdims=True) for part in scores))
    total = jnp.zeros_like(top)
    out = jnp.zeros(q.shape, F32)
    for part, v in zip(scores, values):
        weights = jnp.exp(part - top)
        total += jnp.sum(weights, 0, keepdims=True)
        out += jnp.dot(v[...], weights.astype(jnp.bfloat16), preferred_element_type=F32)
    out_ref[...] = out / total
    norm_ref[0] = jnp.broadcast_to(top + jnp.log(total), norm_ref.shape[1:])


def attend_back_body(info, q_ref, grad_ref, out_ref, norm_ref, *refs, back):
    count = back + 2
    keys, values = refs[:count], refs[count : 2 * count]
    gq_ref, gk_meta, gv_meta, gk_ref, gv_ref = refs[2 * count :]
    turn = pl.program_id(1)
    q, grad = q_ref[...], grad_ref[...]
    norm = norm_ref[0][0:1]
    shared = jnp.sum(grad.astype(F32) * out_ref[...], 0, keepdims=True)
    masks = [None] + block_masks(info[1], back, q.shape[1])

    @pl.when(turn == 0)
    def _():
        for ref in (gk_meta, gv_meta, gk_ref, gv_ref):
            ref[...] = jnp.zeros_like(ref)

    contract = (((1,), (1,)), ((), ()))
    gq = jnp.zeros(q.shape, F32)
    for i in range(count):
        k, v = keys[i][...], values[i][...]
        weights = jnp.exp(key_scores(k, q, masks[i]) - norm)
        grad_weights = lax.dot_general(
            v, grad, (((0,), (0,)), ((), ())), preferred_element_type=F32
        )
        grad_scores = (weights * (grad_weights - shared)).astype(jnp.bfloat16)
        gq += jnp.dot(k, grad_scores, preferred_element_type=F32)
        gk = lax.dot_general(q, grad_scores, contract, preferred_element_type=F32)
        gv = lax.dot_general(
            grad, weights.astype(jnp.bfloat16), contract, preferred_element_type=F32
        )
        if i == 0:
            gk_meta[...] += gk
            gv_meta[...] += gv
        else:
            gk_ref[i - 1] += gk
            gv_ref[i - 1] += gv
    gq_ref[...] = gq * HD ** (-0.5)


def attend_specs(heads, groups, tokens, meta, n, back):
    size = heads // groups
    head = pl.BlockSpec((HD, tokens), lambda g, j, info: (g * size + j, 0))

    def sides(first):
        specs = [pl.BlockSpec((HD, meta), lambda g, j, info: (first + g, 0))]
        for distance in range(back, -1, -1):
            specs.append(
                pl.BlockSpec(
                    (HD, tokens),
                    lambda g, j, info, distance=distance: (
                        first + g, lax.rem(info[0] - distance + n, n),
                    ),
                )
            )
        return specs

    norm = pl.BlockSpec((1, 8, tokens), lambda g, j, info: (g * size + j, 0, 0))
    return head, sides(0) + sides(groups), norm


def attend(info, q_t, kv_t, meta_t, heads, groups, n, back):
    tokens, meta = q_t.shape[1], meta_t.shape[1]
    head, kv, norm = attend_specs(heads, groups, tokens, meta, n, back)
    return pl.pallas_call(
        functools.partial(attend_body, back=back),
        grid_spec=pltpu.PrefetchScalarGridSpec(
            num_scalar_prefetch=1,
            grid=(groups, heads // groups),
            in_specs=[head] + kv,
            out_specs=[head, norm],
        ),
        out_shape=[
            jax.ShapeDtypeStruct(q_t.shape, F32),
            jax.ShapeDtypeStruct((heads, 8, tokens), F32),
        ],
        compiler_params=pltpu.CompilerParams(vmem_limit_bytes=40 * 2**20),
        cost_estimate=busy(25),
        name="attend",
    )(info, q_t, *(([meta_t] + [kv_t] * (back + 1)) * 2))


def attend_back(info, q_t, grad_t, out_t, norms, kv_t, meta_t, heads, groups, n, back):
    tokens, meta = q_t.shape[1], meta_t.shape[1]
    head, kv, norm = attend_specs(heads, groups, tokens, meta, n, back)
    cols = groups * HD
    window = pl.BlockSpec((back + 1, HD, tokens), lambda g, j, info: (0, g, 0))
    side = pl.BlockSpec((HD, meta), lambda g, j, info: (g, 0))
    return pl.pallas_call(
        functools.partial(attend_back_body, back=back),
        grid_spec=pltpu.PrefetchScalarGridSpec(
            num_scalar_prefetch=1,
            grid=(groups, heads // groups),
            in_specs=[head, head, head, norm] + kv,
            out_specs=[head, side, side, window, window],
        ),
        out_shape=[
            jax.ShapeDtypeStruct(q_t.shape, F32),
            jax.ShapeDtypeStruct((cols, meta), F32),
            jax.ShapeDtypeStruct((cols, meta), F32),
            jax.ShapeDtypeStruct((back + 1, cols, tokens), F32),
            jax.ShapeDtypeStruct((back + 1, cols, tokens), F32),
        ],
        compiler_params=pltpu.CompilerParams(vmem_limit_bytes=48 * 2**20),
        cost_estimate=busy(50),
        name="attend_back",
    )(info, q_t, grad_t, out_t, norms, *(([meta_t] + [kv_t] * (back + 1)) * 2))


def turned_sum(blocks):
    n = lax.axis_size("fsdp")
    here = lax.axis_index("fsdp")
    total = lax.dynamic_index_in_dim(blocks, here, 0, False).astype(F32)
    for k in range(1, n):
        part = lax.dynamic_index_in_dim(blocks, (here + k) % n, 0, False)
        total = total + lax.ppermute(part, "fsdp", [(i, (i + k) % n) for i in range(n)]).astype(F32)
    return total


def in_rows(values):
    return with_layout_constraint(values, Layout(major_to_minor=(0, 1)))


def pad_to(values, size, axis):
    widths = [(0, 0)] * values.ndim
    widths[axis] = (0, size - values.shape[axis])
    return jnp.pad(values, widths)


def norm_fwd(values, gains):
    inverse = lax.rsqrt(jnp.mean(values * values, -1, keepdims=True) + EPS)
    return (values * inverse * gains, inverse)


def norm_back(values, inverse, gains, grads):
    weighted = grads * gains
    mean_term = jnp.mean(values * weighted, -1, keepdims=True)
    return (
        inverse * weighted - values * inverse**3 * mean_term,
        jnp.sum(grads * values * inverse, 0),
    )


def silu_slope(values):
    sigmoid = jax.nn.sigmoid(values)
    return sigmoid * (1.0 + values * (1.0 - sigmoid))


def product(one, two, dims, exact=False, out=F32):
    return lax.dot_general(
        one,
        two,
        ((dims[:1], dims[1:]), ((), ())),
        preferred_element_type=F32,
        precision=lax.Precision.HIGH if exact else None,
    ).astype(out)


def shards(
    inputs, starts, norm_gain, in_weight, conv_weight, conv_bias, xproj_weight, dtproj_weight, dt_bias,
    log_decay, skip_gain, meta_tokens, attn_weight, mamba_weight, attn_gain, mamba_gain, ffn_gain,
    gate_weight, up_weight, down_weight, cotangent,
):
    low = jnp.bfloat16
    n, depth = lax.axis_size("seq"), lax.axis_size("fsdp")
    here = lax.axis_index("seq")
    tokens, width = inputs.shape[1:]
    rows = n * tokens
    q_cols, kv_cols = HQ * HD, HK * HD
    qkv_cols = q_cols + 2 * kv_cols
    group_size = HQ // HK
    inner = EI // n
    hidden_units = gate_weight.shape[1]
    units = hidden_units // n
    shard_rows = width // depth

    if n <= GAP:
        carries = jnp.array([0] + [1] * (n - 1), jnp.int32)
        position = here
    else:
        flags = lax.all_gather(starts[0, 0], "seq")
        carries = 1 - flags
        blocks = jnp.arange(n)
        position = here - jnp.max(jnp.where((flags == 1) & (blocks <= here), blocks, 0))
    info = jnp.concatenate([jnp.zeros((1,), jnp.int32), carries])

    def up_to(size, step):
        return -(-size // step) * step

    chunk, unit_chunk = inner // depth, units // depth
    inner_pad = up_to(depth * up_to(chunk, 16), LANES)
    units_pad = up_to(depth * up_to(unit_chunk, 16), LANES)
    chunk_pad, unit_pad = inner_pad // depth, units_pad // depth

    def own_cols(weight, base, total, padded, here=here):
        size = total // (depth * n)
        parts = [
            pad_to(
                lax.dynamic_slice_in_dim(weight, base + j * (total // depth) + here * size, size, 1),
                padded,
                1,
            )
            for j in range(depth)
        ]
        return jnp.concatenate(parts, 1)

    def own_rows(weight, padded, here=here):
        size = weight.shape[0] // n
        return pad_to(lax.dynamic_slice_in_dim(weight, here * size, size, 0), padded, 0)

    def along_depth(values):
        return lax.all_gather(values, "fsdp")

    small = jnp.concatenate(
        [
            conv_weight.T, conv_bias[None], xproj_weight.T, dtproj_weight.T, dt_bias[None], log_decay.T,
            skip_gain[None],
        ],
        0,
    )
    small_rows = up_to(small.shape[0], 16)
    small = pad_to(lax.dynamic_slice_in_dim(small, here * chunk, chunk, 1), chunk_pad, 1)
    own_in = own_cols(in_weight, qkv_cols, EI, chunk_pad)
    own_z = own_cols(in_weight, qkv_cols + EI, EI, chunk_pad)
    gains = pad_to(jnp.stack([norm_gain, attn_gain, mamba_gain, ffn_gain], 0), 16, 0)
    hidden_all, grad_out_all, w_in, small_full, gain_rows, meta_rows = first_gather(
        [inputs[0], cotangent[0]],
        [jnp.concatenate([own_in, own_z], 1), pad_to(small, small_rows, 0), gains, meta_tokens],
        1,
    )
    w_in = w_in.reshape(width, 2 * inner_pad)
    gain_norm, gain_attn, gain_mamba, gain_ffn = (
        gain_rows[:, i].reshape(-1).astype(F32) for i in range(4)
    )

    small_full, later = lax.optimization_barrier((small_full, here))
    small_full = small_full.transpose(1, 0, 2).reshape(small_rows, inner_pad).astype(F32)
    ends = np.cumsum([0, KC, 1, RDT + 2 * NS, RDT, 1, NS, 1])
    taps_t, bias, select_t, steps_t, b_steps, a_logs, skip = (
        small_full[a:b] for a, b in zip(ends[:-1], ends[1:])
    )
    a_t = -jnp.exp(a_logs)

    piece = up_to(-(-shard_rows // n), 8)

    def attn_piece(weight, cols):
        first = jnp.minimum(later * piece, shard_rows - piece)
        part = lax.dynamic_slice(weight, (first, 0), (piece, cols))
        return lax.dynamic_slice_in_dim(pad_to(part, 2 * piece, 0), later * piece - first, piece, 0)

    own_attn = along_depth(
        jnp.concatenate([attn_piece(in_weight, qkv_cols), attn_piece(attn_weight, width)], 1)
    )
    w_mamba = along_depth(own_rows(mamba_weight, chunk_pad, later)).reshape(inner_pad, width)
    meta_rows = meta_rows.reshape(META, width)

    hidden = inputs[0].astype(F32)
    normed_all, _ = norm_fwd(hidden_all.astype(F32), gain_norm)
    normed_all = normed_all.astype(low).reshape(rows, width)
    normed, inv_in = norm_fwd(hidden, gain_norm)
    normed = normed.astype(low)
    mixer_in = product(normed_all, w_in[:, :inner_pad], (1, 0), out=low)
    z_gate = product(normed_all, w_in[:, inner_pad:], (1, 0), out=low).astype(F32)
    conv_pre, mixed = conv_fwd(info, mixer_in, taps_t, bias, n)

    def all_sum(values, call):
        laid = values.reshape(values.shape[0], n, tokens).transpose(1, 0, 2)
        laid = pad_to(laid, up_to(values.shape[0], 16), 1)
        total = seq_total(laid, call)
        return total.transpose(1, 0, 2).reshape(-1, rows)[: values.shape[0]]

    part = product(select_t, mixed, (1, 1), exact=True)
    selected = all_sum(part, 2)
    selected, own_attn = lax.optimization_barrier((selected, own_attn))
    all_attn = lax.all_gather(own_attn, "seq").transpose(1, 0, 2, 3)
    all_attn = all_attn.reshape(depth, n * piece, -1)[:, :shard_rows].reshape(width, -1)
    w_qkv, w_attn = all_attn[:, :qkv_cols], all_attn[:, qkv_cols:]
    w_q, w_kv = w_qkv[:, :q_cols], w_qkv[:, q_cols:]
    ranks, b_sel, c_sel = selected[:RDT], selected[RDT : RDT + NS], selected[RDT + NS :]
    dt_pre = product(ranks, steps_t, (0, 0), exact=True) + b_steps
    steps = jax.nn.softplus(dt_pre)
    steps, last = lax.optimization_barrier((steps, later))
    y_scan, firsts = scan_fwd(info, steps, mixed, b_sel, c_sel, a_t, n)
    w_units = along_depth(
        jnp.concatenate(
            [
                own_cols(gate_weight, 0, hidden_units, unit_pad, last),
                own_cols(up_weight, 0, hidden_units, unit_pad, last),
            ],
            1,
        )
    ).reshape(width, 2 * units_pad)
    w_down = along_depth(own_rows(down_weight, unit_pad, last)).reshape(units_pad, width)
    grad_out_all = grad_out_all.reshape(rows, width)
    y_full = y_scan + skip * mixed
    silu_z = jax.nn.silu(z_gate)
    mamba_low = (y_full * silu_z).astype(low)
    mamba_out = seq_reduce(
        in_rows(product(mamba_low, w_mamba, (1, 0), out=low)).reshape(n, tokens, width), 3
    )

    blocks_back = WIN // tokens
    attend_at = jnp.stack([here, position]).astype(jnp.int32)
    heads = (HQ, HK, n, blocks_back)
    queries = product(w_q, normed, (0, 1), out=low) * HD ** (-0.5)
    keyvals = product(w_kv, normed_all, (0, 1), out=low)
    meta_float = meta_rows.astype(F32)
    meta_normed, meta_inv = norm_fwd(meta_float, gain_norm)
    meta_low = meta_normed.astype(low)
    meta_kv = product(w_kv, meta_low, (0, 1), out=low)
    contexts, log_norms = attend(attend_at, queries, keyvals, meta_kv, *heads)
    attended = contexts.astype(low)
    attn_out = product(attended, w_attn, (0, 0))

    attn_normed, attn_inv = norm_fwd(attn_out, gain_attn)
    mamba_normed, mamba_inv = norm_fwd(mamba_out, gain_mamba)
    middle = hidden + 0.5 * (attn_normed + mamba_normed)
    ffn_normed, ffn_inv = norm_fwd(middle, gain_ffn)
    ffn_all = seq_gather(ffn_normed.astype(low), 4).reshape(rows, width)
    both_pre = product(ffn_all, w_units, (1, 0))
    gate_pre, up_pre = both_pre[:, :units_pad], both_pre[:, units_pad:]
    grad_act = product(grad_out_all, w_down, (1, 1))
    silu_gate = jax.nn.silu(gate_pre)
    activated = (silu_gate * up_pre).astype(low)
    grad_units = jnp.concatenate(
        [
            (grad_act * up_pre * silu_slope(gate_pre)).astype(low),
            (grad_act * silu_gate).astype(low),
        ],
        1,
    )
    grad_ffn_part = in_rows(product(grad_units, w_units, (1, 1), out=low))
    down_part = product(activated, w_down, (1, 0), out=low)
    grad_w_units = product(ffn_all, grad_units, (0, 0), out=low)
    grad_w_down = in_rows(product(activated, grad_out_all, (0, 0), out=low))
    grad_ffn_part, grad_w_units, grad_w_down, down_part = lax.optimization_barrier(
        (grad_ffn_part, grad_w_units, grad_w_down, down_part)
    )
    grad_ffn_in = seq_reduce(grad_ffn_part.reshape(n, tokens, width), 5)

    def depth_sum(part):
        return lax.psum_scatter(part, "fsdp", scatter_dimension=0, tiled=True)

    own_w_units, own_w_down = depth_sum(grad_w_units), depth_sum(grad_w_down)
    down_sum = lax.psum_scatter(down_part, "seq", scatter_dimension=0, tiled=True)

    grad_out = cotangent[0].astype(F32)
    grad_mid_norm, grad_g_ffn = norm_back(middle, ffn_inv, gain_ffn, grad_ffn_in)
    grad_middle = grad_out + grad_mid_norm
    grad_attn_out, grad_g_attn = norm_back(attn_out, attn_inv, gain_attn, 0.5 * grad_middle)
    grad_mamba_out, grad_g_mamba = norm_back(mamba_out, mamba_inv, gain_mamba, 0.5 * grad_middle)
    grad_attn_low = grad_attn_out.astype(low)

    grad_context = product(w_attn, grad_attn_low, (1, 1), out=low)
    grad_queries, grad_k_meta, grad_v_meta, grad_keys, grad_values = attend_back(
        attend_at, queries, grad_context, contexts, log_norms, keyvals, meta_kv, *heads
    )
    grad_queries, own_w_units, own_w_down = lax.optimization_barrier(
        (grad_queries, own_w_units, own_w_down)
    )
    grad_meta_kv = jnp.concatenate([grad_k_meta, grad_v_meta], 0)
    grad_kv_blocks = lax.dynamic_update_slice_in_dim(
        jnp.zeros((blocks_back + n, 2 * kv_cols, tokens), low),
        jnp.concatenate([grad_keys, grad_values], 1).astype(low),
        here,
        0,
    )[blocks_back:]
    grad_keyvals = seq_reduce(grad_kv_blocks, 7)
    grad_qkv = jnp.concatenate([grad_queries, grad_keyvals], 0).astype(low)
    grad_meta_low = product(grad_meta_kv.astype(low), w_kv, (0, 1))
    grad_meta, grad_g_meta = norm_back(meta_float, meta_inv, gain_norm, grad_meta_low)

    meta_high = grad_meta_kv.astype(low)
    meta_rest = (grad_meta_kv - lax.reduce_precision(grad_meta_kv, 8, 7)).astype(low)
    qkv_pad, attn_pad = up_to(qkv_cols, LANES), up_to(width, LANES)
    meta_side = ((q_cols, qkv_pad - qkv_cols), (0, 0))
    grad_w_qkv = product(
        jnp.concatenate([normed, meta_low, meta_low], 0),
        jnp.concatenate(
            [pad_to(grad_qkv, qkv_pad, 0), jnp.pad(meta_high, meta_side), jnp.pad(meta_rest, meta_side)],
            1,
        ),
        (0, 1),
        out=low,
    )
    grad_w_attn = product(attended, pad_to(grad_attn_low, attn_pad, 1), (1, 0), out=low)
    grad_attn = jnp.concatenate([grad_w_qkv, grad_w_attn], 1).reshape(depth, shard_rows, -1)
    meta_own = META // depth
    grad_gains = jnp.stack([grad_g_attn, grad_g_mamba, grad_g_ffn], 0).astype(low)
    grad_gains = grad_gains.reshape(3, depth, shard_rows).transpose(1, 0, 2)
    spare = jnp.concatenate(
        [grad_meta.astype(low).reshape(depth, meta_own, width), pad_to(grad_gains, width, 2)], 1
    )
    spare = pad_to(spare, up_to(meta_own + 3, 16), 1)
    piece = up_to(-(-(shard_rows + spare.shape[1]) // n), 8)
    grad_attn = jnp.concatenate([grad_attn, pad_to(spare, qkv_pad + attn_pad, 2)], 1)
    grad_attn = pad_to(grad_attn, n * piece, 1)
    grad_attn = grad_attn.reshape(depth, n, piece, -1).transpose(1, 0, 2, 3)
    grad_attn = grad_attn.reshape(n * depth * piece, -1)

    grad_mamba_low, grad_attn = lax.optimization_barrier((grad_mamba_out.astype(low), grad_attn))
    grad_mamba_all = seq_gather(grad_mamba_low, 6).reshape(rows, width)
    grad_attn = lax.psum_scatter(grad_attn, "seq", scatter_dimension=0, tiled=True)
    grad_w_mamba = in_rows(product(mamba_low, grad_mamba_all, (0, 0), out=low))
    grad_mix = product(grad_mamba_all, w_mamba, (1, 1))
    grad_y = grad_mix * silu_z
    grad_z = (grad_mix * y_full * silu_slope(z_gate)).astype(low)
    grad_w_z = product(normed_all, grad_z, (0, 0), out=low)
    grad_y, grad_w_z, grad_w_mamba, down_sum = lax.optimization_barrier(
        (grad_y, grad_w_z, grad_w_mamba, down_sum)
    )
    own_mamba, own_z = depth_sum(grad_w_mamba), depth_sum(grad_w_z)
    grad_skip = jnp.sum(grad_y * mixed, 0, keepdims=True)
    grad_steps, grad_x, grad_b, grad_c, grad_a = scan_bwd(
        info, steps, mixed, state_weights(b_sel, c_sel), grad_y, a_t, firsts, n
    )
    grad_dt_pre = grad_steps * jax.nn.sigmoid(dt_pre)
    grad_dt_bias = jnp.sum(grad_dt_pre, 0, keepdims=True)
    grad_ranks = product(steps_t, grad_dt_pre, (1, 1))
    grad_selected = all_sum(jnp.concatenate([grad_ranks, grad_b, grad_c], 0), 8)
    grad_selected, grad_attn = lax.optimization_barrier((grad_selected, grad_attn))
    own_attn = depth_sum(grad_attn)
    grad_w_steps = product(ranks, grad_dt_pre, (1, 0))
    grad_w_select = product(grad_selected, mixed, (1, 0))
    grad_mixed = grad_y * skip + grad_x + product(grad_selected, select_t, (0, 0))
    grad_conv = grad_mixed * silu_slope(conv_pre)
    grad_in, grad_taps, grad_bias = conv_bwd(info, grad_conv, mixer_in, grad_z, taps_t, n)

    grad_w_x = product(normed_all, grad_in[:, :inner_pad], (0, 0), out=low)
    grad_small = jnp.concatenate(
        [grad_taps, grad_bias, grad_w_select, grad_w_steps, grad_dt_bias, grad_a * a_t, grad_skip], 0
    )
    grad_small = pad_to(grad_small, small_rows, 0).astype(low)
    grad_in, grad_w_x, grad_small, own_w_units, own_w_down, own_mamba, own_z = (
        lax.optimization_barrier(
            (grad_in, grad_w_x, grad_small, own_w_units, own_w_down, own_mamba, own_z)
        )
    )
    own_x = depth_sum(grad_w_x)
    all_w_units, all_w_down = lax.all_gather(own_w_units, "seq"), lax.all_gather(own_w_down, "seq")
    own_small = turned_sum(grad_small.reshape(small_rows, depth, chunk_pad).transpose(1, 0, 2))
    grad_normed = in_rows(product(grad_in, w_in, (1, 1), out=low)).reshape(n, tokens, width)
    grad_normed = seq_reduce(grad_normed, 9)
    layer_out = middle + down_sum.astype(F32)
    grad_normed = grad_normed + product(grad_qkv, w_qkv, (0, 1))
    grad_input_norm, grad_g_in = norm_back(hidden, inv_in, gain_norm, grad_normed)
    inputs_grad = (grad_middle + grad_input_norm)[None]
    gain_rows = up_to(-(-width // chunk_pad), 16)
    grad_g_in = pad_to((grad_g_in + grad_g_meta)[None], gain_rows * chunk_pad, 1)
    grad_g_in = grad_g_in.reshape(gain_rows, chunk_pad)
    own_small = jnp.concatenate([own_small, grad_g_in], 0).astype(low)

    all_small, all_x, all_z, all_mamba, all_attn = last_gather(
        [own_small, own_x, own_z, own_mamba, pad_to(own_attn, up_to(piece, 16), 0)], 10
    )
    all_gain = jnp.sum(all_small[:, small_rows:].astype(F32), 0).reshape(-1)[:width]
    all_gain = turned_sum(all_gain.reshape(depth, shard_rows))
    grad_w_mamba = lay_rows(all_mamba, chunk)
    all_attn = all_attn[:, :piece]
    grad_attn = all_attn.reshape(n * piece, -1)
    grad_w_attn = grad_attn[:shard_rows, qkv_pad : qkv_pad + width].astype(F32)
    gains = grad_attn[shard_rows + meta_own : shard_rows + meta_own + 3, :shard_rows].astype(F32)
    grad_meta = grad_attn[shard_rows : shard_rows + meta_own, :width].astype(F32)
    grad_w_proj = lay_cols(
        [(all_x, 0), (all_z, 0)], chunk, chunk_pad, EI, grad_attn[:shard_rows], qkv_cols
    )
    grad_w_proj, all_w_units, all_w_down = lax.optimization_barrier(
        (grad_w_proj, all_w_units, all_w_down)
    )
    unit_cols = (unit_chunk, unit_pad, hidden_units)
    grad_w_gate = lay_cols([(all_w_units, 0)], *unit_cols)
    grad_w_up = lay_cols([(all_w_units, 1)], *unit_cols)
    grad_w_down = lay_rows_turned(all_w_down, unit_chunk).T
    grad_small = lay_cols([(all_small[:, :small_rows], 0)], chunk, chunk_pad, EI // depth)
    grad_taps, grad_bias, grad_w_select, grad_w_steps, grad_dt_bias, grad_decay, grad_skip = (
        grad_small[a:b].T for a, b in zip(ends[:-1], ends[1:])
    )

    return (
        layer_out.astype(low)[None],
        inputs_grad,
        all_gain,
        grad_w_proj,
        grad_taps,
        grad_bias[:, 0],
        grad_w_select,
        grad_w_steps,
        grad_dt_bias[:, 0],
        grad_decay,
        grad_skip[:, 0],
        grad_meta,
        grad_w_attn,
        grad_w_mamba,
        gains[0],
        gains[1],
        gains[2],
        grad_w_gate,
        grad_w_up,
        grad_w_down,
    )


def solution(mesh):
    in_specs = (
        P("fsdp", "seq", None),
        P("fsdp", "seq"),
        P("fsdp"),
        P("fsdp", None),
        P("fsdp", None),
        P("fsdp"),
        P("fsdp", None),
        P("fsdp", None),
        P("fsdp"),
        P("fsdp", None),
        P("fsdp"),
        P("fsdp", None),
        P("fsdp", None),
        P("fsdp", None),
        P("fsdp"),
        P("fsdp"),
        P("fsdp"),
        P("fsdp", None),
        P("fsdp", None),
        P("fsdp", None),
        P("fsdp", "seq", None),
    )
    out_specs = (
        P("fsdp", "seq", None),
        P("fsdp", "seq", None),
        P("fsdp"),
        P("fsdp", None),
        P("fsdp", None),
        P("fsdp"),
        P("fsdp", None),
        P("fsdp", None),
        P("fsdp"),
        P("fsdp", None),
        P("fsdp"),
        P("fsdp", None),
        P("fsdp", None),
        P("fsdp", None),
        P("fsdp"),
        P("fsdp"),
        P("fsdp"),
        P("fsdp", None),
        P("fsdp", None),
        P("fsdp", None),
    )
    return jax.shard_map(shards, mesh=mesh, in_specs=in_specs, out_specs=out_specs, check_vma=False)
```

```python
import functools

import jax
import jax.numpy as jnp
import numpy as np
from jax import lax
from jax.experimental import pallas as pl
from jax.experimental.layout import Layout, with_layout_constraint
from jax.experimental.pallas import tpu as pltpu
from jax.sharding import PartitionSpec as P

HQ = 25
HK = 5
HD = 64
EI = 3200
NS = 16
KC = 4
RDT = 100
META = 128
WIN = 1024
GAP = 8
STEP = 2048
LOG2E = 1.4426950408889634
NEG = -jnp.inf

EPS = 1e-05
HIGH = lax.Precision.HIGHEST
LANES = 128
CHUNK = 128
F32 = jnp.float32
MESH = pl.DeviceIdType.MESH


def fold_rows(first, second, level):
    bit = (lax.broadcasted_iota(jnp.int32, first.shape, 0) >> level) & 1
    upper = bit == 0
    return jnp.where(upper, first, second) + pltpu.roll(
        jnp.where(upper, second, first), 8 - (1 << level), 0
    )


def fold_in(stack, part):
    level = 0
    while stack and stack[-1][0] == level:
        part = fold_rows(stack.pop()[1], part, level)
        level += 1
    stack.append((level, part))


def fold_in_down(stack, part):
    level = 0
    while stack and stack[-1][0] == level:
        part = fold_rows(part, stack.pop()[1], level)
        level += 1
    stack.append((level, part))


def halves(part):
    return part[:8] + part[8:]


def scan_fwd_body(info, dt_ref, x_ref, b_ref, c_ref, a_ref, y_ref, first_ref, state):
    block, piece = pl.program_id(0), pl.program_id(1)
    tiles = a_ref.shape[1] // LANES
    keep = jnp.where(piece == 0, info[1 + block], 1).astype(F32)

    @pl.when((block == 0) & (piece == 0))
    def _():
        state[...] = jnp.zeros_like(state)

    first = state[...] * keep
    first_ref[0] = first
    a2 = a_ref[...] * LOG2E

    def cut(values, l):
        return values[:, l * LANES : (l + 1) * LANES]

    def group(g, carried):
        bt, ct, hs = carried
        stacks = [[] for _ in range(tiles)]
        hs = list(hs)
        for k in range(8):
            bk = jnp.broadcast_to(bt[:, k : k + 1], (NS, LANES))
            ck = jnp.broadcast_to(ct[:, k : k + 1], (NS, LANES))
            for l in range(tiles):
                lane = slice(l * LANES, (l + 1) * LANES)
                dtk = dt_ref[g, k : k + 1, lane]
                uk = dtk * x_ref[g, k : k + 1, lane]
                hs[l] = jnp.exp2(dtk * cut(a2, l)) * hs[l] + uk * bk
                fold_in(stacks[l], halves(hs[l] * ck))
        for l in range(tiles):
            y_ref[g, :, l * LANES : (l + 1) * LANES] = stacks[l][0][1]
        return pltpu.roll(bt, LANES - 8, 1), pltpu.roll(ct, LANES - 8, 1), tuple(hs)

    start = tuple(cut(first, l) for l in range(tiles))
    _, _, hs = lax.fori_loop(0, CHUNK // 8, group, (b_ref[...], c_ref[...], start))
    for l in range(tiles):
        state[:, l * LANES : (l + 1) * LANES] = hs[l]


def spread_lanes(bc_ref, wide, both):
    rows = lax.broadcasted_iota(jnp.int32, (NS, LANES), 0)
    lanes = lax.broadcasted_iota(jnp.int32, (NS, LANES), 1)
    own = (lanes % NS == rows) & (lanes < 4 * NS)

    def lay(g, _):
        for k in range(8):
            span = pl.ds(pl.multiple_of((g * 8 + k) * NS, NS), NS)
            wide[span, :] = jnp.where(own, bc_ref[g, k : k + 1, :], 0.0).astype(jnp.bfloat16)
        return 0

    lax.fori_loop(0, CHUNK // 8, lay, 0)
    source = lax.broadcasted_iota(jnp.int32, (LANES, 2 * LANES), 0)
    target = lax.broadcasted_iota(jnp.int32, (LANES, 2 * LANES), 1)
    ones = (source // (2 * NS) == target // LANES).astype(jnp.bfloat16)

    def multiply(i, _):
        span = pl.ds(pl.multiple_of(i * STEP, STEP), STEP)
        both[span, :] = jnp.dot(wide[span, :], ones, preferred_element_type=F32)
        return 0

    lax.fori_loop(0, CHUNK * NS // STEP, multiply, 0)


def scan_bwd_body(
    info, dt_ref, x_ref, bc_ref, gy_ref, a_ref, first_ref,
    gdt_ref, gx_ref, gb_ref, gc_ref, ga_ref, carry, states, decays, wide, both, lanes_c,
):
    turn, piece = pl.program_id(0), pl.program_id(1)
    n_blocks, pieces = pl.num_programs(0), pl.num_programs(1)
    tiles = a_ref.shape[1] // LANES
    after = jnp.minimum(n_blocks - turn, n_blocks - 1)
    keep = jnp.where(piece == 0, info[1 + after], 1).astype(F32)
    lanes_b = wide

    @pl.when((turn == 0) & (piece == 0))
    def _():
        carry[...] = jnp.zeros_like(carry)
        ga_ref[...] = jnp.zeros_like(ga_ref)

    def cut(values, l):
        return values[:, l * LANES : (l + 1) * LANES]

    spread_lanes(bc_ref, wide, both)
    a2 = a_ref[...] * LOG2E

    def again(g, hs):
        hs = list(hs)
        for k in range(8):
            span = pl.ds(pl.multiple_of((g * 8 + k) * NS, NS), NS)
            bk = both[span, :LANES]
            for l in range(tiles):
                lane = slice(l * LANES, (l + 1) * LANES)
                dtk = dt_ref[g, k : k + 1, lane]
                uk = dtk * x_ref[g, k : k + 1, lane]
                decay = jnp.exp2(dtk * cut(a2, l))
                hs[l] = decay * hs[l] + uk * bk
                decays[g * 8 + k, :, lane] = decay
                states[g * 8 + k + 1, :, lane] = hs[l]
        return tuple(hs)

    states[0] = first_ref[0]
    lax.fori_loop(0, CHUNK // 8, again, tuple(cut(first_ref[0], l) for l in range(tiles)))

    def group(turn_g, gs):
        g = CHUNK // 8 - 1 - turn_g
        gs = list(gs)
        logs, drives = [[] for _ in range(tiles)], [[] for _ in range(tiles)]
        sums = [None] * tiles
        for k in reversed(range(8)):
            t = g * 8 + k
            span = pl.ds(pl.multiple_of(t * NS, NS), NS)
            bk, ck = both[span, :LANES], both[span, LANES:]
            to_b = to_c = None
            for l in range(tiles):
                lane = slice(l * LANES, (l + 1) * LANES)
                gyk = gy_ref[g, k : k + 1, lane]
                dtk = dt_ref[g, k : k + 1, lane]
                uk = dtk * x_ref[g, k : k + 1, lane]
                grad = ck * gyk + gs[l]
                gs[l] = decays[t, :, lane] * grad
                log = gs[l] * states[t, :, lane]
                fold_in_down(logs[l], halves(log * cut(a_ref[...], l)))
                fold_in_down(drives[l], halves(grad * bk))
                part_b = grad * uk
                part_c = states[t + 1, :, lane] * gyk
                to_b = part_b if to_b is None else to_b + part_b
                to_c = part_c if to_c is None else to_c + part_c
                part_a = log * dtk
                sums[l] = part_a if sums[l] is None else sums[l] + part_a
            lanes_b[span, :] = to_b.astype(jnp.bfloat16)
            lanes_c[span, :] = to_c.astype(jnp.bfloat16)
        for l in range(tiles):
            lane = slice(l * LANES, (l + 1) * LANES)
            driven = drives[l][0][1]
            gdt_ref[g, :, lane] = logs[l][0][1] + driven * x_ref[g, :, lane]
            gx_ref[g, :, lane] = driven * dt_ref[g, :, lane]
            ga_ref[:, lane] += sums[l]
        return tuple(gs)

    held = tuple(carry[:, l * LANES : (l + 1) * LANES] * keep for l in range(tiles))
    gs = lax.fori_loop(0, CHUNK // 8, group, held)
    for l in range(tiles):
        carry[:, l * LANES : (l + 1) * LANES] = gs[l]

    lane_ids = lax.broadcasted_iota(jnp.int32, (NS, LANES), 1)
    ones = jnp.ones((LANES, LANES), jnp.bfloat16)

    def collect(i, carried):
        gbt, gct = carried
        span = pl.ds(pl.multiple_of(i * STEP, STEP), STEP)
        sum_b = jnp.dot(lanes_b[span, :], ones, preferred_element_type=F32)
        sum_c = jnp.dot(lanes_c[span, :], ones, preferred_element_type=F32)
        for k in range(STEP // NS):
            here = lane_ids == i * (STEP // NS) + k
            gbt = jnp.where(here, sum_b[k * NS : (k + 1) * NS], gbt)
            gct = jnp.where(here, sum_c[k * NS : (k + 1) * NS], gct)
        return gbt, gct

    zero = jnp.zeros((NS, LANES), F32)
    gbt, gct = lax.fori_loop(0, CHUNK * NS // STEP, collect, (zero, zero))
    gb_ref[...] = gbt
    gc_ref[...] = gct


def state_weights(b_t, c_t):
    parts = []
    for values in (b_t.T, c_t.T):
        high = lax.reduce_precision(values, 8, 7)
        parts += [high, values - high]
    return jnp.pad(jnp.concatenate(parts, 1), ((0, 0), (0, LANES - 4 * NS)))


def scan_fwd(info, dt, x, b_t, c_t, a_t, n_blocks):
    rows, width = dt.shape
    pieces = rows // n_blocks // CHUNK

    def at(i, j, info):
        return (i ^ info[0]) * pieces + j

    wide = pl.BlockSpec((CHUNK // 8, 8, width), lambda i, j, info: (at(i, j, info), 0, 0))
    tall = pl.BlockSpec((NS, CHUNK), lambda i, j, info: (0, at(i, j, info)))
    whole = pl.BlockSpec((NS, width), lambda i, j, info: (0, 0))
    dt, x = (v.reshape(-1, 8, width) for v in (dt, x))
    y, firsts = pl.pallas_call(
        scan_fwd_body,
        grid_spec=pltpu.PrefetchScalarGridSpec(
            num_scalar_prefetch=1,
            grid=(n_blocks, pieces),
            in_specs=[wide, wide, tall, tall, whole],
            out_specs=[
                wide,
                pl.BlockSpec((1, NS, width), lambda i, j, info: (i * pieces + j, 0, 0)),
            ],
            scratch_shapes=[pltpu.VMEM((NS, width), F32)],
        ),
        out_shape=[
            jax.ShapeDtypeStruct((rows // 8, 8, width), F32),
            jax.ShapeDtypeStruct((n_blocks * pieces, NS, width), F32),
        ],
        compiler_params=pltpu.CompilerParams(vmem_limit_bytes=32 * 2**20),
        cost_estimate=busy(36),
        name="scan_fwd",
    )(info, dt, x, b_t, c_t, a_t)
    return y.reshape(rows, width), firsts


def scan_bwd(info, dt, x, bc, gy, a_t, firsts, n_blocks):
    rows, width = dt.shape
    pieces = rows // n_blocks // CHUNK

    def at(i, j):
        return (n_blocks - 1 - i) * pieces + pieces - 1 - j

    wide = pl.BlockSpec((CHUNK // 8, 8, width), lambda i, j, info: (at(i, j), 0, 0))
    tall = pl.BlockSpec((CHUNK // 8, 8, LANES), lambda i, j, info: (at(i, j), 0, 0))
    turned = pl.BlockSpec((NS, CHUNK), lambda i, j, info: (0, at(i, j)))
    whole = pl.BlockSpec((NS, width), lambda i, j, info: (0, 0))
    first = pl.BlockSpec((1, NS, width), lambda i, j, info: (at(i, j), 0, 0))
    gdt, gx, gb, gc, ga = pl.pallas_call(
        scan_bwd_body,
        grid_spec=pltpu.PrefetchScalarGridSpec(
            num_scalar_prefetch=1,
            grid=(n_blocks, pieces),
            in_specs=[wide, wide, tall, wide, whole, first],
            out_specs=[wide, wide, turned, turned, whole],
            scratch_shapes=[
                pltpu.VMEM((NS, width), F32),
                pltpu.VMEM((CHUNK + 1, NS, width), F32),
                pltpu.VMEM((CHUNK, NS, width), F32),
                pltpu.VMEM((CHUNK * NS, LANES), jnp.bfloat16),
                pltpu.VMEM((CHUNK * NS, 2 * LANES), F32),
                pltpu.VMEM((CHUNK * NS, LANES), jnp.bfloat16),
            ],
        ),
        out_shape=[
            jax.ShapeDtypeStruct((rows // 8, 8, width), F32),
            jax.ShapeDtypeStruct((rows // 8, 8, width), F32),
            jax.ShapeDtypeStruct((NS, rows), F32),
            jax.ShapeDtypeStruct((NS, rows), F32),
            jax.ShapeDtypeStruct((NS, width), F32),
        ],
        compiler_params=pltpu.CompilerParams(vmem_limit_bytes=40 * 2**20),
        cost_estimate=busy(90),
        name="scan_bwd",
    )(
        info, dt.reshape(-1, 8, width), x.reshape(-1, 8, width), bc.reshape(-1, 8, LANES),
        gy.reshape(-1, 8, width), a_t, firsts,
    )
    return gdt.reshape(rows, width), gx.reshape(rows, width), gb, gc, ga


def conv_fwd_body(info, x_ref, taps_ref, bias_ref, out_ref, mixed_ref, padded, *, taps):
    block = pl.program_id(0)
    rows = x_ref.shape[0]
    keep = info[1 + block].astype(F32)

    @pl.when(block == 0)
    def _():
        padded[...] = jnp.zeros_like(padded)

    padded[0:8, :] = padded[rows : rows + 8, :] * keep
    padded[8 : rows + 8, :] = x_ref[...].astype(F32)
    total = bias_ref[...] + taps_ref[0:1, :] * padded[8 - taps + 1 : 8 - taps + 1 + rows, :]
    for i in range(1, taps):
        total += taps_ref[i : i + 1, :] * padded[8 - taps + 1 + i : 8 - taps + 1 + i + rows, :]
    out_ref[...] = total
    mixed_ref[...] = jax.nn.silu(total)


def conv_bwd_body(info, g_ref, x_ref, z_ref, taps_ref, gx_ref, gw_ref, gb_ref, padded, *, taps):
    turn = pl.program_id(0)
    n_blocks = pl.num_programs(0)
    rows = x_ref.shape[0]
    after = jnp.minimum(n_blocks - turn, n_blocks - 1)
    keep = info[1 + after].astype(F32)

    @pl.when(turn == 0)
    def _():
        padded[...] = jnp.zeros_like(padded)
        gw_ref[...] = jnp.zeros_like(gw_ref)
        gb_ref[...] = jnp.zeros_like(gb_ref)

    padded[rows : rows + 8, :] = padded[0:8, :] * keep
    padded[0:rows, :] = g_ref[...]
    x = x_ref[...].astype(F32)
    total = None
    for i in range(taps):
        moved = padded[taps - 1 - i : taps - 1 - i + rows, :]
        part = taps_ref[i : i + 1, :] * moved
        total = part if total is None else total + part
        gw_ref[i : i + 1, :] += jnp.sum(x * moved, 0, keepdims=True)
    width = x.shape[1]
    gx_ref[:, :width] = total.astype(gx_ref.dtype)
    gx_ref[:, width:] = z_ref[...]
    gb_ref[...] += jnp.sum(padded[0:rows, :], 0, keepdims=True)


def conv_fwd(info, x, taps_t, bias, n_blocks):
    rows, width = x.shape
    block = rows // n_blocks
    wide = pl.BlockSpec((block, width), lambda i, info: (i ^ info[0], 0))
    return pl.pallas_call(
        functools.partial(conv_fwd_body, taps=taps_t.shape[0]),
        grid_spec=pltpu.PrefetchScalarGridSpec(
            num_scalar_prefetch=1,
            grid=(n_blocks,),
            in_specs=[
                wide,
                pl.BlockSpec(taps_t.shape, lambda i, info: (0, 0)),
                pl.BlockSpec((1, width), lambda i, info: (0, 0)),
            ],
            out_specs=[wide, wide],
            scratch_shapes=[pltpu.VMEM((block + 8, width), F32)],
        ),
        out_shape=[jax.ShapeDtypeStruct((rows, width), F32)] * 2,
        compiler_params=pltpu.CompilerParams(vmem_limit_bytes=32 * 2**20),
        cost_estimate=busy(5),
        name="conv_fwd",
    )(info, x, taps_t, bias)


def conv_bwd(info, grad, x, grad_z, taps_t, n_blocks):
    rows, width = x.shape
    block = rows // n_blocks
    wide = pl.BlockSpec((block, width), lambda i, info: ((n_blocks - 1 - i) ^ info[0], 0))
    both = pl.BlockSpec((block, 2 * width), lambda i, info: ((n_blocks - 1 - i) ^ info[0], 0))
    taps_at = pl.BlockSpec(taps_t.shape, lambda i, info: (0, 0))
    one = pl.BlockSpec((1, width), lambda i, info: (0, 0))
    return pl.pallas_call(
        functools.partial(conv_bwd_body, taps=taps_t.shape[0]),
        grid_spec=pltpu.PrefetchScalarGridSpec(
            num_scalar_prefetch=1,
            grid=(n_blocks,),
            in_specs=[wide, wide, wide, taps_at],
            out_specs=[both, taps_at, one],
            scratch_shapes=[pltpu.VMEM((block + 8, width), F32)],
        ),
        out_shape=[
            jax.ShapeDtypeStruct((rows, 2 * width), jnp.bfloat16),
            jax.ShapeDtypeStruct(taps_t.shape, F32),
            jax.ShapeDtypeStruct((1, width), F32),
        ],
        compiler_params=pltpu.CompilerParams(vmem_limit_bytes=32 * 2**20),
        cost_estimate=busy(9),
        name="conv_bwd",
    )(info, grad, x, grad_z, taps_t)


def busy(us):
    return pl.CostEstimate(flops=int(us * 1.1e9), bytes_accessed=0, transcendentals=0)


def on_seq(index):
    return {"seq": index}


def masks_of(n):
    return [1 << bit for bit in range(n.bit_length() - 1)]


def greet_seq(n):
    here = lax.axis_index("seq")
    barrier = pltpu.get_barrier_semaphore()
    masks = masks_of(n)
    for mask in masks:
        pl.semaphore_signal(barrier, inc=1, device_id=on_seq(here ^ mask), device_id_type=MESH)
    return len(masks)


def send_to(source, target, sems, at, mask):
    send, recv = sems
    here = lax.axis_index("seq")
    return pltpu.make_async_remote_copy(
        src_ref=source,
        dst_ref=target,
        send_sem=send.at[at],
        recv_sem=recv.at[at],
        device_id=on_seq(here ^ mask),
        device_id_type=MESH,
    )


def crossed(rows, n):
    return n == 8 and rows >= 64


def gather_start(src, out, sems, n):
    here = lax.axis_index("seq")
    if not crossed(src.shape[0], n):
        copies = []

        def bit_step(bit):
            def run():
                if bit:
                    copies[-1].wait_recv()
                size = 1 << bit
                span = pl.ds((here >> bit) << bit, size)
                copy = send_to(out.at[span], out.at[span], sems, bit, size)
                copy.start()
                copies.append(copy)

            return run

        def last():
            copies[-1].wait_recv()
            for copy in copies:
                copy.wait_send()

        return [bit_step(bit) for bit in range(n.bit_length() - 1)] + [last]

    half = -(-src.shape[0] // 32) * 16
    low, high = pl.ds(0, half), pl.ds(half, src.shape[0] - half)
    own = out.at[here]
    to_2, to_4, to_1 = (
        send_to(src, own, sems, 0, 2),
        send_to(src, own, sems, 1, 4),
        send_to(src, own, sems, 2, 1),
    )
    for copy in (to_2, to_4, to_1):
        copy.start()
    from_2, from_4, from_6 = out.at[here ^ 2], out.at[here ^ 4], out.at[here ^ 6]
    on_4 = send_to(from_2.at[low], from_2.at[low], sems, 3, 4)
    on_2 = send_to(from_4.at[high], from_4.at[high], sems, 4, 2)
    core_2, core_4, core_6 = (
        send_to(block, block, sems, 5 + i, 1) for i, block in enumerate((from_2, from_4, from_6))
    )

    def second():
        to_2.wait_recv()
        on_4.start()
        core_2.start()
        to_4.wait_recv()
        on_2.start()
        core_4.start()

    def third():
        on_4.wait_recv()
        on_2.wait_recv()
        core_6.start()

    def last():
        for copy in (to_1, core_2, core_4, core_6):
            copy.wait_recv()
        for copy in (to_2, to_4, to_1, on_4, on_2, core_2, core_4, core_6):
            copy.wait_send()

    return [second, third, last]


def gather_body(src, out, local, send, recv, *, n):
    here = lax.axis_index("seq")
    own = pltpu.make_async_copy(src, out.at[here], local)
    own.start()
    count = greet_seq(n)
    pl.semaphore_wait(pltpu.get_barrier_semaphore(), count)
    cross = crossed(src.shape[0], n)
    if not cross:
        own.wait()
    for step in gather_start(src, out, (send, recv), n):
        step()
    if cross:
        own.wait()


def seq_gather(block, call):
    n = lax.axis_size("seq")
    return pl.pallas_call(
        functools.partial(gather_body, n=n),
        out_shape=jax.ShapeDtypeStruct((n,) + block.shape, block.dtype),
        in_specs=[pl.BlockSpec(memory_space=pl.ANY)],
        out_specs=pl.BlockSpec(memory_space=pl.ANY),
        scratch_shapes=[
            pltpu.SemaphoreType.DMA(()),
            pltpu.SemaphoreType.DMA((8,)),
            pltpu.SemaphoreType.DMA((8,)),
        ],
        compiler_params=pltpu.CompilerParams(collective_id=call, has_side_effects=True),
        cost_estimate=busy(35),
        name="seq_gather",
    )(block)


def add_rows(out, one, two, start, size, step=16):
    def turn(i, _):
        rows = pl.ds(pl.multiple_of(start + i * step, step), step)
        out[rows, :] = (one[rows, :].astype(F32) + two[rows, :].astype(F32)).astype(out.dtype)
        return 0

    lax.fori_loop(0, size // step, turn, 0)


def reduce_steps(blocks, out, came, sums, ends, sems, n, at=0):
    here = lax.axis_index("seq")
    tokens = blocks.shape[1]
    if n != 8:
        held = blocks
        for k, bit in enumerate(reversed(range(n.bit_length() - 1))):
            size = 1 << bit
            first = (here >> bit) & 1
            other = pl.ds((1 - first) * size, size)
            copy = send_to(held.at[other], came.at[pl.ds(size, size)], sems, at + k, size)
            copy.start()
            copy.wait()
            for j in range(size):
                add_rows(
                    sums.at[size + j], held.at[first * size + j], came.at[size + j], 0, tokens
                )
            held = sums.at[pl.ds(size, size)]
        total = sums.at[1]

        def turn(i, _):
            rows = pl.ds(pl.multiple_of(i * 16, 16), 16)
            out[rows, :] = total[rows, :].astype(out.dtype)
            return 0

        lax.fori_loop(0, tokens // 16, turn, 0)
        return
    half = tokens // 2
    low, high = pl.ds(0, half), pl.ds(half, half)
    step = 16 if half % 16 == 0 else 8
    core = [
        send_to(blocks.at[here ^ (mask | 1)], came.at[i], sems, at + i, 1)
        for i, mask in enumerate((6, 2, 4, 0))
    ]
    for copy in core:
        copy.start()
    by_6, by_2, by_4 = (sums.at[i] for i in range(3))
    end_2, end_4, mid_2, mid_4 = ends.at[0], ends.at[1], ends.at[2], ends.at[3]
    dia_2 = send_to(by_6.at[low], mid_4.at[low], sems, at + 4, 2)
    dia_4 = send_to(by_6.at[high], mid_2.at[high], sems, at + 5, 4)
    x_low = send_to(by_2.at[low], end_2.at[low], sems, at + 6, 2)
    y_high = send_to(by_4.at[high], end_4.at[high], sems, at + 7, 4)
    x_high = send_to(by_2.at[high], end_2.at[high], sems, at + 8, 2)
    y_low = send_to(by_4.at[low], end_4.at[low], sems, at + 9, 4)
    core[0].wait_recv()
    add_rows(by_6, blocks.at[here ^ 6], came.at[0], 0, tokens, step)
    dia_2.start()
    dia_4.start()
    core[1].wait_recv()
    add_rows(by_2, blocks.at[here ^ 2], came.at[1], 0, tokens, step)
    x_low.start()
    core[2].wait_recv()
    add_rows(by_4, blocks.at[here ^ 4], came.at[2], 0, tokens, step)
    y_high.start()
    dia_4.wait_recv()
    add_rows(by_2, by_2, mid_2, half, half, step)
    x_high.start()
    dia_2.wait_recv()
    add_rows(by_4, by_4, mid_4, 0, half, step)
    y_low.start()
    core[3].wait_recv()
    add_rows(out, blocks.at[here], came.at[3], 0, tokens, step)
    x_low.wait_recv()
    x_high.wait_recv()
    add_rows(out, out, end_2, 0, tokens, step)
    y_high.wait_recv()
    y_low.wait_recv()
    add_rows(out, out, end_4, 0, tokens, step)
    for copy in core + [dia_2, dia_4, x_low, y_high, x_high, y_low]:
        copy.wait_send()


def reduce_body(blocks, out, came, sums, ends, send, recv, *, n):
    count = greet_seq(n)
    pl.semaphore_wait(pltpu.get_barrier_semaphore(), count)
    reduce_steps(blocks, out, came, sums, ends, (send, recv), n)


def reduce_scratch(n, rows, width, dtype):
    if n != 8:
        return [pltpu.VMEM((n, rows, width), dtype)] * 2 + [pltpu.VMEM((1, 8, 128), dtype)]
    return [
        pltpu.VMEM((4, rows, width), dtype),
        pltpu.VMEM((3, rows, width), dtype),
        pltpu.VMEM((4, rows, width), dtype),
    ]


def seq_reduce(blocks, call):
    n, rows, width = blocks.shape
    return pl.pallas_call(
        functools.partial(reduce_body, n=n),
        out_shape=jax.ShapeDtypeStruct((rows, width), F32),
        in_specs=[pl.BlockSpec(memory_space=pltpu.VMEM)],
        out_specs=pl.BlockSpec(memory_space=pltpu.VMEM),
        scratch_shapes=reduce_scratch(n, rows, width, blocks.dtype)
        + [pltpu.SemaphoreType.DMA((10,)), pltpu.SemaphoreType.DMA((10,))],
        compiler_params=pltpu.CompilerParams(
            collective_id=call, has_side_effects=True, vmem_limit_bytes=56 * 2**20
        ),
        cost_estimate=busy(blocks.size / 8e4),
        name="seq_reduce",
    )(blocks)


def total_body(blocks, out, total, came, sums, ends, send, recv, local, *, n):
    here = lax.axis_index("seq")
    count = greet_seq(n)
    pl.semaphore_wait(pltpu.get_barrier_semaphore(), count)
    reduce_steps(blocks, total, came, sums, ends, (send, recv), n)
    own = pltpu.make_async_copy(total, out.at[here], local)
    own.start()
    cross = crossed(total.shape[0], n)
    if not cross:
        own.wait()
    for step in gather_start(total, out, (send.at[pl.ds(10, 8)], recv.at[pl.ds(10, 8)]), n):
        step()
    if cross:
        own.wait()


def seq_total(blocks, call):
    n, rows, width = blocks.shape
    return pl.pallas_call(
        functools.partial(total_body, n=n),
        out_shape=jax.ShapeDtypeStruct(blocks.shape, F32),
        in_specs=[pl.BlockSpec(memory_space=pltpu.VMEM)],
        out_specs=pl.BlockSpec(memory_space=pltpu.VMEM),
        scratch_shapes=[pltpu.VMEM((rows, width), F32)]
        + reduce_scratch(n, rows, width, F32)
        + [
            pltpu.SemaphoreType.DMA((18,)),
            pltpu.SemaphoreType.DMA((18,)),
            pltpu.SemaphoreType.DMA(()),
        ],
        compiler_params=pltpu.CompilerParams(
            collective_id=call, has_side_effects=True, vmem_limit_bytes=40 * 2**20
        ),
        cost_estimate=busy(20),
        name="seq_total",
    )(blocks)


def line_steps(srcs, outs, send, recv, depth):
    here = lax.axis_index("fsdp")

    def passed(a, k, side):
        shard = here - (k - 1) if side == 0 else here + (k - 1)
        shard = jnp.clip(shard, 0, depth - 1)
        target = here + 1 if side == 0 else here - 1
        target = jnp.clip(target, 0, depth - 1)
        block = outs[a].at[shard]
        return pltpu.make_async_remote_copy(
            src_ref=srcs[a] if k == 1 else block,
            dst_ref=block,
            send_sem=send.at[a, side, k - 1],
            recv_sem=recv.at[a, side, k - 1],
            device_id={"fsdp": target},
            device_id_type=MESH,
        )

    def sends(k, side):
        if side == 0:
            return (here >= k - 1) & (here < depth - 1)
        return (here <= depth - k) & (here > 0)

    def gets(k, side):
        return here >= k if side == 0 else here <= depth - 1 - k

    def arrived(k):
        for side in range(2):

            @pl.when(gets(k, side))
            def _():
                for a in range(len(srcs)):
                    passed(a, k, side).wait_recv()

    def step(k):
        def run():
            if k > 1:
                arrived(k - 1)
            for side in range(2):

                @pl.when(sends(k, side))
                def _():
                    for a in range(len(srcs)):
                        passed(a, k, side).start()

        return run

    def last():
        arrived(depth - 1)
        for k in range(1, depth):
            for side in range(2):

                @pl.when(sends(k, side))
                def _():
                    for a in range(len(srcs)):
                        passed(a, k, side).wait_send()

    return [step(k) for k in range(1, depth)] + [last]


def first_body(*refs, n, depth, blocks, lines):
    srcs, refs = refs[: blocks + lines], refs[blocks + lines :]
    outs = refs[: blocks + lines]
    local, send, recv, line_send, line_recv = refs[blocks + lines :]
    here, level = lax.axis_index("seq"), lax.axis_index("fsdp")
    owns = []
    for a in range(blocks + lines):
        place = outs[a].at[here if a < blocks else level]
        owns.append(pltpu.make_async_copy(srcs[a], place, local.at[a]))
        owns[-1].start()
    count = greet_seq(n)
    barrier = pltpu.get_barrier_semaphore()
    for ready, other in ((level > 0, level - 1), (level < depth - 1, level + 1)):

        @pl.when(ready)
        def _():
            pl.semaphore_signal(
                barrier, inc=1, device_id={"fsdp": jnp.clip(other, 0, depth - 1)}, device_id_type=MESH
            )

    count = count + (level > 0).astype(jnp.int32) + (level < depth - 1).astype(jnp.int32)
    pl.semaphore_wait(barrier, count)
    cross = crossed(srcs[0].shape[0], n)
    if not cross:
        for own in owns[:blocks]:
            own.wait()
    line = line_steps(srcs[blocks:], outs[blocks:], line_send, line_recv, depth)
    line.pop(0)()
    turns = []
    for a in range(blocks):
        along = gather_start(srcs[a], outs[a], (send.at[a], recv.at[a]), n)
        turns += [(2 * i + 2 * a, step) for i, step in enumerate(along)]
    turns += [(2 * i + 0.5, step) for i, step in enumerate(line)]
    for _, step in sorted(turns, key=lambda turn: turn[0]):
        step()
    if cross:
        for own in owns[:blocks]:
            own.wait()
    for own in owns[blocks:]:
        own.wait()


def first_gather(blocks, arrays, call):
    n, depth = lax.axis_size("seq"), lax.axis_size("fsdp")
    count, lines = len(blocks), len(arrays)
    anywhere = pl.BlockSpec(memory_space=pl.ANY)
    return pl.pallas_call(
        functools.partial(first_body, n=n, depth=depth, blocks=count, lines=lines),
        out_shape=[jax.ShapeDtypeStruct((n,) + block.shape, block.dtype) for block in blocks]
        + [jax.ShapeDtypeStruct((depth,) + array.shape, array.dtype) for array in arrays],
        in_specs=[anywhere] * (count + lines),
        out_specs=[anywhere] * (count + lines),
        scratch_shapes=[
            pltpu.SemaphoreType.DMA((count + lines,)),
            pltpu.SemaphoreType.DMA((count, 8)),
            pltpu.SemaphoreType.DMA((count, 8)),
            pltpu.SemaphoreType.DMA((lines, 2, depth - 1)),
            pltpu.SemaphoreType.DMA((lines, 2, depth - 1)),
        ],
        compiler_params=pltpu.CompilerParams(collective_id=call, has_side_effects=True),
        cost_estimate=busy(60),
        name="first_gather",
    )(*blocks, *arrays)


def last_body(*refs, n, count):
    srcs, outs = refs[:count], refs[count : 2 * count]
    local, send, recv = refs[2 * count :]
    here = lax.axis_index("seq")
    owns = [pltpu.make_async_copy(srcs[a], outs[a].at[here], local.at[a]) for a in range(count)]
    for own in owns:
        own.start()
    peers = greet_seq(n)
    pl.semaphore_wait(pltpu.get_barrier_semaphore(), peers)
    cross = [crossed(src.shape[0], n) for src in srcs]
    for a in range(count):
        if not cross[a]:
            owns[a].wait()
    steps = [gather_start(srcs[a], outs[a], (send.at[a], recv.at[a]), n) for a in range(count)]
    for i in range(max(len(part) for part in steps)):
        for part in steps:
            if i < len(part):
                part[i]()
    for a in range(count):
        if cross[a]:
            owns[a].wait()


def last_gather(arrays, call):
    n = lax.axis_size("seq")
    count = len(arrays)
    anywhere = pl.BlockSpec(memory_space=pl.ANY)
    return pl.pallas_call(
        functools.partial(last_body, n=n, count=count),
        out_shape=[jax.ShapeDtypeStruct((n,) + array.shape, array.dtype) for array in arrays],
        in_specs=[anywhere] * count,
        out_specs=[anywhere] * count,
        scratch_shapes=[
            pltpu.SemaphoreType.DMA((count,)),
            pltpu.SemaphoreType.DMA((count, 8)),
            pltpu.SemaphoreType.DMA((count, 8)),
        ],
        compiler_params=pltpu.CompilerParams(collective_id=call, has_side_effects=True),
        cost_estimate=busy(60),
        name="last_gather",
    )(*arrays)


def lay_cols_body(*refs, n, depth, groups, chunk, padded, total, front):
    out = refs[-1]
    if front:
        out[:, :front] = refs[0][:, :front].astype(F32)
    parts = refs[len(refs) - 1 - groups : -1]
    for g, part in enumerate(parts):
        for s in range(n):
            values = part[s].astype(F32)
            for j in range(depth):
                at = front + g * total + j * (total // depth) + s * chunk
                out[:, at : at + chunk] = values[:, j * padded : j * padded + chunk]


def lay_cols(parts, chunk, padded, total, first=None, front=0):
    n, rows, _ = parts[0][0].shape
    depth = total // (n * chunk)
    width = depth * padded
    turns = 1 if rows % 40 else 5
    step = rows // turns
    ins = [] if first is None else [first]
    specs = [] if first is None else [pl.BlockSpec((step, first.shape[1]), lambda i: (i, 0))]
    for _, block in parts:
        specs.append(pl.BlockSpec((n, step, width), lambda i, block=block: (0, i, block)))
    return pl.pallas_call(
        functools.partial(
            lay_cols_body, n=n, depth=depth, groups=len(parts), chunk=chunk, padded=padded,
            total=total, front=front,
        ),
        grid=(turns,),
        out_shape=jax.ShapeDtypeStruct((rows, front + len(parts) * total), F32),
        in_specs=specs,
        out_specs=pl.BlockSpec((step, front + len(parts) * total), lambda i: (i, 0)),
        compiler_params=pltpu.CompilerParams(vmem_limit_bytes=48 * 2**20),
        cost_estimate=busy(8),
        name="lay_cols",
    )(*ins, *(array for array, _ in parts))


def lay_rows_body(parts, out, *, n, chunk):
    for s in range(n):
        out[s * chunk : (s + 1) * chunk, :] = parts[s, :chunk, :].astype(F32)


def lay_rows(parts, chunk):
    n, _, width = parts.shape
    return pl.pallas_call(
        functools.partial(lay_rows_body, n=n, chunk=chunk),
        out_shape=jax.ShapeDtypeStruct((n * chunk, width), F32),
        in_specs=[pl.BlockSpec(memory_space=pltpu.VMEM)],
        out_specs=pl.BlockSpec(memory_space=pltpu.VMEM),
        compiler_params=pltpu.CompilerParams(vmem_limit_bytes=48 * 2**20),
        cost_estimate=busy(4),
        name="lay_rows",
    )(parts)


def lay_rows_turned_body(parts, out, *, n, chunk):
    for s in range(n):
        out[:, s * chunk : (s + 1) * chunk] = parts[s].astype(F32).T[:, :chunk]


def lay_rows_turned(parts, chunk):
    n, padded, width = parts.shape
    return pl.pallas_call(
        functools.partial(lay_rows_turned_body, n=n, chunk=chunk),
        grid=(-(-width // LANES),),
        in_specs=[pl.BlockSpec((n, padded, LANES), lambda i: (0, 0, i))],
        out_specs=pl.BlockSpec((LANES, n * chunk), lambda i: (i, 0)),
        out_shape=jax.ShapeDtypeStruct((width, n * chunk), F32),
        compiler_params=pltpu.CompilerParams(vmem_limit_bytes=48 * 2**20),
        cost_estimate=busy(8),
        name="lay_rows_turned",
    )(parts)


def key_scores(k, q, allowed):
    scores = lax.dot_general(k, q, (((0,), (0,)), ((), ())), preferred_element_type=F32)
    return scores if allowed is None else jnp.where(allowed, scores, NEG)


def block_masks(position, back, rows):
    key = lax.broadcasted_iota(jnp.int32, (rows, rows), 0)
    query = lax.broadcasted_iota(jnp.int32, (rows, rows), 1)
    masks = []
    for distance in range(back, 0, -1):
        reached = jnp.broadcast_to(position >= distance, (rows, rows))
        masks.append((key > query) & reached if distance == back else reached)
    return masks + [key <= query]


def attend_body(info, q_ref, *refs, back):
    keys, values = refs[: back + 2], refs[back + 2 : 2 * back + 4]
    out_ref, norm_ref = refs[2 * back + 4 :]
    q = q_ref[...]
    masks = [None] + block_masks(info[1], back, q.shape[1])
    scores = [key_scores(k[...], q, mask) for k, mask in zip(keys, masks)]
    top = functools.reduce(jnp.maximum, (jnp.max(part, 0, keepdims=True) for part in scores))
    total = jnp.zeros_like(top)
    out = jnp.zeros(q.shape, F32)
    for part, v in zip(scores, values):
        weights = jnp.exp(part - top)
        total += jnp.sum(weights, 0, keepdims=True)
        out += jnp.dot(v[...], weights.astype(jnp.bfloat16), preferred_element_type=F32)
    out_ref[...] = out / total
    norm_ref[0] = jnp.broadcast_to(top + jnp.log(total), norm_ref.shape[1:])


def attend_back_body(info, q_ref, grad_ref, out_ref, norm_ref, *refs, back):
    count = back + 2
    keys, values = refs[:count], refs[count : 2 * count]
    gq_ref, gk_meta, gv_meta, gk_ref, gv_ref = refs[2 * count :]
    turn = pl.program_id(1)
    q, grad = q_ref[...], grad_ref[...]
    norm = norm_ref[0][0:1]
    shared = jnp.sum(grad.astype(F32) * out_ref[...], 0, keepdims=True)
    masks = [None] + block_masks(info[1], back, q.shape[1])

    @pl.when(turn == 0)
    def _():
        for ref in (gk_meta, gv_meta, gk_ref, gv_ref):
            ref[...] = jnp.zeros_like(ref)

    contract = (((1,), (1,)), ((), ()))
    gq = jnp.zeros(q.shape, F32)
    for i in range(count):
        k, v = keys[i][...], values[i][...]
        weights = jnp.exp(key_scores(k, q, masks[i]) - norm)
        grad_weights = lax.dot_general(
            v, grad, (((0,), (0,)), ((), ())), preferred_element_type=F32
        )
        grad_scores = (weights * (grad_weights - shared)).astype(jnp.bfloat16)
        gq += jnp.dot(k, grad_scores, preferred_element_type=F32)
        gk = lax.dot_general(q, grad_scores, contract, preferred_element_type=F32)
        gv = lax.dot_general(
            grad, weights.astype(jnp.bfloat16), contract, preferred_element_type=F32
        )
        if i == 0:
            gk_meta[...] += gk
            gv_meta[...] += gv
        else:
            gk_ref[i - 1] += gk
            gv_ref[i - 1] += gv
    gq_ref[...] = gq * HD ** (-0.5)


def attend_specs(heads, groups, tokens, meta, n, back):
    size = heads // groups
    head = pl.BlockSpec((HD, tokens), lambda g, j, info: (g * size + j, 0))

    def sides(first):
        specs = [pl.BlockSpec((HD, meta), lambda g, j, info: (first + g, 0))]
        for distance in range(back, -1, -1):
            specs.append(
                pl.BlockSpec(
                    (HD, tokens),
                    lambda g, j, info, distance=distance: (
                        first + g, lax.rem(info[0] - distance + n, n),
                    ),
                )
            )
        return specs

    norm = pl.BlockSpec((1, 8, tokens), lambda g, j, info: (g * size + j, 0, 0))
    return head, sides(0) + sides(groups), norm


def attend(info, q_t, kv_t, meta_t, heads, groups, n, back):
    tokens, meta = q_t.shape[1], meta_t.shape[1]
    head, kv, norm = attend_specs(heads, groups, tokens, meta, n, back)
    return pl.pallas_call(
        functools.partial(attend_body, back=back),
        grid_spec=pltpu.PrefetchScalarGridSpec(
            num_scalar_prefetch=1,
            grid=(groups, heads // groups),
            in_specs=[head] + kv,
            out_specs=[head, norm],
        ),
        out_shape=[
            jax.ShapeDtypeStruct(q_t.shape, F32),
            jax.ShapeDtypeStruct((heads, 8, tokens), F32),
        ],
        compiler_params=pltpu.CompilerParams(vmem_limit_bytes=40 * 2**20),
        cost_estimate=busy(25),
        name="attend",
    )(info, q_t, *(([meta_t] + [kv_t] * (back + 1)) * 2))


def attend_back(info, q_t, grad_t, out_t, norms, kv_t, meta_t, heads, groups, n, back):
    tokens, meta = q_t.shape[1], meta_t.shape[1]
    head, kv, norm = attend_specs(heads, groups, tokens, meta, n, back)
    cols = groups * HD
    window = pl.BlockSpec((back + 1, HD, tokens), lambda g, j, info: (0, g, 0))
    side = pl.BlockSpec((HD, meta), lambda g, j, info: (g, 0))
    return pl.pallas_call(
        functools.partial(attend_back_body, back=back),
        grid_spec=pltpu.PrefetchScalarGridSpec(
            num_scalar_prefetch=1,
            grid=(groups, heads // groups),
            in_specs=[head, head, head, norm] + kv,
            out_specs=[head, side, side, window, window],
        ),
        out_shape=[
            jax.ShapeDtypeStruct(q_t.shape, F32),
            jax.ShapeDtypeStruct((cols, meta), F32),
            jax.ShapeDtypeStruct((cols, meta), F32),
            jax.ShapeDtypeStruct((back + 1, cols, tokens), F32),
            jax.ShapeDtypeStruct((back + 1, cols, tokens), F32),
        ],
        compiler_params=pltpu.CompilerParams(vmem_limit_bytes=48 * 2**20),
        cost_estimate=busy(50),
        name="attend_back",
    )(info, q_t, grad_t, out_t, norms, *(([meta_t] + [kv_t] * (back + 1)) * 2))


def turned_sum(blocks):
    n = lax.axis_size("fsdp")
    here = lax.axis_index("fsdp")
    total = lax.dynamic_index_in_dim(blocks, here, 0, False).astype(F32)
    for k in range(1, n):
        part = lax.dynamic_index_in_dim(blocks, (here + k) % n, 0, False)
        total = total + lax.ppermute(part, "fsdp", [(i, (i + k) % n) for i in range(n)]).astype(F32)
    return total


def in_rows(values):
    return with_layout_constraint(values, Layout(major_to_minor=(0, 1)))


def pad_to(values, size, axis):
    widths = [(0, 0)] * values.ndim
    widths[axis] = (0, size - values.shape[axis])
    return jnp.pad(values, widths)


def norm_fwd(values, gains):
    inverse = lax.rsqrt(jnp.mean(values * values, -1, keepdims=True) + EPS)
    return (values * inverse * gains, inverse)


def norm_back(values, inverse, gains, grads):
    weighted = grads * gains
    mean_term = jnp.mean(values * weighted, -1, keepdims=True)
    return (
        inverse * weighted - values * inverse**3 * mean_term,
        jnp.sum(grads * values * inverse, 0),
    )


def silu_slope(values):
    sigmoid = jax.nn.sigmoid(values)
    return sigmoid * (1.0 + values * (1.0 - sigmoid))


def product(one, two, dims, exact=False, out=F32):
    return lax.dot_general(
        one,
        two,
        ((dims[:1], dims[1:]), ((), ())),
        preferred_element_type=F32,
        precision=lax.Precision.HIGH if exact else None,
    ).astype(out)


def shards(
    inputs, starts, norm_gain, in_weight, conv_weight, conv_bias, xproj_weight, dtproj_weight, dt_bias,
    log_decay, skip_gain, meta_tokens, attn_weight, mamba_weight, attn_gain, mamba_gain, ffn_gain,
    gate_weight, up_weight, down_weight, cotangent,
):
    low = jnp.bfloat16
    n, depth = lax.axis_size("seq"), lax.axis_size("fsdp")
    here = lax.axis_index("seq")
    tokens, width = inputs.shape[1:]
    rows = n * tokens
    q_cols, kv_cols = HQ * HD, HK * HD
    qkv_cols = q_cols + 2 * kv_cols
    group_size = HQ // HK
    inner = EI // n
    hidden_units = gate_weight.shape[1]
    units = hidden_units // n
    shard_rows = width // depth

    if n <= GAP:
        carries = jnp.array([0] + [1] * (n - 1), jnp.int32)
        position = here
    else:
        flags = lax.all_gather(starts[0, 0], "seq")
        carries = 1 - flags
        blocks = jnp.arange(n)
        position = here - jnp.max(jnp.where((flags == 1) & (blocks <= here), blocks, 0))
    info = jnp.concatenate([jnp.zeros((1,), jnp.int32), carries])

    def up_to(size, step):
        return -(-size // step) * step

    chunk, unit_chunk = inner // depth, units // depth
    inner_pad = up_to(depth * up_to(chunk, 16), LANES)
    units_pad = up_to(depth * up_to(unit_chunk, 16), LANES)
    chunk_pad, unit_pad = inner_pad // depth, units_pad // depth

    def own_cols(weight, base, total, padded, here=here):
        size = total // (depth * n)
        parts = [
            pad_to(
                lax.dynamic_slice_in_dim(weight, base + j * (total // depth) + here * size, size, 1),
                padded,
                1,
            )
            for j in range(depth)
        ]
        return jnp.concatenate(parts, 1)

    def own_rows(weight, padded, here=here):
        size = weight.shape[0] // n
        return pad_to(lax.dynamic_slice_in_dim(weight, here * size, size, 0), padded, 0)

    def along_depth(values):
        return lax.all_gather(values, "fsdp")

    small = jnp.concatenate(
        [
            conv_weight.T, conv_bias[None], xproj_weight.T, dtproj_weight.T, dt_bias[None], log_decay.T,
            skip_gain[None],
        ],
        0,
    )
    small_rows = up_to(small.shape[0], 16)
    small = pad_to(lax.dynamic_slice_in_dim(small, here * chunk, chunk, 1), chunk_pad, 1)
    own_in = own_cols(in_weight, qkv_cols, EI, chunk_pad)
    own_z = own_cols(in_weight, qkv_cols + EI, EI, chunk_pad)
    gains = pad_to(jnp.stack([norm_gain, attn_gain, mamba_gain, ffn_gain], 0), 16, 0)
    hidden_all, grad_out_all, w_in, small_full, gain_rows, meta_rows = first_gather(
        [inputs[0], cotangent[0]],
        [jnp.concatenate([own_in, own_z], 1), pad_to(small, small_rows, 0), gains, meta_tokens],
        1,
    )
    w_in = w_in.reshape(width, 2 * inner_pad)
    gain_norm, gain_attn, gain_mamba, gain_ffn = (
        gain_rows[:, i].reshape(-1).astype(F32) for i in range(4)
    )

    small_full, later = lax.optimization_barrier((small_full, here))
    small_full = small_full.transpose(1, 0, 2).reshape(small_rows, inner_pad).astype(F32)
    ends = np.cumsum([0, KC, 1, RDT + 2 * NS, RDT, 1, NS, 1])
    taps_t, bias, select_t, steps_t, b_steps, a_logs, skip = (
        small_full[a:b] for a, b in zip(ends[:-1], ends[1:])
    )
    a_t = -jnp.exp(a_logs)

    piece = up_to(-(-shard_rows // n), 8)

    def attn_piece(weight, cols):
        first = jnp.minimum(later * piece, shard_rows - piece)
        part = lax.dynamic_slice(weight, (first, 0), (piece, cols))
        return lax.dynamic_slice_in_dim(pad_to(part, 2 * piece, 0), later * piece - first, piece, 0)

    own_attn = along_depth(
        jnp.concatenate([attn_piece(in_weight, qkv_cols), attn_piece(attn_weight, width)], 1)
    )
    w_mamba = along_depth(own_rows(mamba_weight, chunk_pad, later)).reshape(inner_pad, width)
    meta_rows = meta_rows.reshape(META, width)

    hidden = inputs[0].astype(F32)
    normed_all, _ = norm_fwd(hidden_all.astype(F32), gain_norm)
    normed_all = normed_all.astype(low).reshape(rows, width)
    normed, inv_in = norm_fwd(hidden, gain_norm)
    normed = normed.astype(low)
    mixer_in = product(normed_all, w_in[:, :inner_pad], (1, 0), out=low)
    z_gate = product(normed_all, w_in[:, inner_pad:], (1, 0), out=low).astype(F32)
    conv_pre, mixed = conv_fwd(info, mixer_in, taps_t, bias, n)

    def all_sum(values, call):
        laid = values.reshape(values.shape[0], n, tokens).transpose(1, 0, 2)
        laid = pad_to(laid, up_to(values.shape[0], 16), 1)
        total = seq_total(laid, call)
        return total.transpose(1, 0, 2).reshape(-1, rows)[: values.shape[0]]

    part = product(select_t, mixed, (1, 1), exact=True)
    selected = all_sum(part, 2)
    selected, own_attn = lax.optimization_barrier((selected, own_attn))
    all_attn = lax.all_gather(own_attn, "seq").transpose(1, 0, 2, 3)
    all_attn = all_attn.reshape(depth, n * piece, -1)[:, :shard_rows].reshape(width, -1)
    w_qkv, w_attn = all_attn[:, :qkv_cols], all_attn[:, qkv_cols:]
    w_q, w_kv = w_qkv[:, :q_cols], w_qkv[:, q_cols:]
    ranks, b_sel, c_sel = selected[:RDT], selected[RDT : RDT + NS], selected[RDT + NS :]
    dt_pre = product(ranks, steps_t, (0, 0), exact=True) + b_steps
    steps = jax.nn.softplus(dt_pre)
    steps, last = lax.optimization_barrier((steps, later))
    y_scan, firsts = scan_fwd(info, steps, mixed, b_sel, c_sel, a_t, n)
    w_units = along_depth(
        jnp.concatenate(
            [
                own_cols(gate_weight, 0, hidden_units, unit_pad, last),
                own_cols(up_weight, 0, hidden_units, unit_pad, last),
            ],
            1,
        )
    ).reshape(width, 2 * units_pad)
    w_down = along_depth(own_rows(down_weight, unit_pad, last)).reshape(units_pad, width)
    grad_out_all = grad_out_all.reshape(rows, width)
    y_full = y_scan + skip * mixed
    silu_z = jax.nn.silu(z_gate)
    mamba_low = (y_full * silu_z).astype(low)
    mamba_out = seq_reduce(
        in_rows(product(mamba_low, w_mamba, (1, 0), out=low)).reshape(n, tokens, width), 3
    )

    blocks_back = WIN // tokens
    attend_at = jnp.stack([here, position]).astype(jnp.int32)
    heads = (HQ, HK, n, blocks_back)
    queries = product(w_q, normed, (0, 1), out=low) * HD ** (-0.5)
    keyvals = product(w_kv, normed_all, (0, 1), out=low)
    meta_float = meta_rows.astype(F32)
    meta_normed, meta_inv = norm_fwd(meta_float, gain_norm)
    meta_low = meta_normed.astype(low)
    meta_kv = product(w_kv, meta_low, (0, 1), out=low)
    contexts, log_norms = attend(attend_at, queries, keyvals, meta_kv, *heads)
    attended = contexts.astype(low)
    attn_out = product(attended, w_attn, (0, 0))

    attn_normed, attn_inv = norm_fwd(attn_out, gain_attn)
    mamba_normed, mamba_inv = norm_fwd(mamba_out, gain_mamba)
    middle = hidden + 0.5 * (attn_normed + mamba_normed)
    ffn_normed, ffn_inv = norm_fwd(middle, gain_ffn)
    ffn_all = seq_gather(ffn_normed.astype(low), 4).reshape(rows, width)
    both_pre = product(ffn_all, w_units, (1, 0))
    gate_pre, up_pre = both_pre[:, :units_pad], both_pre[:, units_pad:]
    grad_act = product(grad_out_all, w_down, (1, 1))
    silu_gate = jax.nn.silu(gate_pre)
    activated = (silu_gate * up_pre).astype(low)
    grad_units = jnp.concatenate(
        [
            (grad_act * up_pre * silu_slope(gate_pre)).astype(low),
            (grad_act * silu_gate).astype(low),
        ],
        1,
    )
    grad_ffn_part = in_rows(product(grad_units, w_units, (1, 1), out=low))
    down_part = product(activated, w_down, (1, 0), out=low)
    grad_w_units = product(ffn_all, grad_units, (0, 0), out=low)
    grad_w_down = in_rows(product(activated, grad_out_all, (0, 0), out=low))
    grad_ffn_part, grad_w_units, grad_w_down, down_part = lax.optimization_barrier(
        (grad_ffn_part, grad_w_units, grad_w_down, down_part)
    )
    grad_ffn_in = seq_reduce(grad_ffn_part.reshape(n, tokens, width), 5)

    def depth_sum(part):
        return lax.psum_scatter(part, "fsdp", scatter_dimension=0, tiled=True)

    own_w_units, own_w_down = depth_sum(grad_w_units), depth_sum(grad_w_down)
    down_sum = lax.psum_scatter(down_part, "seq", scatter_dimension=0, tiled=True)

    grad_out = cotangent[0].astype(F32)
    grad_mid_norm, grad_g_ffn = norm_back(middle, ffn_inv, gain_ffn, grad_ffn_in)
    grad_middle = grad_out + grad_mid_norm
    grad_attn_out, grad_g_attn = norm_back(attn_out, attn_inv, gain_attn, 0.5 * grad_middle)
    grad_mamba_out, grad_g_mamba = norm_back(mamba_out, mamba_inv, gain_mamba, 0.5 * grad_middle)
    grad_attn_low = grad_attn_out.astype(low)

    grad_context = product(w_attn, grad_attn_low, (1, 1), out=low)
    grad_queries, grad_k_meta, grad_v_meta, grad_keys, grad_values = attend_back(
        attend_at, queries, grad_context, contexts, log_norms, keyvals, meta_kv, *heads
    )
    grad_queries, own_w_units, own_w_down = lax.optimization_barrier(
        (grad_queries, own_w_units, own_w_down)
    )
    grad_meta_kv = jnp.concatenate([grad_k_meta, grad_v_meta], 0)
    grad_kv_blocks = lax.dynamic_update_slice_in_dim(
        jnp.zeros((blocks_back + n, 2 * kv_cols, tokens), low),
        jnp.concatenate([grad_keys, grad_values], 1).astype(low),
        here,
        0,
    )[blocks_back:]
    grad_keyvals = seq_reduce(grad_kv_blocks, 7)
    grad_qkv = jnp.concatenate([grad_queries, grad_keyvals], 0).astype(low)
    grad_meta_low = product(grad_meta_kv.astype(low), w_kv, (0, 1))
    grad_meta, grad_g_meta = norm_back(meta_float, meta_inv, gain_norm, grad_meta_low)

    meta_high = grad_meta_kv.astype(low)
    meta_rest = (grad_meta_kv - lax.reduce_precision(grad_meta_kv, 8, 7)).astype(low)
    qkv_pad, attn_pad = up_to(qkv_cols, LANES), up_to(width, LANES)
    meta_side = ((q_cols, qkv_pad - qkv_cols), (0, 0))
    grad_w_qkv = product(
        jnp.concatenate([normed, meta_low, meta_low], 0),
        jnp.concatenate(
            [pad_to(grad_qkv, qkv_pad, 0), jnp.pad(meta_high, meta_side), jnp.pad(meta_rest, meta_side)],
            1,
        ),
        (0, 1),
        out=low,
    )
    grad_w_attn = product(attended, pad_to(grad_attn_low, attn_pad, 1), (1, 0), out=low)
    grad_attn = jnp.concatenate([grad_w_qkv, grad_w_attn], 1).reshape(depth, shard_rows, -1)
    meta_own = META // depth
    grad_gains = jnp.stack([grad_g_attn, grad_g_mamba, grad_g_ffn], 0).astype(low)
    grad_gains = grad_gains.reshape(3, depth, shard_rows).transpose(1, 0, 2)
    spare = jnp.concatenate(
        [grad_meta.astype(low).reshape(depth, meta_own, width), pad_to(grad_gains, width, 2)], 1
    )
    spare = pad_to(spare, up_to(meta_own + 3, 16), 1)
    piece = up_to(-(-(shard_rows + spare.shape[1]) // n), 8)
    grad_attn = jnp.concatenate([grad_attn, pad_to(spare, qkv_pad + attn_pad, 2)], 1)
    grad_attn = pad_to(grad_attn, n * piece, 1)
    grad_attn = grad_attn.reshape(depth, n, piece, -1).transpose(1, 0, 2, 3)
    grad_attn = grad_attn.reshape(n * depth * piece, -1)

    grad_mamba_low, grad_attn = lax.optimization_barrier((grad_mamba_out.astype(low), grad_attn))
    grad_mamba_all = seq_gather(grad_mamba_low, 6).reshape(rows, width)
    grad_attn = lax.psum_scatter(grad_attn, "seq", scatter_dimension=0, tiled=True)
    grad_w_mamba = in_rows(product(mamba_low, grad_mamba_all, (0, 0), out=low))
    grad_mix = product(grad_mamba_all, w_mamba, (1, 1))
    grad_y = grad_mix * silu_z
    grad_z = (grad_mix * y_full * silu_slope(z_gate)).astype(low)
    grad_w_z = product(normed_all, grad_z, (0, 0), out=low)
    grad_y, grad_w_z, grad_w_mamba, down_sum = lax.optimization_barrier(
        (grad_y, grad_w_z, grad_w_mamba, down_sum)
    )
    own_mamba, own_z = depth_sum(grad_w_mamba), depth_sum(grad_w_z)
    grad_skip = jnp.sum(grad_y * mixed, 0, keepdims=True)
    grad_steps, grad_x, grad_b, grad_c, grad_a = scan_bwd(
        info, steps, mixed, state_weights(b_sel, c_sel), grad_y, a_t, firsts, n
    )
    grad_dt_pre = grad_steps * jax.nn.sigmoid(dt_pre)
    grad_dt_bias = jnp.sum(grad_dt_pre, 0, keepdims=True)
    grad_ranks = product(steps_t, grad_dt_pre, (1, 1))
    grad_selected = all_sum(jnp.concatenate([grad_ranks, grad_b, grad_c], 0), 8)
    grad_selected, grad_attn = lax.optimization_barrier((grad_selected, grad_attn))
    own_attn = depth_sum(grad_attn)
    grad_w_steps = product(ranks, grad_dt_pre, (1, 0))
    grad_w_select = product(grad_selected, mixed, (1, 0))
    grad_mixed = grad_y * skip + grad_x + product(grad_selected, select_t, (0, 0))
    grad_conv = grad_mixed * silu_slope(conv_pre)
    grad_in, grad_taps, grad_bias = conv_bwd(info, grad_conv, mixer_in, grad_z, taps_t, n)

    grad_w_x = product(normed_all, grad_in[:, :inner_pad], (0, 0), out=low)
    grad_small = jnp.concatenate(
        [grad_taps, grad_bias, grad_w_select, grad_w_steps, grad_dt_bias, grad_a * a_t, grad_skip], 0
    )
    grad_small = pad_to(grad_small, small_rows, 0).astype(low)
    grad_in, grad_w_x, grad_small, own_w_units, own_w_down, own_mamba, own_z = (
        lax.optimization_barrier(
            (grad_in, grad_w_x, grad_small, own_w_units, own_w_down, own_mamba, own_z)
        )
    )
    own_x = depth_sum(grad_w_x)
    all_w_units, all_w_down = lax.all_gather(own_w_units, "seq"), lax.all_gather(own_w_down, "seq")
    own_small = turned_sum(grad_small.reshape(small_rows, depth, chunk_pad).transpose(1, 0, 2))
    grad_normed = in_rows(product(grad_in, w_in, (1, 1), out=low)).reshape(n, tokens, width)
    grad_normed = seq_reduce(grad_normed, 9)
    layer_out = middle + down_sum.astype(F32)
    grad_normed = grad_normed + product(grad_qkv, w_qkv, (0, 1))
    grad_input_norm, grad_g_in = norm_back(hidden, inv_in, gain_norm, grad_normed)
    inputs_grad = (grad_middle + grad_input_norm)[None]
    gain_rows = up_to(-(-width // chunk_pad), 16)
    grad_g_in = pad_to((grad_g_in + grad_g_meta)[None], gain_rows * chunk_pad, 1)
    grad_g_in = grad_g_in.reshape(gain_rows, chunk_pad)
    own_small = jnp.concatenate([own_small, grad_g_in], 0).astype(low)

    all_small, all_x, all_z, all_mamba, all_attn = last_gather(
        [own_small, own_x, own_z, own_mamba, pad_to(own_attn, up_to(piece, 16), 0)], 10
    )
    all_gain = jnp.sum(all_small[:, small_rows:].astype(F32), 0).reshape(-1)[:width]
    all_gain = turned_sum(all_gain.reshape(depth, shard_rows))
    grad_w_mamba = lay_rows(all_mamba, chunk)
    all_attn = all_attn[:, :piece]
    grad_attn = all_attn.reshape(n * piece, -1)
    grad_w_attn = grad_attn[:shard_rows, qkv_pad : qkv_pad + width].astype(F32)
    gains = grad_attn[shard_rows + meta_own : shard_rows + meta_own + 3, :shard_rows].astype(F32)
    grad_meta = grad_attn[shard_rows : shard_rows + meta_own, :width].astype(F32)
    grad_w_proj = lay_cols(
        [(all_x, 0), (all_z, 0)], chunk, chunk_pad, EI, grad_attn[:shard_rows], qkv_cols
    )
    grad_w_proj, all_w_down = lax.optimization_barrier((grad_w_proj, all_w_down))
    grad_w_down = lay_rows_turned(all_w_down, unit_chunk)
    grad_w_down, all_w_units = lax.optimization_barrier((grad_w_down, all_w_units))
    grad_w_down = grad_w_down.T
    unit_cols = (unit_chunk, unit_pad, hidden_units)
    grad_w_gate = lay_cols([(all_w_units, 0)], *unit_cols)
    grad_w_up = lay_cols([(all_w_units, 1)], *unit_cols)
    grad_small = lay_cols([(all_small[:, :small_rows], 0)], chunk, chunk_pad, EI // depth)
    grad_taps, grad_bias, grad_w_select, grad_w_steps, grad_dt_bias, grad_decay, grad_skip = (
        grad_small[a:b].T for a, b in zip(ends[:-1], ends[1:])
    )

    return (
        layer_out.astype(low)[None],
        inputs_grad,
        all_gain,
        grad_w_proj,
        grad_taps,
        grad_bias[:, 0],
        grad_w_select,
        grad_w_steps,
        grad_dt_bias[:, 0],
        grad_decay,
        grad_skip[:, 0],
        grad_meta,
        grad_w_attn,
        grad_w_mamba,
        gains[0],
        gains[1],
        gains[2],
        grad_w_gate,
        grad_w_up,
        grad_w_down,
    )


def solution(mesh):
    in_specs = (
        P("fsdp", "seq", None),
        P("fsdp", "seq"),
        P("fsdp"),
        P("fsdp", None),
        P("fsdp", None),
        P("fsdp"),
        P("fsdp", None),
        P("fsdp", None),
        P("fsdp"),
        P("fsdp", None),
        P("fsdp"),
        P("fsdp", None),
        P("fsdp", None),
        P("fsdp", None),
        P("fsdp"),
        P("fsdp"),
        P("fsdp"),
        P("fsdp", None),
        P("fsdp", None),
        P("fsdp", None),
        P("fsdp", "seq", None),
    )
    out_specs = (
        P("fsdp", "seq", None),
        P("fsdp", "seq", None),
        P("fsdp"),
        P("fsdp", None),
        P("fsdp", None),
        P("fsdp"),
        P("fsdp", None),
        P("fsdp", None),
        P("fsdp"),
        P("fsdp", None),
        P("fsdp"),
        P("fsdp", None),
        P("fsdp", None),
        P("fsdp", None),
        P("fsdp"),
        P("fsdp"),
        P("fsdp"),
        P("fsdp", None),
        P("fsdp", None),
        P("fsdp", None),
    )
    return jax.shard_map(shards, mesh=mesh, in_specs=in_specs, out_specs=out_specs, check_vma=False)
```
